32 devices in a mesh: fsdp: 8 (over y, x, core), ctx: 4 (over z).
Axes of the slice: x: 2, y: 2, z: 4, core: 2. Of those that a mesh axis runs over, the one named last changes fastest.
Arguments:
- tokens_in: bfloat16 [4096, 2048], P(('fsdp', 'ctx')), may hold values from -6 to 6
- cotangent: bfloat16 [4096, 2048], P(('fsdp', 'ctx')), may hold values from -6 to 6
- routes: int32 [4096, 6], P(('fsdp', 'ctx')), may hold values from 0 to 15, all different within a row; in each aligned block of 512 rows (0 to 511, 512 to 1023, ...) at most 240 rows name the same one
- segments: int32 [4096], P(('fsdp', 'ctx')), may hold values from 0 to 23, as said below
- norm_in: float32 [2048], replicated, may hold values from 0.5 to 1.5
- w_query: bfloat16 [2048, 3072], P('fsdp', 'ctx'), may hold values from -0.125 to 0.125
- w_latent: bfloat16 [2048, 576], P(('fsdp', 'ctx')), may hold values from -0.125 to 0.125
- latent_gain: float32 [512], replicated, may hold values from 0.5 to 1.5
- w_expand: bfloat16 [512, 4096], P('fsdp', 'ctx'), may hold values from -0.25 to 0.25
- w_output: bfloat16 [2048, 2048], P('ctx', 'fsdp'), may hold values from -2 to 2
- norm_mid: float32 [2048], replicated, may hold values from 0.5 to 1.5
- w_router: bfloat16 [2048, 16], P(('fsdp', 'ctx')), may hold values from -0.0625 to 0.0625
- shared_gate: bfloat16 [2048, 2816], P('fsdp', 'ctx'), may hold values from -0.125 to 0.125
- shared_up: bfloat16 [2048, 2816], P('fsdp', 'ctx'), may hold values from -0.125 to 0.125
- shared_down: bfloat16 [2816, 2048], P('ctx', 'fsdp'), may hold values from -0.109375 to 0.109375
- expert_gate: bfloat16 [16, 1408, 2048], P('fsdp', 'ctx'), may hold values from -0.125 to 0.125
- routed_up_weight: bfloat16 [16, 1408, 2048], P('fsdp', 'ctx'), may hold values from -0.125 to 0.125
- expert_down: bfloat16 [16, 1408, 2048], P('fsdp', 'ctx'), may hold values from -0.15625 to 0.15625
Outputs:
- block_out: bfloat16 [4096, 2048], P(('fsdp', 'ctx'))
- grad_input: bfloat16 [4096, 2048], P(('fsdp', 'ctx'))
- grad_norm_in: float32 [2048], P(('fsdp', 'ctx'))
- grad_query: float32 [2048, 3072], P('fsdp', 'ctx')
- grad_latent: float32 [2048, 576], P(('fsdp', 'ctx'))
- grad_latent_gain: float32 [512], P(('fsdp', 'ctx'))
- grad_expand: float32 [512, 4096], P('fsdp', 'ctx')
- grad_output: float32 [2048, 2048], P('ctx', 'fsdp')
- grad_norm_mid: float32 [2048], P(('fsdp', 'ctx'))
- grad_router: float32 [2048, 16], P(('fsdp', 'ctx'))
- grad_shared_gate: float32 [2048, 2816], P('fsdp', 'ctx')
- grad_shared_up: float32 [2048, 2816], P('fsdp', 'ctx')
- grad_shared_down: float32 [2816, 2048], P('ctx', 'fsdp')
- grad_expert_gate: float32 [16, 1408, 2048], P('fsdp', 'ctx')
- grad_expert_up: float32 [16, 1408, 2048], P('fsdp', 'ctx')
- grad_expert_down: float32 [16, 1408, 2048], P('fsdp', 'ctx')
The draws below stay inside these ranges and needn't reach their ends.
Inputs may be any that keep to these rules, and one draw needn't show every extreme that they name: `routes`: in each aligned block of 512 rows (one group) no expert is named by more than 240 rows, a bound that some block reaches; each row names 6 different experts. `segments`: ids never fall; aligned block g of 512 rows holds the ids 3 g, 3 g + 1 and 3 g + 2, the first and the last of them on fewer than 128 rows.
All inputs are finite; a program needn't handle non-finite values.
Results may differ from the reference program's by a relative error of at most 0.02.
Values may be sent and summed in bfloat16 or wider, within the bound.
No kernel may reach another device: no remote copies, remote signals or barrier semaphores. Data moves between devices by JAX's collectives and lax.ppermute only.
A program may use at most 384 MiB of HBM per device.

```python
import math
import jax
import jax.numpy as jnp
import numpy as np
from jax import lax

D = 2048
H = 16
NOPE = 128
ROPE = 64
VD = 128
LAT = 512
FE = 1408
SHARED = 2816
TOP = 6
TOK_DEV = 128
EXPERTS = 16
TOKENS = 4096
CAP = 240
N_FSDP = 8
N_CTX = 4


def draw_segments(key, part):
    key = jax.random.fold_in(key, 11)
    first_key, last_key = jax.random.split(key)
    group_rows = TOK_DEV * N_CTX
    begin = jax.random.randint(first_key, (N_FSDP, 1), 1, TOK_DEV)
    finish = group_rows - jax.random.randint(last_key, (N_FSDP, 1), 1, TOK_DEV)
    steps = jnp.arange(group_rows, dtype=jnp.int32)[None, :]
    local = (steps >= begin).astype(jnp.int32) + (steps >= finish).astype(jnp.int32)
    base = 3 * jnp.arange(N_FSDP, dtype=jnp.int32)[:, None]
    return (base + local).reshape(-1)


def shard_levels(rng, shape, cuts, low, largest):
    def one(axis_at, blocks):
        draws = jax.random.uniform(jax.random.fold_in(jax.random.fold_in(rng, 6), axis_at), (blocks,), jnp.float32, low / len(cuts), largest / len(cuts))
        return jnp.repeat(jnp.exp(draws), shape[axis_at] // blocks).reshape((-1,) + (1,) * (len(shape) - axis_at - 1))

    level = one(*cuts[0])
    for cut in cuts[1:]:
        level = level * one(*cut)
    return level


def shared_out(own_key, own, number, rows, amount, top, limit, skew):
    ranking = jax.random.permutation(own_key, amount)
    crowded, common = portions_of(amount, rows * top, limit, skew, True), portions_of(amount, rows * top, limit, skew, False)
    places = jnp.arange(amount)

    def named(tallies, offset_by):
        used = int((tallies > 0).sum())
        fixed = max(1, used // 4)
        shifted = fixed + (places - fixed + offset_by * (used - fixed)) % max(1, amount - fixed)
        return jnp.zeros((amount,), jnp.int32).at[ranking[jnp.where(places < fixed, places, shifted)]].set(jnp.asarray(tallies, jnp.int32))

    tallies = jnp.where(number % 4 == 0, named(crowded, number // 4), named(common, number - number // 4 - 1))
    mixed = jax.random.permutation(jax.random.fold_in(own, 3), amount)
    donor, sink = mixed[0:amount // 2 * 2:2], mixed[1:amount // 2 * 2:2]
    room = jnp.minimum(tallies[donor] - 1, limit - tallies[sink]) // 2
    room = jnp.where((donor == ranking[0]) | (sink == ranking[0]) | (tallies[sink] == 0), 0, jnp.maximum(room, 0))
    shifted = jax.random.randint(jax.random.fold_in(own, 4), (amount // 2,), 0, 1 << 20) % (room + 1)
    tallies = tallies.at[donor].add(-shifted).at[sink].add(shifted)
    members = jnp.searchsorted(jnp.cumsum(tallies), jnp.arange(rows * top), side="right").astype(jnp.int32)
    table = members.reshape(top, rows).T
    table = table[jax.random.permutation(jax.random.fold_in(own, 1), rows)]
    offset_by = jax.random.randint(jax.random.fold_in(own, 2), (rows, 1), 0, top)
    return jnp.take_along_axis(table, (jnp.arange(top)[None, :] + offset_by) % top, axis=1)


def portions_of(count, total, limit, skew, full):
    portions = [(1 << 20) // math.isqrt(grade ** skew) + 1 for grade in range(1, count + 1)]
    largest = limit if full else min(limit, max(-(-total // count), total * portions[0] // sum(portions)))
    least = 1 if total - largest >= count - 1 else 0
    counts, surplus = [largest] + [least] * (count - 1), total - largest - least * (count - 1)
    while surplus > 0:
        free = [i for i in range(1, count) if counts[i] < largest] or [i for i in range(1, count) if counts[i] < limit]
        pool, budget = sum([portions[i] for i in free]), surplus
        for i in free:
            more = min(limit - counts[i], max(1, budget * portions[i] // pool), surplus)
            counts[i] = counts[i] + more
            surplus = surplus - more
    return np.array(counts)


def normal_values(own_key, extent, scale, limit, cuts=(), held_as=jnp.bfloat16):
    entries = scale * jax.random.normal(own_key, extent, jnp.float32)
    if cuts:
        entries = entries * shard_levels(own_key, extent, cuts, -0.22, 0.18)
    return jnp.clip(entries, -limit, limit).astype(held_as)


def setup_inputs(seed: int = 0) -> dict:
    splits = jax.random.split(jax.random.key(seed), 19)
    tokens_in = normal_values(splits[0], (TOKENS, D), 1.0, 6.0, ((0, 32),))
    cotangent = normal_values(splits[1], (TOKENS, D), 1.0, 6.0, ((0, 32),))
    routes_keys = jax.random.split(jax.random.fold_in(splits[2], 1), TOKENS // (TOK_DEV * N_CTX))
    routes_turns = jax.random.permutation(jax.random.fold_in(splits[2], 3), TOKENS // (TOK_DEV * N_CTX))
    routes = jax.vmap(lambda own, number: shared_out(jax.random.fold_in(splits[2], 2), own, number, TOK_DEV * N_CTX, EXPERTS, TOP, CAP, 1))(routes_keys, routes_turns).reshape((TOKENS, TOP))
    segments = draw_segments(jax.random.fold_in(splits[18], 71), 0)
    norm_in = jnp.clip(1.0 + 0.1 * jax.random.normal(splits[4], (D,), jnp.float32), 0.5, 1.5)
    w_query = normal_values(splits[5], (D, H * (NOPE + ROPE)), D ** -0.5, 0.125, ((0, 8), (1, 4)))
    w_latent = normal_values(splits[6], (D, LAT + ROPE), D ** -0.5, 0.125, ((0, 32),))
    latent_gain = jnp.clip(1.0 + 0.1 * jax.random.normal(splits[7], (LAT,), jnp.float32), 0.5, 1.5)
    w_expand = normal_values(splits[8], (LAT, H * (NOPE + VD)), LAT ** -0.5, 0.25, ((0, 8), (1, 4)))
    w_output = normal_values(splits[9], (H * VD, D), (max(H * VD // 256, 1)) ** -0.5, 2.0, ((0, 4), (1, 8)))
    norm_mid = jnp.clip(1.0 + 0.1 * jax.random.normal(splits[10], (D,), jnp.float32), 0.5, 1.5)
    w_router = normal_values(splits[11], (D, EXPERTS), (4 * D) ** -0.5, 0.0625, ((0, 32),))
    shared_gate = normal_values(splits[12], (D, SHARED), D ** -0.5, 0.125, ((0, 8), (1, 4)))
    shared_up = normal_values(splits[13], (D, SHARED), D ** -0.5, 0.125, ((0, 8), (1, 4)))
    shared_down = normal_values(splits[14], (SHARED, D), SHARED ** -0.5, 0.109375, ((0, 4), (1, 8)))
    expert_gate = normal_values(splits[15], (EXPERTS, FE, D), D ** -0.5, 0.125, ((0, 8), (1, 4)))
    routed_up_weight = normal_values(splits[16], (EXPERTS, FE, D), D ** -0.5, 0.125, ((0, 8), (1, 4)))
    expert_down = normal_values(splits[17], (EXPERTS, FE, D), FE ** -0.5, 0.15625, ((0, 8), (1, 4)))
    return dict(tokens_in=tokens_in, cotangent=cotangent, routes=routes, segments=segments, norm_in=norm_in, w_query=w_query, w_latent=w_latent, latent_gain=latent_gain, w_expand=w_expand, w_output=w_output, norm_mid=norm_mid, w_router=w_router, shared_gate=shared_gate, shared_up=shared_up, shared_down=shared_down, expert_gate=expert_gate, routed_up_weight=routed_up_weight, expert_down=expert_down)


@jax.custom_vjp
def low(v):
    return lax.optimization_barrier(v.astype(jnp.bfloat16)).astype(jnp.float32)

@jax.custom_vjp
def low_back(v):
    return v

def low_keep(v):
    return (low(v), None)

def low_pass(kept, grad):
    return (grad,)

def back_keep(v):
    return (v, None)

def back_low(kept, grad):
    return (low(grad),)
low.defvjp(low_keep, low_pass)
low_back.defvjp(back_keep, back_low)
EPS = 1e-06
THETA = 50000.0
ROUTE_SCALE = 2.446
HIGH = lax.Precision.HIGHEST

def both(v):
    return low_back(low(v))

def matmul(left, right):
    return jnp.dot(left, right, precision=HIGH)

def rms(v, gain):
    return v * lax.rsqrt(lax.optimization_barrier(jnp.mean(v * v, axis=-1, keepdims=True)) + EPS) * gain

def turn(v, cosine, sine):
    half = v.shape[-1] // 2
    first, second = (v[..., :half], v[..., half:])
    return jnp.concatenate([first * cosine - second * sine, second * cosine + first * sine], axis=-1)

def group_forward(weights, xg, seg, route):
    norm_in, w_query, w_latent, latent_gain, w_expand, w_output, norm_mid, w_router, shared_gate, shared_up, shared_down, expert_gate, routed_up_weight, expert_down = weights
    count = xg.shape[0]
    steps = jnp.arange(count, dtype=jnp.int32)
    fresh = jnp.concatenate([jnp.ones((1,), dtype=bool), seg[1:] != seg[:-1]])
    start = lax.cummax(jnp.where(fresh, steps, 0), axis=0)
    place = (steps - start).astype(jnp.float32)
    freq = THETA ** (-(jnp.arange(ROPE // 2, dtype=jnp.float32) * 2.0 / ROPE))
    angle = place[:, None] * freq[None, :]
    cosine, sine = (jnp.cos(angle), jnp.sin(angle))
    allowed = (seg[None, :] == seg[:, None]) & (steps[None, :] <= steps[:, None])
    scale = (NOPE + ROPE) ** (-0.5)
    width = H // N_CTX
    xl = low(rms(xg, norm_in))
    attn = jnp.zeros((count, D), jnp.float32)
    for group in range(N_CTX):
        qcols = w_query[:, group * width * (NOPE + ROPE):(group + 1) * width * (NOPE + ROPE)]
        kvcols = w_expand[:, group * width * (NOPE + VD):(group + 1) * width * (NOPE + VD)]
        orows = w_output[group * width * VD:(group + 1) * width * VD]
        q_raw = low_back(matmul(xl, qcols)).reshape(count, width, NOPE + ROPE)
        query = low(jnp.concatenate([q_raw[..., :NOPE], turn(q_raw[..., NOPE:], cosine[:, None, :], sine[:, None, :])], axis=-1))
        latent_raw = low_back(matmul(xl, w_latent))
        latent = low(rms(latent_raw[:, :LAT], latent_gain))
        krope = low(turn(latent_raw[:, LAT:], cosine, sine))
        kv_raw = low_back(matmul(latent, kvcols)).reshape(count, width, NOPE + VD)
        keys = jnp.concatenate([low(kv_raw[..., :NOPE]), jnp.broadcast_to(krope[:, None, :], (count, width, ROPE))], axis=-1)
        values = low(kv_raw[..., NOPE:])
        scores = low_back(jnp.einsum('qhd,khd->hqk', query, keys, precision=HIGH) * scale)
        scores = jnp.where(allowed[None], scores, -1e+30)
        probs = low(jax.nn.softmax(scores, axis=-1))
        heads_out = both(jnp.einsum('hqk,khd->qhd', probs, values, precision=HIGH))
        attn = attn + matmul(heads_out.reshape(count, width * VD), orows)
    attn = low_back(attn)
    resid = xg + attn
    mid = low(rms(resid, norm_mid))
    sig = jax.nn.sigmoid(matmul(mid, w_router))
    pick = (route[:, :, None] == jnp.arange(EXPERTS, dtype=jnp.int32)[None, None, :]).astype(jnp.float32)
    chosen = jnp.einsum('gke,ge->gk', pick, sig, precision=HIGH)
    gates = ROUTE_SCALE * chosen / lax.optimization_barrier(jnp.sum(chosen, axis=-1, keepdims=True))
    flat = route.reshape(-1)
    hits = (flat[:, None] == jnp.arange(EXPERTS, dtype=jnp.int32)[None, :]).astype(jnp.int32)
    slot = lax.optimization_barrier(jnp.sum(jnp.cumsum(hits, axis=0) * hits, axis=1)) - 1
    index = (flat * CAP + slot).astype(jnp.int32)
    pairs = jnp.arange(count * TOP, dtype=jnp.int32)
    rows = jnp.zeros((EXPERTS * CAP, D), jnp.float32).at[index].set(mid[pairs // TOP]).reshape(EXPERTS, CAP, D)
    part = FE // N_CTX
    y_sum = jnp.zeros((EXPERTS, CAP, D), jnp.float32)
    for lane in range(N_CTX):
        own = low_back(rows)
        gate = low_back(jnp.einsum('ecd,efd->ecf', own, expert_gate[:, lane * part:(lane + 1) * part, :], precision=HIGH))
        upper = low_back(jnp.einsum('ecd,efd->ecf', own, routed_up_weight[:, lane * part:(lane + 1) * part, :], precision=HIGH))
        act = low(jax.nn.silu(gate) * upper)
        y_sum = y_sum + both(jnp.einsum('ecf,efd->ecd', act, expert_down[:, lane * part:(lane + 1) * part, :], precision=HIGH))
    picked = y_sum.reshape(EXPERTS * CAP, D)[index].reshape(count, TOP, D)
    routed = jnp.einsum('gk,gkd->gd', gates, picked, precision=HIGH)
    sgate = low_back(matmul(mid, shared_gate))
    sup = low_back(matmul(mid, shared_up))
    shared = matmul(low(jax.nn.silu(sgate) * sup), shared_down)
    return resid + routed + shared

def reference(tokens_in, cotangent, routes, segments, norm_in, w_query, w_latent, latent_gain, w_expand, w_output, norm_mid, w_router, shared_gate, shared_up, shared_down, expert_gate, routed_up_weight, expert_down):
    weights = tuple((w.astype(jnp.float32) for w in (norm_in, w_query, w_latent, latent_gain, w_expand, w_output, norm_mid, w_router, shared_gate, shared_up, shared_down, expert_gate, routed_up_weight, expert_down)))
    group_rows = TOK_DEV * N_CTX
    xs = tokens_in.astype(jnp.float32).reshape(N_FSDP, group_rows, D)
    segs = segments.reshape(N_FSDP, group_rows)
    picks = routes.reshape(N_FSDP, group_rows, TOP)
    run_group = jax.checkpoint(group_forward)

    def forward(weights, xs):

        def step(carry, item):
            return (carry, run_group(weights, item[0], item[1], item[2]))
        _, outs = lax.scan(step, None, (xs, segs, picks))
        return outs
    outs, pull = jax.vjp(forward, weights, xs)
    grad_weights, grad_xs = pull(cotangent.astype(jnp.float32).reshape(N_FSDP, group_rows, D))
    block_out = outs.reshape(TOKENS, D).astype(jnp.bfloat16)
    grad_input = grad_xs.reshape(TOKENS, D).astype(jnp.bfloat16)
    return (block_out, grad_input, grad_weights[0], grad_weights[1], grad_weights[2], grad_weights[3], grad_weights[4], grad_weights[5], grad_weights[6], grad_weights[7], grad_weights[8], grad_weights[9], grad_weights[10], grad_weights[11], grad_weights[12], grad_weights[13])
```

```python
import functools

import jax
import jax.numpy as jnp
from jax import lax
from jax.experimental import pallas as pl
from jax.experimental.pallas import tpu as pltpu
from jax.sharding import PartitionSpec as P

NOPE = 128
ROPE = 64
VD = 128
LAT = 512


EPS = 1e-06
THETA = 50000.0
ROUTE_SCALE = 2.446
MIB = 1024 * 1024
NEG_FILL = -1e30


def dot32(left, right):
    return jnp.dot(left, right, preferred_element_type=jnp.float32)


def dot_nt(left, right):
    return lax.dot_general(
        left, right, (((1,), (1,)), ((), ())), preferred_element_type=jnp.float32
    )


def dot_tn(left, right):
    return lax.dot_general(
        left, right, (((0,), (0,)), ((), ())), preferred_element_type=jnp.float32
    )


def precise_nt(left, right):
    return lax.dot_general(
        left,
        right,
        (((1,), (1,)), ((), ())),
        precision=lax.Precision.HIGHEST,
        preferred_element_type=jnp.float32,
    )


def precise_tn(left, right):
    return lax.dot_general(
        left,
        right,
        (((0,), (0,)), ((), ())),
        precision=lax.Precision.HIGHEST,
        preferred_element_type=jnp.float32,
    )


def norm_parts(value, gain):
    factor = lax.rsqrt(jnp.mean(value * value, axis=-1, keepdims=True) + EPS)
    unit = value * factor
    return (unit * gain, unit, factor)


def norm_back(grad_out, unit, factor, gain):
    grad_unit = grad_out * gain
    return factor * (grad_unit - unit * jnp.mean(grad_unit * unit, axis=-1, keepdims=True))


def turn(value, cosine, sine):
    half = value.shape[-1] // 2
    first, second = (value[..., :half], value[..., half:])
    return jnp.concatenate(
        [first * cosine - second * sine, second * cosine + first * sine], axis=-1
    )


def turn_back(grad, cosine, sine):
    half = grad.shape[-1] // 2
    first, second = (grad[..., :half], grad[..., half:])
    return jnp.concatenate(
        [first * cosine + second * sine, second * cosine - first * sine], axis=-1
    )


def silu_slope(value):
    sig = jax.nn.sigmoid(value)
    return (sig * (1.0 + value * (1.0 - sig)), value * sig)


def after(value, *others):
    return lax.optimization_barrier((value,) + others)[0]


def gather_ctx(value):
    lanes, lane = (lax.axis_size("ctx"), lax.axis_index("ctx"))
    rows = value.shape[0]
    whole = jnp.zeros((lanes * rows,) + value.shape[1:], value.dtype)
    whole = lax.dynamic_update_slice_in_dim(whole, value, lane * rows, 0)
    for hop in range(1, lanes):
        got = lax.ppermute(value, "ctx", [(i, (i + hop) % lanes) for i in range(lanes)])
        source = lax.rem(lane + lanes - hop, lanes)
        whole = lax.dynamic_update_slice_in_dim(whole, got, source * rows, 0)
    return whole


def scatter_ctx(value):
    lanes, lane = (lax.axis_size("ctx"), lax.axis_index("ctx"))
    rows = value.shape[0] // lanes
    total = lax.dynamic_slice_in_dim(value, lane * rows, rows, 0).astype(jnp.float32)
    for hop in range(1, lanes):
        target = lax.rem(lane + hop, lanes)
        part = lax.dynamic_slice_in_dim(value, target * rows, rows, 0)
        got = lax.ppermute(part, "ctx", [(i, (i + hop) % lanes) for i in range(lanes)])
        total = total + got.astype(jnp.float32)
    return total


class Plan:
    def __init__(self, exp_dev, hidden, shared, experts, top):
        self.exp_dev, self.hidden, self.experts, self.top = (exp_dev, hidden, experts, top)
        self.units = exp_dev * hidden
        self.shared = -(-shared // 8) * 8
        at = self.units + self.shared
        if at // 128 != (at + experts - 1) // 128:
            at = -(-at // 128) * 128
        self.router = at
        self.cols = -(-(at + experts) // 128) * 128
        self.even = (self.cols - 1) // 256 * 256
        self.tail = self.cols - self.even
        self.block = at // 128 * 128
        assert self.block >= self.even and self.block + 128 >= at + experts

    def join(self, gate, upper):
        return jnp.concatenate(
            [gate[: self.even], gate[self.even :], upper[self.even :], upper[: self.even]]
        )


def back_kernel(plan, first_ref, mid_ref, dout_ref, meta_ref, w1_ref, wd_ref, *refs):
    f32, bf16 = (jnp.float32, jnp.bfloat16)
    even, tail, hidden = (plan.even, plan.tail, plan.hidden)
    rows, model = mid_ref.shape
    rows_ref, gud_ref, act_ref = refs[-3:]
    mid = mid_ref[...]
    dout = dout_ref[...].reshape(rows, model)
    lanes = lax.broadcasted_iota(jnp.int32, (rows, 128), 1)
    off = plan.router - plan.block
    first = first_ref[0]
    sums = [jnp.zeros((rows, 128), f32) for _ in range(plan.exp_dev)]

    def elements(own, at, gate, upper, act_grad, gate_at, up_at):
        for b in range(0, gate.shape[1], 128):
            low = at + b
            g, u, da = (gate[:, b : b + 128], upper[:, b : b + 128], act_grad[:, b : b + 128])
            sig = jax.nn.sigmoid(g)
            swish = g * sig
            act = swish * u
            weighted = act * da
            scale = None
            for e in range(plan.exp_dev):
                start, stop = (e * hidden, (e + 1) * hidden)
                if stop <= low or start >= low + 128:
                    continue
                if start <= low and stop >= low + 128:
                    scale = own[e]
                    sums[e] = sums[e] + weighted
                else:
                    mine = (low + lanes >= start) & (low + lanes < stop)
                    sums[e] = sums[e] + jnp.where(mine, weighted, 0.0)
                    rest = jnp.ones((rows, 128), f32) if scale is None else scale
                    scale = jnp.where(mine, own[e], rest)
            if scale is not None:
                act = act * scale
                da = da * scale
            act_ref[:, low : low + 128] = act.astype(bf16)
            slope = sig + swish * (1.0 - sig)
            gud_ref[:, gate_at + b : gate_at + b + 128] = (da * u * slope).astype(bf16)
            gud_ref[:, up_at + b : up_at + b + 128] = (da * swish).astype(bf16)

    joint = dot_nt(mid, w1_ref[even : even + 2 * tail, :])
    at_block = plan.block - even
    sig = jax.nn.sigmoid(joint[:, at_block : at_block + 128])
    named = meta_ref[...].reshape(rows, 128).astype(f32)
    expert = (lanes - off).astype(f32)
    member = jnp.zeros((rows, 128), f32)
    for k in range(plan.top):
        member = jnp.where(expert == named[:, k : k + 1], 1.0, member)
    member = jnp.where((lanes >= off) & (lanes < off + plan.experts), member, 0.0)
    chosen = sig * member
    gates = ROUTE_SCALE * chosen / jnp.sum(chosen, axis=1, keepdims=True)
    own = [
        jnp.sum(jnp.where(lanes - off == first + e, gates, 0.0), axis=1, keepdims=True)
        for e in range(plan.exp_dev)
    ]
    act_grad = dot_nt(dout, wd_ref[even : even + tail, :])
    elements(own, even, joint[:, :tail], joint[:, tail:], act_grad, even, even + tail)
    for at in range(0, even, 256):
        up_at = even + 2 * tail + at
        elements(
            own,
            at,
            dot_nt(mid, w1_ref[at : at + 256, :]),
            dot_nt(mid, w1_ref[up_at : up_at + 256, :]),
            dot_nt(dout, wd_ref[at : at + 256, :]),
            at,
            up_at,
        )
    step = 512
    for at in range(0, model, step):
        rows_ref[:, at : at + step] = dot32(gud_ref[...], w1_ref[:, at : at + step]).astype(bf16)
    ends = jnp.zeros((rows, 128), f32)
    for e in range(plan.exp_dev):
        grad = jnp.sum(sums[e], axis=1, keepdims=True)
        high = grad.astype(bf16).astype(f32)
        ends = jnp.where(lanes == first + e, high, ends)
        ends = jnp.where(lanes == plan.experts + first + e, grad - high, ends)
    rows_ref[:, model:] = ends.astype(bf16)


def experts_back(plan, chunk, first, mid, dout, w1, wd, *held):
    tokens, model = mid.shape
    _, chunks, rows, _ = dout.shape
    tile = min(512, tokens)

    def row(width):
        return pl.BlockSpec((tile, width), lambda i: (i, 0))

    def slot(width):
        return pl.BlockSpec((None, tile, width), lambda i: (chunk, i, 0))

    def whole(value):
        return pl.BlockSpec(value.shape, lambda i: (0, 0), pipeline_mode=pl.Buffered(1))

    def outer(width, at):
        return pl.BlockSpec((tile // rows, None, rows, width), lambda i: (i, chunk, 0, at))

    bf16 = jnp.bfloat16
    return pl.pallas_call(
        functools.partial(back_kernel, plan),
        grid=(tokens // tile,),
        in_specs=[
            pl.BlockSpec(memory_space=pltpu.SMEM),
            row(model),
            outer(model, 0),
            outer(128, model // 128),
            whole(w1),
            whole(wd),
        ]
        + [pl.BlockSpec(memory_space=pl.ANY) for _ in held],
        out_specs=[row(model + 128), slot(2 * plan.cols), slot(plan.cols)],
        out_shape=[
            jax.ShapeDtypeStruct((tokens, model + 128), bf16),
            jax.ShapeDtypeStruct((chunks, tokens, 2 * plan.cols), bf16),
            jax.ShapeDtypeStruct((chunks, tokens, plan.cols), bf16),
        ],
        input_output_aliases={6 + n: 1 + n for n in range(len(held))},
        compiler_params=pltpu.CompilerParams(
            dimension_semantics=("arbitrary",), vmem_limit_bytes=58 * MIB
        ),
        cost_estimate=pl.CostEstimate(
            flops=10 * tokens * plan.cols * model,
            bytes_accessed=tokens * 6 * (model + plan.cols),
            transcendentals=tokens * plan.cols,
        ),
        name="experts_back",
    )(first, mid, dout, dout, w1, wd, *held)


def out_kernel(act_ref, wd_ref, *refs):
    out_ref = refs[-1]
    rows, model = (act_ref.shape[0], wd_ref.shape[1])
    act = act_ref[...]
    for at in range(0, model, 512):
        part = dot32(act, wd_ref[:, at : at + 512]).astype(jnp.bfloat16)
        out_ref[:, :, at : at + 512] = part.reshape(out_ref.shape[0], out_ref.shape[1], 512)


def experts_out(plan, groups, lanes, start, chunks, act, wd, *others):
    _, tokens, cols = act.shape
    model = wd.shape[1]
    count = tokens // groups
    rows = count // lanes
    return pl.pallas_call(
        out_kernel,
        grid=(chunks, groups),
        in_specs=[
            pl.BlockSpec((None, count, cols), lambda h, g: (start + h, g, 0)),
            pl.BlockSpec(wd.shape, lambda h, g: (0, 0), pipeline_mode=pl.Buffered(1)),
        ]
        + [pl.BlockSpec(memory_space=pl.ANY) for _ in others],
        out_specs=pl.BlockSpec((None, lanes, None, rows, model), lambda h, g: (g, 0, h, 0, 0)),
        out_shape=jax.ShapeDtypeStruct((groups, lanes, chunks, rows, model), jnp.bfloat16),
        compiler_params=pltpu.CompilerParams(
            dimension_semantics=("arbitrary", "arbitrary"), vmem_limit_bytes=32 * MIB
        ),
        cost_estimate=pl.CostEstimate(
            flops=2 * chunks * tokens * cols * model,
            bytes_accessed=2 * chunks * tokens * (cols + model),
            transcendentals=0,
        ),
        name="experts_out",
    )(act, wd, *others).reshape(groups * lanes * chunks * rows, model)


def sum_kernel(plan, h_ref, z_ref, out_ref, shared_ref):
    @pl.when((pl.program_id(0) == 0) & (pl.program_id(1) == 0))
    def _():
        out_ref[...] = jnp.zeros_like(out_ref)
        shared_ref[...] = jnp.zeros_like(shared_ref)

    h = h_ref[...]
    rows, model = (h.shape[0], z_ref.shape[2])
    step = 512
    for at in range(0, model, step):
        part = dot_tn(h, z_ref[:, :, at : at + step].reshape(rows, step))
        out_ref[:, at : at + step] += part[: plan.units]
        shared_ref[:, at : at + step] += part[plan.units : plan.units + plan.shared]


def down_sum(plan, model, act, dout):
    chunks, tokens, cols = act.shape
    rows = dout.shape[2]
    tile = min(512, tokens)
    shapes = [(plan.units, model), (plan.shared, model)]
    return pl.pallas_call(
        functools.partial(sum_kernel, plan),
        grid=(chunks, tokens // tile),
        in_specs=[
            pl.BlockSpec((None, tile, cols), lambda h, i: (h, i, 0)),
            pl.BlockSpec((tile // rows, None, rows, model), lambda h, i: (i, h, 0, 0)),
        ],
        out_specs=[pl.BlockSpec(s, lambda h, i: (0, 0)) for s in shapes],
        out_shape=[jax.ShapeDtypeStruct(s, jnp.float32) for s in shapes],
        compiler_params=pltpu.CompilerParams(
            dimension_semantics=("arbitrary", "arbitrary"), vmem_limit_bytes=48 * MIB
        ),
        cost_estimate=pl.CostEstimate(
            flops=2 * chunks * tokens * cols * model,
            bytes_accessed=2 * chunks * tokens * (model + cols) + 4 * plan.units * model,
            transcendentals=0,
        ),
        name="down_sum",
    )(act, dout)


def pair_kernel(plan, h_ref, *refs):
    mid_refs, (gate_ref, up_ref, shared_ref) = (refs[:-3], refs[-3:])
    chunk = pl.program_id(0)

    @pl.when((chunk == 0) & (pl.program_id(1) == 0))
    def _():
        gate_ref[...] = jnp.zeros_like(gate_ref)
        up_ref[...] = jnp.zeros_like(up_ref)
        shared_ref[...] = jnp.zeros_like(shared_ref)

    even, tail, units, shared = (plan.even, plan.tail, plan.units, plan.shared)
    second = even + 2 * tail
    step = 256

    def add(z_ref):
        h = h_ref[...]
        for at in range(0, z_ref.shape[1], step):
            cut = slice(at, at + step)
            part = dot_tn(h, z_ref[:, cut])
            gate_ref[:, cut] += part[:units]
            lead = min(units, even)
            up_ref[:lead, cut] += part[second : second + lead]
            if units > even:
                up_ref[even:, cut] += part[even + tail : tail + units]
            joint = jnp.concatenate([part[second:], part[even + tail : second]])
            shared_ref[0, :, cut] += part[units : units + shared]
            shared_ref[1, :, cut] += joint[units : units + shared]

    for h, z_ref in enumerate(mid_refs):
        pl.when(chunk == h)(functools.partial(add, z_ref))


def pair_sum(plan, gud, mids):
    chunks, tokens, cols = gud.shape
    model = mids[0].shape[1]
    tile = min(512, tokens) if chunks <= 2 else 128
    steps = tokens // tile
    shapes = [(plan.units, model), (plan.units, model), (2, plan.shared, model)]

    def part(h):
        def place(c, i):
            return (jnp.where(c == h, i, jnp.where(c < h, 0, steps - 1)), 0)

        return pl.BlockSpec((tile, model), place)

    return pl.pallas_call(
        functools.partial(pair_kernel, plan),
        grid=(chunks, steps),
        in_specs=[pl.BlockSpec((None, tile, cols), lambda c, i: (c, i, 0))]
        + [part(h) for h in range(chunks)],
        out_specs=[
            pl.BlockSpec(s, lambda c, i, n=len(s): (0,) * n, pipeline_mode=pl.Buffered(1))
            for s in shapes
        ],
        out_shape=[jax.ShapeDtypeStruct(s, jnp.float32) for s in shapes],
        compiler_params=pltpu.CompilerParams(
            dimension_semantics=("arbitrary", "arbitrary"), vmem_limit_bytes=58 * MIB
        ),
        cost_estimate=pl.CostEstimate(
            flops=2 * chunks * tokens * cols * model,
            bytes_accessed=2 * chunks * tokens * (model + cols) + 8 * plan.units * model,
            transcendentals=0,
        ),
        name="pair_sum",
    )(gud, *mids)


def pack_kernel(lead, x_ref, heads_grad_ref, latent_ref, qr_ref, heads_ref, kv_ref, extra_ref, out_ref):
    bf16 = jnp.bfloat16
    first = dot_tn(x_ref[...], qr_ref[...])
    out_ref[:, : lead - 128] = first[:, : lead - 128].astype(bf16)
    out_ref[:, lead - 128 : lead] = (first[:, lead - 128 :] + extra_ref[...]).astype(bf16)
    latent = dot32(latent_ref[...], kv_ref[...])
    rows = latent.shape[0]
    pieces = out_ref.shape[0] // rows
    wide = kv_ref.shape[1] // pieces
    for k in range(pieces):
        out_ref[k * rows : (k + 1) * rows, lead : lead + wide] = latent[
            :, k * wide : (k + 1) * wide
        ].astype(bf16)
    out_ref[:, lead + wide :] = dot_tn(heads_grad_ref[...], heads_ref[...]).astype(bf16)


def packed_grads(groups, x_low, attn_low, latent_t, qr, heads_low, kv_grad, extra):
    count, model = x_low.shape
    depth = model // groups
    rows = latent_t.shape[0] // groups
    lead = qr.shape[1]
    wide = kv_grad.shape[1] * rows // depth
    cols = lead + wide + heads_low.shape[1]

    def whole(value):
        return pl.BlockSpec(value.shape, lambda i: (0, 0))

    return pl.pallas_call(
        functools.partial(pack_kernel, lead),
        grid=(groups,),
        in_specs=[
            pl.BlockSpec((count, depth), lambda i: (0, i)),
            pl.BlockSpec((count, depth), lambda i: (0, i)),
            pl.BlockSpec((rows, count), lambda i: (i, 0)),
            whole(qr),
            whole(heads_low),
            whole(kv_grad),
            pl.BlockSpec((depth, 128), lambda i: (i, 0)),
        ],
        out_specs=pl.BlockSpec((depth, cols), lambda i: (i, 0)),
        out_shape=jax.ShapeDtypeStruct((model, cols), jnp.bfloat16),
        compiler_params=pltpu.CompilerParams(
            dimension_semantics=("arbitrary",), vmem_limit_bytes=40 * MIB
        ),
        cost_estimate=pl.CostEstimate(
            flops=2 * count * model * cols, bytes_accessed=16 * MIB, transcendentals=0
        ),
        name="packed_grads",
    )(x_low, attn_low, latent_t, qr, heads_low, kv_grad, extra)


def per_device(
    tokens_in,
    cotangent,
    routes,
    segments,
    norm_in,
    w_query,
    w_latent,
    latent_gain,
    w_expand,
    w_output,
    norm_mid,
    w_router,
    shared_gate,
    shared_up,
    shared_down,
    expert_gate,
    routed_up_weight,
    expert_down,
):
    f32, bf16 = (jnp.float32, jnp.bfloat16)
    groups, lanes = (lax.axis_size("fsdp"), lax.axis_size("ctx"))
    group = lax.axis_index("fsdp")
    tok_dev, model_w = tokens_in.shape
    count = tok_dev * lanes
    depth = w_query.shape[0]
    query_c, expand_c, heads_c = (w_query.shape[1], w_expand.shape[1], w_output.shape[0])
    exp_dev, hidden, _ = expert_gate.shape
    experts_n, top_k = (w_router.shape[1], routes.shape[1])
    sh_units = shared_gate.shape[1] // groups
    plan = Plan(exp_dev, hidden, sh_units, experts_n, top_k)
    units = plan.units
    chunks = max(2, groups * count // 2048)
    width = query_c // (NOPE + ROPE)
    scale = (NOPE + ROPE) ** (-0.5)

    small_c = -(-(LAT + ROPE + experts_n + 3) // 128) * 128
    assert small_c - 128 <= LAT + ROPE
    at_router = LAT + ROPE
    at_seg = at_router + experts_n
    seg_cols = segments.astype(bf16).reshape(w_latent.shape[0], -1)
    spare = small_c - at_seg - seg_cols.shape[1]
    small = jnp.concatenate(
        [w_latent, w_router, seg_cols, jnp.zeros((w_latent.shape[0], spare), bf16)], axis=1
    )
    small = gather_ctx(small)
    seg_all = small[:, at_seg : at_seg + seg_cols.shape[1]].astype(jnp.int32).reshape(count)
    pieces = depth // w_expand.shape[0]
    wide = expand_c // pieces
    expand_blocks = [w_expand[:, k * wide : (k + 1) * wide] for k in range(pieces)]
    packed = jnp.concatenate(
        [w_query, small, jnp.concatenate(expand_blocks, axis=0), w_output.T], axis=1
    )
    packed = lax.all_gather(packed, "fsdp", axis=0, tiled=True)
    at_expand = query_c + small_c
    at_output = at_expand + wide
    query_w = packed[:, :query_c]
    latent_w = packed[:, query_c : query_c + LAT + ROPE]
    router_w = packed[:, query_c + LAT + ROPE : query_c + LAT + ROPE + experts_n]
    expand_w = (
        packed[:, at_expand:at_output]
        .reshape(groups, pieces, LAT // groups, wide)
        .transpose(0, 2, 1, 3)
        .reshape(LAT, expand_c)
    )
    output_wt = packed[:, at_output:]

    meta = jnp.concatenate(
        [routes.astype(bf16), jnp.zeros((tok_dev, 128 - top_k), bf16)], axis=1
    )
    dout_own, small = lax.optimization_barrier((jnp.concatenate([cotangent, meta], axis=1), small))
    dout_group = gather_ctx(dout_own)
    x_own, dout_group = lax.optimization_barrier((tokens_in, dout_group))
    x_all = gather_ctx(x_own)
    dout_all = lax.all_gather(dout_group, "fsdp", axis=0, tiled=True)
    dout_all = dout_all.reshape(groups * lanes, chunks, tok_dev // chunks, model_w + 128)

    shared = jnp.stack([shared_gate.T, shared_up.T, shared_down]).reshape(
        3, groups, sh_units, depth
    )
    shared = lax.all_to_all(shared, "fsdp", split_axis=1, concat_axis=1, tiled=True)
    shared = shared.transpose(0, 2, 1, 3).reshape(3, sh_units, model_w)
    x_all = after(x_all, shared)

    def hidden_rows(experts, mine, router):
        gap = jnp.zeros((plan.router - units - sh_units, model_w), bf16)
        end = jnp.zeros((plan.cols - plan.router - router.shape[0], model_w), bf16)
        return jnp.concatenate([experts.reshape(units, model_w), mine, gap, router, end])

    none = jnp.zeros((0, model_w), bf16)
    w1 = plan.join(
        hidden_rows(expert_gate, shared[0], router_w.T),
        hidden_rows(routed_up_weight, shared[1], none),
    )
    wd = hidden_rows(expert_down, shared[2], none)

    steps = jnp.arange(count, dtype=jnp.int32)
    same = seg_all[:, None] == seg_all[None, :]
    start = jnp.min(jnp.where(same, steps[None, :], count), axis=1)
    place = (steps - start).astype(f32)
    freq = THETA ** (-(jnp.arange(ROPE // 2, dtype=f32) * 2.0 / ROPE))
    angle = place[:, None] * freq[None, :]
    cosine, sine = (jnp.cos(angle), jnp.sin(angle))
    normed, unit_in, _ = norm_parts(x_all.astype(f32), norm_in)
    x_low = normed.astype(bf16)
    q_raw = dot32(x_low, query_w).reshape(count, width, NOPE + ROPE)
    q_nope = q_raw[..., :NOPE].astype(bf16)
    q_rope = turn(q_raw[..., NOPE:], cosine[:, None], sine[:, None]).astype(bf16)
    latent_raw = dot32(x_low, latent_w)
    latent_n, unit_lat, factor_lat = norm_parts(latent_raw[:, :LAT], latent_gain)
    latent_low = latent_n.astype(bf16)
    krope = turn(latent_raw[:, LAT:], cosine, sine).astype(bf16)
    kv_raw = dot32(latent_low, expand_w).astype(bf16).reshape(count, width, NOPE + VD)
    knope = kv_raw[..., :NOPE]
    values = kv_raw[..., NOPE:]
    raw = jnp.einsum("qhd,khd->hqk", q_nope, knope, preferred_element_type=f32)
    raw = raw + jnp.einsum("qhd,kd->hqk", q_rope, krope, preferred_element_type=f32)
    keep = same & (steps[None, :] <= steps[:, None])
    logits = jnp.where(keep[None], raw * scale, NEG_FILL)
    expo = jnp.exp(logits - jnp.max(logits, axis=-1, keepdims=True))
    probs = expo / jnp.sum(expo, axis=-1, keepdims=True)
    probs_low = probs.astype(bf16)
    heads_low = (
        jnp.einsum("hqk,khd->qhd", probs_low, values, preferred_element_type=f32)
        .astype(bf16)
        .reshape(count, heads_c)
    )
    resid = tokens_in.astype(f32) + scatter_ctx(dot_nt(heads_low, output_wt).astype(bf16))
    mid, unit_mid, factor_mid = norm_parts(resid, norm_mid)
    mid_low = mid.astype(bf16)

    first = (group * exp_dev).astype(jnp.int32)[None]
    part = tok_dev // chunks
    mids, rows_parts, rows_own, held = ([], [], [], ())
    last = dout_all
    for h in range(chunks):
        mid_part = gather_ctx(mid_low[h * part : (h + 1) * part])
        last = lax.all_gather(after(mid_part, last), "fsdp", axis=0, tiled=True)
        mids.append(last)
    for h in range(chunks):
        rows_part, *held = experts_back(plan, h, first, mids[h], dout_all, w1, wd, *held)
        rows_part = after(rows_part, last)
        last = lax.psum_scatter(rows_part, "fsdp", scatter_dimension=0, tiled=True)
        rows_parts.append(last)
    gud, act = held
    edown_grad, sdown_grad = down_sum(plan, model_w, act, dout_all)
    egate_grad, eup_grad, sgu_grad = pair_sum(plan, gud, mids)
    out_parts = [
        experts_out(plan, groups, lanes, h, 2, act, wd, edown_grad, egate_grad) for h in range(0, chunks, 2)
    ]
    rows_own = [scatter_ctx(rows) for rows in rows_parts]
    rows_grad = jnp.concatenate(rows_own)
    rows_grad = after(rows_grad, edown_grad, egate_grad, *out_parts)
    mid_grad = rows_grad[:, :model_w]
    gates_grad = (
        rows_grad[:, model_w : model_w + experts_n]
        + rows_grad[:, model_w + experts_n : model_w + 2 * experts_n]
    )

    sig = jax.nn.sigmoid(dot32(mid_low, router_w))
    hit = routes[:, :, None] == jnp.arange(experts_n, dtype=jnp.int32)[None, None, :]
    member = jnp.any(hit, axis=1).astype(f32)
    chosen_sum = jnp.sum(sig * member, axis=-1, keepdims=True)
    gates = ROUTE_SCALE * sig * member / chosen_sum
    spread = jnp.sum(gates_grad * gates, axis=-1, keepdims=True)
    chosen_grad = (ROUTE_SCALE * gates_grad - spread) / chosen_sum
    logit_grad = chosen_grad * member * sig * (1.0 - sig)
    router_grad = precise_tn(mid_low.astype(f32), logit_grad)
    mid_grad = mid_grad + precise_nt(logit_grad, router_w.astype(f32))
    resid_grad = norm_back(mid_grad, unit_mid, factor_mid, norm_mid) + cotangent.astype(f32)
    mid_gain_grad = jnp.sum(mid_grad * unit_mid, axis=0)
    attn_low = gather_ctx(resid_grad.astype(bf16))

    out_sums = []
    for out_part in out_parts:
        last = lax.psum_scatter(after(out_part, last), "fsdp", scatter_dimension=0, tiled=True)
        out_sums.append(last)
    moe = jnp.concatenate([scatter_ctx(rows) for rows in out_sums])
    block_out = (resid + moe).astype(bf16)
    shared_grad = jnp.concatenate([sgu_grad, sdown_grad[None]])[:, :sh_units].astype(bf16)
    shared_grad = shared_grad.reshape(3, sh_units, groups, depth).transpose(0, 2, 1, 3)
    shared_grad = lax.all_to_all(shared_grad, "fsdp", split_axis=1, concat_axis=1, tiled=True)
    shared_grad = shared_grad.reshape(3, sh_units * groups, depth).astype(f32)

    heads_grad = dot32(attn_low, output_wt).astype(bf16).reshape(count, width, VD)
    prob_grad = jnp.einsum("qhd,khd->hqk", heads_grad, values, preferred_element_type=f32)
    delta = jnp.sum(probs * prob_grad, axis=-1, keepdims=True)
    score_grad = (probs * (prob_grad - delta)).astype(bf16)
    q_nope_grad = jnp.einsum("hqk,khd->qhd", score_grad, knope, preferred_element_type=f32) * scale
    q_rope_grad = jnp.einsum("hqk,kd->qhd", score_grad, krope, preferred_element_type=f32) * scale
    knope_grad = jnp.einsum("hqk,qhd->khd", score_grad, q_nope, preferred_element_type=f32) * scale
    krope_grad = jnp.einsum("hqk,qhd->kd", score_grad, q_rope, preferred_element_type=f32) * scale
    values_grad = jnp.einsum("hqk,qhd->khd", probs_low, heads_grad, preferred_element_type=f32)
    q_raw_grad = (
        jnp.concatenate(
            [q_nope_grad, turn_back(q_rope_grad, cosine[:, None], sine[:, None])], axis=-1
        )
        .astype(bf16)
        .reshape(count, query_c)
    )
    kv_grad = (
        jnp.concatenate([knope_grad, values_grad], axis=-1).astype(bf16).reshape(count, expand_c)
    )
    latent_out_grad = dot_nt(kv_grad, expand_w)
    latent_gain_grad = jnp.sum(latent_out_grad * unit_lat, axis=0)
    latent_grad = norm_back(latent_out_grad, unit_lat, factor_lat, latent_gain)
    raw_grad = jnp.concatenate([latent_grad, turn_back(krope_grad, cosine, sine)], axis=-1).astype(
        bf16
    )
    qr_grad = jnp.concatenate(
        [q_raw_grad, raw_grad, jnp.zeros((count, small_c - LAT - ROPE), bf16)], axis=1
    )
    normed_grad = dot_nt(qr_grad, packed[:, :at_expand])
    in_gain_grad = jnp.sum(normed_grad * unit_in, axis=0)
    normed_own = scatter_ctx(normed_grad.astype(bf16))
    _, unit_own, factor_own = norm_parts(tokens_in.astype(f32), norm_in)
    grad_input = norm_back(normed_own, unit_own, factor_own, norm_in) + resid_grad

    latent_gain_col = jnp.pad(
        latent_gain_grad.reshape(groups * lanes, -1),
        ((0, 0), (0, depth // lanes - LAT // (groups * lanes))),
    ).reshape(model_w, 1)
    before = LAT + ROPE - (small_c - 128)
    extra = jnp.concatenate(
        [
            jnp.zeros((model_w, before), f32),
            router_grad,
            in_gain_grad[:, None],
            mid_gain_grad[:, None],
            latent_gain_col,
            jnp.zeros((model_w, 128 - before - experts_n - 3), f32),
        ],
        axis=1,
    )
    grads = packed_grads(
        groups, x_low, attn_low, latent_low.T, qr_grad, heads_low, kv_grad, extra
    )
    grads = lax.psum_scatter(after(grads, last), "fsdp", scatter_dimension=0, tiled=True)
    small_own = scatter_ctx(grads[:, query_c:at_expand])
    g_query = grads[:, :query_c].astype(f32)
    g_expand = grads[:, at_expand:at_output].astype(f32)
    g_expand = jnp.concatenate(
        [g_expand[k * w_expand.shape[0] : (k + 1) * w_expand.shape[0]] for k in range(pieces)],
        axis=1,
    )
    g_output = grads[:, at_output:].astype(f32).T
    at_gain = at_router + experts_n
    return (
        block_out,
        grad_input.astype(bf16),
        small_own[:, at_gain],
        g_query,
        small_own[:, :at_router],
        small_own[: LAT // (groups * lanes), at_gain + 2],
        g_expand,
        g_output,
        small_own[:, at_gain + 1],
        small_own[:, at_router:at_gain],
        shared_grad[0].T,
        shared_grad[1].T,
        shared_grad[2],
        egate_grad.reshape(expert_gate.shape),
        eup_grad.reshape(expert_gate.shape),
        edown_grad.reshape(expert_gate.shape),
    )


def solution(mesh):
    in_specs = (
        P(("fsdp", "ctx"), None),
        P(("fsdp", "ctx"), None),
        P(("fsdp", "ctx"), None),
        P(("fsdp", "ctx")),
        P(),
        P("fsdp", "ctx"),
        P(("fsdp", "ctx"), None),
        P(),
        P("fsdp", "ctx"),
        P("ctx", "fsdp"),
        P(),
        P(("fsdp", "ctx"), None),
        P("fsdp", "ctx"),
        P("fsdp", "ctx"),
        P("ctx", "fsdp"),
        P("fsdp", "ctx", None),
        P("fsdp", "ctx", None),
        P("fsdp", "ctx", None),
    )
    out_specs = (
        P(("fsdp", "ctx"), None),
        P(("fsdp", "ctx"), None),
        P(("fsdp", "ctx")),
        P("fsdp", "ctx"),
        P(("fsdp", "ctx"), None),
        P(("fsdp", "ctx")),
        P("fsdp", "ctx"),
        P("ctx", "fsdp"),
        P(("fsdp", "ctx")),
        P(("fsdp", "ctx"), None),
        P("fsdp", "ctx"),
        P("fsdp", "ctx"),
        P("ctx", "fsdp"),
        P("fsdp", "ctx", None),
        P("fsdp", "ctx", None),
        P("fsdp", "ctx", None),
    )
    return jax.shard_map(
        per_device, mesh=mesh, in_specs=in_specs, out_specs=out_specs, check_vma=False
    )
```

```python
import functools

import jax
import jax.numpy as jnp
from jax import lax
from jax.experimental import pallas as pl
from jax.experimental.pallas import tpu as pltpu
from jax.sharding import PartitionSpec as P

NOPE = 128
ROPE = 64
VD = 128
LAT = 512


EPS = 1e-06
THETA = 50000.0
ROUTE_SCALE = 2.446
MIB = 1024 * 1024
NEG_FILL = -1e30


def dot32(left, right):
    return jnp.dot(left, right, preferred_element_type=jnp.float32)


def dot_nt(left, right):
    return lax.dot_general(
        left, right, (((1,), (1,)), ((), ())), preferred_element_type=jnp.float32
    )


def dot_tn(left, right):
    return lax.dot_general(
        left, right, (((0,), (0,)), ((), ())), preferred_element_type=jnp.float32
    )


def precise_nt(left, right):
    return lax.dot_general(
        left,
        right,
        (((1,), (1,)), ((), ())),
        precision=lax.Precision.HIGHEST,
        preferred_element_type=jnp.float32,
    )


def precise_tn(left, right):
    return lax.dot_general(
        left,
        right,
        (((0,), (0,)), ((), ())),
        precision=lax.Precision.HIGHEST,
        preferred_element_type=jnp.float32,
    )


def norm_parts(value, gain):
    factor = lax.rsqrt(jnp.mean(value * value, axis=-1, keepdims=True) + EPS)
    unit = value * factor
    return (unit * gain, unit, factor)


def norm_back(grad_out, unit, factor, gain):
    grad_unit = grad_out * gain
    return factor * (grad_unit - unit * jnp.mean(grad_unit * unit, axis=-1, keepdims=True))


def turn(value, cosine, sine):
    half = value.shape[-1] // 2
    first, second = (value[..., :half], value[..., half:])
    return jnp.concatenate(
        [first * cosine - second * sine, second * cosine + first * sine], axis=-1
    )


def turn_back(grad, cosine, sine):
    half = grad.shape[-1] // 2
    first, second = (grad[..., :half], grad[..., half:])
    return jnp.concatenate(
        [first * cosine + second * sine, second * cosine - first * sine], axis=-1
    )


def silu_slope(value):
    sig = jax.nn.sigmoid(value)
    return (sig * (1.0 + value * (1.0 - sig)), value * sig)


def after(value, *others):
    return lax.optimization_barrier((value,) + others)[0]


def gather_ctx(value):
    lanes, lane = (lax.axis_size("ctx"), lax.axis_index("ctx"))
    rows = value.shape[0]
    whole = jnp.zeros((lanes * rows,) + value.shape[1:], value.dtype)
    whole = lax.dynamic_update_slice_in_dim(whole, value, lane * rows, 0)
    for hop in range(1, lanes):
        got = lax.ppermute(value, "ctx", [(i, (i + hop) % lanes) for i in range(lanes)])
        source = lax.rem(lane + lanes - hop, lanes)
        whole = lax.dynamic_update_slice_in_dim(whole, got, source * rows, 0)
    return whole


def scatter_ctx(value):
    lanes, lane = (lax.axis_size("ctx"), lax.axis_index("ctx"))
    rows = value.shape[0] // lanes
    total = lax.dynamic_slice_in_dim(value, lane * rows, rows, 0).astype(jnp.float32)
    for hop in range(1, lanes):
        target = lax.rem(lane + hop, lanes)
        part = lax.dynamic_slice_in_dim(value, target * rows, rows, 0)
        got = lax.ppermute(part, "ctx", [(i, (i + hop) % lanes) for i in range(lanes)])
        total = total + got.astype(jnp.float32)
    return total


class Plan:
    def __init__(self, exp_dev, hidden, shared, experts, top):
        self.exp_dev, self.hidden, self.experts, self.top = (exp_dev, hidden, experts, top)
        self.units = exp_dev * hidden
        self.shared = -(-shared // 8) * 8
        at = self.units + self.shared
        if at // 128 != (at + experts - 1) // 128:
            at = -(-at // 128) * 128
        self.router = at
        self.cols = -(-(at + experts) // 128) * 128
        self.even = (self.cols - 1) // 256 * 256
        self.tail = self.cols - self.even
        self.block = at // 128 * 128
        assert self.block >= self.even and self.block + 128 >= at + experts

    def join(self, gate, upper):
        return jnp.concatenate(
            [gate[: self.even], gate[self.even :], upper[self.even :], upper[: self.even]]
        )


def back_kernel(plan, first_ref, mid_ref, dout_ref, meta_ref, w1_ref, wd_ref, *refs):
    f32, bf16 = (jnp.float32, jnp.bfloat16)
    even, tail, hidden = (plan.even, plan.tail, plan.hidden)
    rows, model = mid_ref.shape
    rows_ref, gud_ref, act_ref = refs[-3:]
    mid = mid_ref[...]
    dout = dout_ref[...].reshape(rows, model)
    lanes = lax.broadcasted_iota(jnp.int32, (rows, 128), 1)
    off = plan.router - plan.block
    first = first_ref[0]
    sums = [jnp.zeros((rows, 128), f32) for _ in range(plan.exp_dev)]

    def elements(own, at, gate, upper, act_grad, gate_at, up_at):
        for b in range(0, gate.shape[1], 128):
            low = at + b
            g, u, da = (gate[:, b : b + 128], upper[:, b : b + 128], act_grad[:, b : b + 128])
            sig = jax.nn.sigmoid(g)
            swish = g * sig
            act = swish * u
            weighted = act * da
            scale = None
            for e in range(plan.exp_dev):
                start, stop = (e * hidden, (e + 1) * hidden)
                if stop <= low or start >= low + 128:
                    continue
                if start <= low and stop >= low + 128:
                    scale = own[e]
                    sums[e] = sums[e] + weighted
                else:
                    mine = (low + lanes >= start) & (low + lanes < stop)
                    sums[e] = sums[e] + jnp.where(mine, weighted, 0.0)
                    rest = jnp.ones((rows, 128), f32) if scale is None else scale
                    scale = jnp.where(mine, own[e], rest)
            if scale is not None:
                act = act * scale
                da = da * scale
            act_ref[:, low : low + 128] = act.astype(bf16)
            slope = sig + swish * (1.0 - sig)
            gud_ref[:, gate_at + b : gate_at + b + 128] = (da * u * slope).astype(bf16)
            gud_ref[:, up_at + b : up_at + b + 128] = (da * swish).astype(bf16)

    joint = dot_nt(mid, w1_ref[even : even + 2 * tail, :])
    at_block = plan.block - even
    sig = jax.nn.sigmoid(joint[:, at_block : at_block + 128])
    named = meta_ref[...].reshape(rows, 128).astype(f32)
    expert = (lanes - off).astype(f32)
    member = jnp.zeros((rows, 128), f32)
    for k in range(plan.top):
        member = jnp.where(expert == named[:, k : k + 1], 1.0, member)
    member = jnp.where((lanes >= off) & (lanes < off + plan.experts), member, 0.0)
    chosen = sig * member
    gates = ROUTE_SCALE * chosen / jnp.sum(chosen, axis=1, keepdims=True)
    own = [
        jnp.sum(jnp.where(lanes - off == first + e, gates, 0.0), axis=1, keepdims=True)
        for e in range(plan.exp_dev)
    ]
    act_grad = dot_nt(dout, wd_ref[even : even + tail, :])
    elements(own, even, joint[:, :tail], joint[:, tail:], act_grad, even, even + tail)
    for at in range(0, even, 256):
        up_at = even + 2 * tail + at
        elements(
            own,
            at,
            dot_nt(mid, w1_ref[at : at + 256, :]),
            dot_nt(mid, w1_ref[up_at : up_at + 256, :]),
            dot_nt(dout, wd_ref[at : at + 256, :]),
            at,
            up_at,
        )
    step = 512
    for at in range(0, model, step):
        rows_ref[:, at : at + step] = dot32(gud_ref[...], w1_ref[:, at : at + step]).astype(bf16)
    ends = jnp.zeros((rows, 128), f32)
    for e in range(plan.exp_dev):
        grad = jnp.sum(sums[e], axis=1, keepdims=True)
        high = grad.astype(bf16).astype(f32)
        ends = jnp.where(lanes == first + e, high, ends)
        ends = jnp.where(lanes == plan.experts + first + e, grad - high, ends)
    rows_ref[:, model:] = ends.astype(bf16)


def experts_back(plan, chunk, first, mid, dout, w1, wd, *held):
    tokens, model = mid.shape
    _, chunks, rows, _ = dout.shape
    tile = min(512, tokens)

    def row(width):
        return pl.BlockSpec((tile, width), lambda i: (i, 0))

    def slot(width):
        return pl.BlockSpec((None, tile, width), lambda i: (chunk, i, 0))

    def whole(value):
        return pl.BlockSpec(value.shape, lambda i: (0, 0), pipeline_mode=pl.Buffered(1))

    def outer(width, at):
        return pl.BlockSpec((tile // rows, None, rows, width), lambda i: (i, chunk, 0, at))

    bf16 = jnp.bfloat16
    return pl.pallas_call(
        functools.partial(back_kernel, plan),
        grid=(tokens // tile,),
        in_specs=[
            pl.BlockSpec(memory_space=pltpu.SMEM),
            row(model),
            outer(model, 0),
            outer(128, model // 128),
            whole(w1),
            whole(wd),
        ]
        + [pl.BlockSpec(memory_space=pl.ANY) for _ in held],
        out_specs=[row(model + 128), slot(2 * plan.cols), slot(plan.cols)],
        out_shape=[
            jax.ShapeDtypeStruct((tokens, model + 128), bf16),
            jax.ShapeDtypeStruct((chunks, tokens, 2 * plan.cols), bf16),
            jax.ShapeDtypeStruct((chunks, tokens, plan.cols), bf16),
        ],
        input_output_aliases={6 + n: 1 + n for n in range(len(held))},
        compiler_params=pltpu.CompilerParams(
            dimension_semantics=("arbitrary",), vmem_limit_bytes=58 * MIB
        ),
        cost_estimate=pl.CostEstimate(
            flops=10 * tokens * plan.cols * model,
            bytes_accessed=tokens * 6 * (model + plan.cols),
            transcendentals=tokens * plan.cols,
        ),
        name="experts_back",
    )(first, mid, dout, dout, w1, wd, *held)


def out_kernel(act_ref, wd_ref, *refs):
    out_ref = refs[-1]
    rows, model = (act_ref.shape[0], wd_ref.shape[1])
    act = act_ref[...]
    for at in range(0, model, 512):
        part = dot32(act, wd_ref[:, at : at + 512]).astype(jnp.bfloat16)
        out_ref[:, :, at : at + 512] = part.reshape(out_ref.shape[0], out_ref.shape[1], 512)


def experts_out(plan, groups, lanes, start, chunks, act, wd, *others):
    _, tokens, cols = act.shape
    model = wd.shape[1]
    count = tokens // groups
    rows = count // lanes
    return pl.pallas_call(
        out_kernel,
        grid=(chunks, groups),
        in_specs=[
            pl.BlockSpec((None, count, cols), lambda h, g: (start + h, g, 0)),
            pl.BlockSpec(wd.shape, lambda h, g: (0, 0), pipeline_mode=pl.Buffered(1)),
        ]
        + [pl.BlockSpec(memory_space=pl.ANY) for _ in others],
        out_specs=pl.BlockSpec((None, lanes, None, rows, model), lambda h, g: (g, 0, h, 0, 0)),
        out_shape=jax.ShapeDtypeStruct((groups, lanes, chunks, rows, model), jnp.bfloat16),
        compiler_params=pltpu.CompilerParams(
            dimension_semantics=("arbitrary", "arbitrary"), vmem_limit_bytes=32 * MIB
        ),
        cost_estimate=pl.CostEstimate(
            flops=2 * chunks * tokens * cols * model,
            bytes_accessed=2 * chunks * tokens * (cols + model),
            transcendentals=0,
        ),
        name="experts_out",
    )(act, wd, *others).reshape(groups * lanes * chunks * rows, model)


def sum_kernel(plan, h_ref, z_ref, out_ref, shared_ref):
    @pl.when((pl.program_id(0) == 0) & (pl.program_id(1) == 0))
    def _():
        out_ref[...] = jnp.zeros_like(out_ref)
        shared_ref[...] = jnp.zeros_like(shared_ref)

    h = h_ref[...]
    rows, model = (h.shape[0], z_ref.shape[2])
    step = 512
    for at in range(0, model, step):
        part = dot_tn(h, z_ref[:, :, at : at + step].reshape(rows, step))
        out_ref[:, at : at + step] += part[: plan.units]
        shared_ref[:, at : at + step] += part[plan.units : plan.units + plan.shared]


def down_sum(plan, model, act, dout):
    chunks, tokens, cols = act.shape
    rows = dout.shape[2]
    tile = min(512, tokens)
    shapes = [(plan.units, model), (plan.shared, model)]
    return pl.pallas_call(
        functools.partial(sum_kernel, plan),
        grid=(chunks, tokens // tile),
        in_specs=[
            pl.BlockSpec((None, tile, cols), lambda h, i: (h, i, 0)),
            pl.BlockSpec((tile // rows, None, rows, model), lambda h, i: (i, h, 0, 0)),
        ],
        out_specs=[pl.BlockSpec(s, lambda h, i: (0, 0)) for s in shapes],
        out_shape=[jax.ShapeDtypeStruct(s, jnp.float32) for s in shapes],
        compiler_params=pltpu.CompilerParams(
            dimension_semantics=("arbitrary", "arbitrary"), vmem_limit_bytes=48 * MIB
        ),
        cost_estimate=pl.CostEstimate(
            flops=2 * chunks * tokens * cols * model,
            bytes_accessed=2 * chunks * tokens * (model + cols) + 4 * plan.units * model,
            transcendentals=0,
        ),
        name="down_sum",
    )(act, dout)


def pair_kernel(plan, chunks, h_ref, *refs):
    mid_refs, (gate_ref, up_ref, shared_ref) = (refs[:chunks], refs[-3:])
    chunk = pl.program_id(0)

    @pl.when((chunk == 0) & (pl.program_id(1) == 0))
    def _():
        gate_ref[...] = jnp.zeros_like(gate_ref)
        up_ref[...] = jnp.zeros_like(up_ref)
        shared_ref[...] = jnp.zeros_like(shared_ref)

    even, tail, units, shared = (plan.even, plan.tail, plan.units, plan.shared)
    second = even + 2 * tail
    step = 256

    def add(z_ref):
        h = h_ref[...]
        for at in range(0, z_ref.shape[1], step):
            cut = slice(at, at + step)
            part = dot_tn(h, z_ref[:, cut])
            gate_ref[:, cut] += part[:units]
            lead = min(units, even)
            up_ref[:lead, cut] += part[second : second + lead]
            if units > even:
                up_ref[even:, cut] += part[even + tail : tail + units]
            joint = jnp.concatenate([part[second:], part[even + tail : second]])
            shared_ref[0, :, cut] += part[units : units + shared]
            shared_ref[1, :, cut] += joint[units : units + shared]

    for h, z_ref in enumerate(mid_refs):
        pl.when(chunk == h)(functools.partial(add, z_ref))


def pair_sum(plan, gud, mids, *others):
    chunks, tokens, cols = gud.shape
    model = mids[0].shape[1]
    tile = min(512, tokens) if chunks <= 2 else 128
    steps = tokens // tile
    shapes = [(plan.units, model), (plan.units, model), (2, plan.shared, model)]

    def part(h):
        def place(c, i):
            return (jnp.where(c == h, i, jnp.where(c < h, 0, steps - 1)), 0)

        return pl.BlockSpec((tile, model), place)

    return pl.pallas_call(
        functools.partial(pair_kernel, plan, chunks),
        grid=(chunks, steps),
        in_specs=[pl.BlockSpec((None, tile, cols), lambda c, i: (c, i, 0))]
        + [part(h) for h in range(chunks)]
        + [pl.BlockSpec(memory_space=pl.ANY) for _ in others],
        out_specs=[
            pl.BlockSpec(s, lambda c, i, n=len(s): (0,) * n, pipeline_mode=pl.Buffered(1))
            for s in shapes
        ],
        out_shape=[jax.ShapeDtypeStruct(s, jnp.float32) for s in shapes],
        compiler_params=pltpu.CompilerParams(
            dimension_semantics=("arbitrary", "arbitrary"), vmem_limit_bytes=58 * MIB
        ),
        cost_estimate=pl.CostEstimate(
            flops=2 * chunks * tokens * cols * model,
            bytes_accessed=2 * chunks * tokens * (model + cols) + 8 * plan.units * model,
            transcendentals=0,
        ),
        name="pair_sum",
    )(gud, *mids, *others)


def pack_kernel(lead, x_ref, heads_grad_ref, latent_ref, qr_ref, heads_ref, kv_ref, extra_ref, out_ref):
    bf16 = jnp.bfloat16
    first = dot_tn(x_ref[...], qr_ref[...])
    out_ref[:, : lead - 128] = first[:, : lead - 128].astype(bf16)
    out_ref[:, lead - 128 : lead] = (first[:, lead - 128 :] + extra_ref[...].T).astype(bf16)
    latent = dot32(latent_ref[...], kv_ref[...])
    rows = latent.shape[0]
    pieces = out_ref.shape[0] // rows
    wide = kv_ref.shape[1] // pieces
    for k in range(pieces):
        out_ref[k * rows : (k + 1) * rows, lead : lead + wide] = latent[
            :, k * wide : (k + 1) * wide
        ].astype(bf16)
    out_ref[:, lead + wide :] = dot_tn(heads_grad_ref[...], heads_ref[...]).astype(bf16)


def packed_grads(groups, x_low, attn_low, latent_t, qr, heads_low, kv_grad, extra):
    count, model = x_low.shape
    depth = model // groups
    rows = latent_t.shape[0] // groups
    lead = qr.shape[1]
    wide = kv_grad.shape[1] * rows // depth
    cols = lead + wide + heads_low.shape[1]

    def whole(value):
        return pl.BlockSpec(value.shape, lambda i: (0, 0))

    return pl.pallas_call(
        functools.partial(pack_kernel, lead),
        grid=(groups,),
        in_specs=[
            pl.BlockSpec((count, depth), lambda i: (0, i)),
            pl.BlockSpec((count, depth), lambda i: (0, i)),
            pl.BlockSpec((rows, count), lambda i: (i, 0)),
            whole(qr),
            whole(heads_low),
            whole(kv_grad),
            pl.BlockSpec((128, depth), lambda i: (0, i)),
        ],
        out_specs=pl.BlockSpec((depth, cols), lambda i: (i, 0)),
        out_shape=jax.ShapeDtypeStruct((model, cols), jnp.bfloat16),
        compiler_params=pltpu.CompilerParams(
            dimension_semantics=("arbitrary",), vmem_limit_bytes=40 * MIB
        ),
        cost_estimate=pl.CostEstimate(
            flops=2 * count * model * cols, bytes_accessed=16 * MIB, transcendentals=0
        ),
        name="packed_grads",
    )(x_low, attn_low, latent_t, qr, heads_low, kv_grad, extra)


class Heads:
    def __init__(self, width, groups, depth, small_c, wide, heads_c):
        self.width, self.groups, self.depth = (width, groups, depth)
        self.half = ROPE // 2
        self.flat = width * NOPE
        self.query = self.flat + 256
        self.lead = self.query + small_c
        self.wide = wide
        self.output = self.lead + wide
        self.cols = self.output + heads_c
        self.scale = (NOPE + ROPE) ** (-0.5)
        assert width * self.half <= 128 and small_c == LAT + 128

    def order(self):
        at = jnp.arange(self.query)[None, :]
        rotary = at - self.flat
        head, within = (rotary % 128 // self.half, rotary % 128 % self.half)
        turned = head * (NOPE + ROPE) + NOPE + rotary // 128 * self.half + within
        plain = at // NOPE * (NOPE + ROPE) + at % NOPE
        source = jnp.where(at < self.flat, plain, jnp.where(head < self.width, turned, -1))
        return (jnp.arange(self.width * (NOPE + ROPE))[:, None] == source).astype(jnp.bfloat16)


def expand_rows(heads, w_ref, expand_ref):
    rows = LAT // heads.groups
    for f in range(heads.groups):
        for k in range(heads.depth // rows):
            at = f * heads.depth + k * rows
            expand_ref[f * rows : (f + 1) * rows, k * heads.wide : (k + 1) * heads.wide] = w_ref[
                at : at + rows, heads.lead : heads.output
            ]


def head_parts(heads, h, lanes, q_ref, kv_ref, kr_ref):
    mine = (lanes % 128 >= h * heads.half) & (lanes % 128 < (h + 1) * heads.half)
    rotary = q_ref[:, heads.flat : heads.query]
    rotary = jnp.where(mine, rotary, jnp.zeros_like(rotary))
    query = jnp.concatenate([q_ref[:, h * NOPE : (h + 1) * NOPE], rotary], axis=1)
    at = h * (NOPE + VD)
    key = jnp.concatenate([kv_ref[:, at : at + NOPE], kr_ref[...]], axis=1)
    return (mine, query, key, kv_ref[:, at + NOPE : at + NOPE + VD])


def allowed(seg_col_ref, seg_row_ref):
    count = seg_col_ref.shape[0]
    rows = lax.broadcasted_iota(jnp.int32, (count, count), 0)
    cols = lax.broadcasted_iota(jnp.int32, (count, count), 1)
    return (seg_col_ref[...] == seg_row_ref[...]) & (cols <= rows)


def attend_kernel(heads, extra, x_ref, w_ref, cos_ref, sin_ref, seg_col_ref, seg_row_ref, gain_ref, *refs):
    q_ref, kv_ref, kr_ref, lat_ref, low_ref, lse_ref, heads_ref, attn_ref, expand_ref = refs[extra:]
    f32, bf16 = (jnp.float32, jnp.bfloat16)
    count = x_ref.shape[0]
    x = x_ref[...]
    cosine, sine = (cos_ref[...], sin_ref[...])
    query = dot32(x, w_ref[:, : heads.query])
    first = query[:, heads.flat : heads.flat + 128]
    second = query[:, heads.flat + 128 :]
    q_ref[:, : heads.flat] = query[:, : heads.flat].astype(bf16)
    q_ref[:, heads.flat : heads.flat + 128] = (first * cosine - second * sine).astype(bf16)
    q_ref[:, heads.flat + 128 :] = (second * cosine + first * sine).astype(bf16)
    latent = dot32(x, w_ref[:, heads.query : heads.lead])
    ends = latent[:, LAT:]
    latent = latent[:, :LAT]
    lat_ref[...] = latent
    factor = lax.rsqrt(jnp.mean(latent * latent, axis=-1, keepdims=True) + EPS)
    low_ref[...] = (latent * factor * gain_ref[...]).astype(bf16)
    lanes = lax.broadcasted_iota(jnp.int32, (count, 128), 1)
    half = heads.half

    def repeated(value):
        value = value + pltpu.roll(value, half, 1)
        return value + pltpu.roll(value, 2 * half, 1)

    first = repeated(jnp.where(lanes < half, ends, 0.0))
    second = repeated(jnp.where((lanes >= half) & (lanes < 2 * half), ends, 0.0))
    kr_ref[:, :128] = (first * cosine - second * sine).astype(bf16)
    kr_ref[:, 128:] = (second * cosine + first * sine).astype(bf16)
    expand_rows(heads, w_ref, expand_ref)
    kv_ref[...] = dot32(low_ref[...], expand_ref[...]).astype(bf16)
    keep = allowed(seg_col_ref, seg_row_ref)
    wide_lanes = lax.broadcasted_iota(jnp.int32, (count, 256), 1)
    lse = jnp.zeros((count, 128), f32)
    for h in range(heads.width):
        _, query, key, value = head_parts(heads, h, wide_lanes, q_ref, kv_ref, kr_ref)
        scores = jnp.where(keep, dot_nt(query, key) * heads.scale, NEG_FILL)
        peak = jnp.max(scores, axis=-1, keepdims=True)
        expo = jnp.exp(scores - peak)
        total = jnp.sum(expo, axis=-1, keepdims=True)
        lse = jnp.where(lanes == h, peak + jnp.log(total), lse)
        probs = (expo * (1.0 / total)).astype(bf16)
        heads_ref[:, h * VD : (h + 1) * VD] = dot32(probs, value).astype(bf16)
    lse_ref[...] = lse
    out = heads_ref[...]
    step = 512
    for at in range(0, attn_ref.shape[1], step):
        attn_ref[:, at : at + step] = dot_nt(out, w_ref[at : at + step, heads.output :]).astype(bf16)


def attend(heads, x_low, packed, cosine, sine, seg_col, seg_row, gain, *others):
    count, model = x_low.shape
    kv_c, heads_c = (heads.width * (NOPE + VD), heads.width * VD)
    f32, bf16 = (jnp.float32, jnp.bfloat16)
    shapes = [
        ((count, heads.query), bf16),
        ((count, kv_c), bf16),
        ((count, 256), bf16),
        ((count, LAT), f32),
        ((count, LAT), bf16),
        ((count, 128), f32),
        ((count, heads_c), bf16),
        ((count, model), bf16),
    ]
    vmem = pl.BlockSpec(memory_space=pltpu.VMEM)
    return pl.pallas_call(
        functools.partial(attend_kernel, heads, len(others)),
        in_specs=[vmem] * 7 + [pl.BlockSpec(memory_space=pl.ANY) for _ in others],
        out_specs=[vmem] * len(shapes),
        out_shape=[jax.ShapeDtypeStruct(*s) for s in shapes],
        scratch_shapes=[pltpu.VMEM((LAT, kv_c), bf16)],
        compiler_params=pltpu.CompilerParams(vmem_limit_bytes=58 * MIB),
        cost_estimate=pl.CostEstimate(
            flops=2 * count * (model * heads.cols + LAT * kv_c + heads.width * count * 512),
            bytes_accessed=2 * (model * heads.cols + 4 * count * model),
            transcendentals=heads.width * count * count,
        ),
        name="attend",
    )(x_low, packed, cosine, sine, seg_col, seg_row, gain, *others)


def attend_back_kernel(
    heads,
    extra,
    dattn_ref,
    x_ref,
    factor_ref,
    w_ref,
    cos_ref,
    sin_ref,
    seg_col_ref,
    seg_row_ref,
    gain_ref,
    q_ref,
    kv_ref,
    kr_ref,
    lat_ref,
    lse_ref,
    *refs,
):
    qr_ref, kvg_ref, normed_ref, in_gain_ref, lat_gain_ref, expand_ref = refs[extra:]
    f32, bf16 = (jnp.float32, jnp.bfloat16)
    count, model = x_ref.shape
    half = heads.half
    cosine, sine = (cos_ref[...], sin_ref[...])
    expand_rows(heads, w_ref, expand_ref)
    dheads = dot32(dattn_ref[...], w_ref[:, heads.output :]).astype(bf16)
    keep = allowed(seg_col_ref, seg_row_ref)
    lanes = lax.broadcasted_iota(jnp.int32, (count, 128), 1)
    wide_lanes = lax.broadcasted_iota(jnp.int32, (count, 256), 1)
    lse = lse_ref[...]
    dq_rot = jnp.zeros((count, 256), f32)
    dk_rot = jnp.zeros((count, 256), f32)
    for h in range(heads.width):
        mine, query, key, value = head_parts(heads, h, wide_lanes, q_ref, kv_ref, kr_ref)
        scores = jnp.where(keep, dot_nt(query, key) * heads.scale, NEG_FILL)
        probs = jnp.exp(scores - lse[:, h : h + 1])
        dhead = dheads[:, h * VD : (h + 1) * VD]
        dprobs = dot_nt(dhead, value)
        delta = jnp.sum(probs * dprobs, axis=-1, keepdims=True)
        dscores = (probs * (dprobs - delta)).astype(bf16)
        dquery = dot32(dscores, key) * heads.scale
        dkey = dot_tn(dscores, query) * heads.scale
        qr_ref[:, h * NOPE : (h + 1) * NOPE] = dquery[:, :NOPE].astype(bf16)
        dq_rot = dq_rot + jnp.where(mine, dquery[:, NOPE:], 0.0)
        dk_rot = dk_rot + dkey[:, NOPE:]
        at = h * (NOPE + VD)
        kvg_ref[:, at : at + NOPE] = dkey[:, :NOPE].astype(bf16)
        kvg_ref[:, at + NOPE : at + NOPE + VD] = dot_tn(probs.astype(bf16), dhead).astype(bf16)
    first, second = (dq_rot[:, :128], dq_rot[:, 128:])
    qr_ref[:, heads.flat : heads.flat + 128] = (first * cosine + second * sine).astype(bf16)
    qr_ref[:, heads.flat + 128 : heads.query] = (second * cosine - first * sine).astype(bf16)

    def folded(part):
        part = part + pltpu.roll(part, half, 1)
        return part + pltpu.roll(part, 2 * half, 1)

    first, second = (folded(dk_rot[:, :128]), folded(dk_rot[:, 128:]))
    ends = jnp.where(
        lanes < half,
        first * cosine + second * sine,
        jnp.where(lanes < 2 * half, second * cosine - first * sine, 0.0),
    )
    qr_ref[:, heads.query + LAT : heads.lead] = ends.astype(bf16)
    dlow = dot_nt(kvg_ref[...], expand_ref[...])
    latent = lat_ref[...]
    factor = lax.rsqrt(jnp.mean(latent * latent, axis=-1, keepdims=True) + EPS)
    unit = latent * factor
    lat_gain_ref[...] = jnp.sum(dlow * unit, axis=0, keepdims=True)
    dlatent = norm_back(dlow, unit, factor, gain_ref[...])
    qr_ref[:, heads.query : heads.query + LAT] = dlatent.astype(bf16)
    qr = qr_ref[...]
    step = 512
    for at in range(0, model, step):
        part = dot_nt(qr, w_ref[at : at + step, : heads.lead])
        normed_ref[:, at : at + step] = part.astype(bf16)
        unit_in = x_ref[:, at : at + step].astype(f32) * factor_ref[...]
        in_gain_ref[:, at : at + step] = jnp.sum(part * unit_in, axis=0, keepdims=True)


def attend_back(heads, *operands, others=()):
    count, model = operands[1].shape
    kv_c = heads.width * (NOPE + VD)
    f32, bf16 = (jnp.float32, jnp.bfloat16)
    shapes = [
        ((count, heads.lead), bf16),
        ((count, kv_c), bf16),
        ((count, model), bf16),
        ((1, model), f32),
        ((1, LAT), f32),
    ]
    vmem = pl.BlockSpec(memory_space=pltpu.VMEM)
    return pl.pallas_call(
        functools.partial(attend_back_kernel, heads, len(others)),
        in_specs=[vmem] * len(operands) + [pl.BlockSpec(memory_space=pl.ANY) for _ in others],
        out_specs=[vmem] * len(shapes),
        out_shape=[jax.ShapeDtypeStruct(*s) for s in shapes],
        scratch_shapes=[pltpu.VMEM((LAT, kv_c), bf16)],
        compiler_params=pltpu.CompilerParams(vmem_limit_bytes=58 * MIB),
        cost_estimate=pl.CostEstimate(
            flops=2 * count * (model * heads.cols + LAT * kv_c + heads.width * count * 1600),
            bytes_accessed=2 * (model * heads.cols + 4 * count * model),
            transcendentals=heads.width * count * count,
        ),
        name="attend_back",
    )(*operands, *others)


def per_device(
    tokens_in,
    cotangent,
    routes,
    segments,
    norm_in,
    w_query,
    w_latent,
    latent_gain,
    w_expand,
    w_output,
    norm_mid,
    w_router,
    shared_gate,
    shared_up,
    shared_down,
    expert_gate,
    routed_up_weight,
    expert_down,
):
    f32, bf16 = (jnp.float32, jnp.bfloat16)
    groups, lanes = (lax.axis_size("fsdp"), lax.axis_size("ctx"))
    group = lax.axis_index("fsdp")
    tok_dev, model_w = tokens_in.shape
    count = tok_dev * lanes
    depth = w_query.shape[0]
    query_c, expand_c, heads_c = (w_query.shape[1], w_expand.shape[1], w_output.shape[0])
    exp_dev, hidden, _ = expert_gate.shape
    experts_n, top_k = (w_router.shape[1], routes.shape[1])
    sh_units = shared_gate.shape[1] // groups
    plan = Plan(exp_dev, hidden, sh_units, experts_n, top_k)
    units = plan.units
    chunks = max(2, groups * count // 2048)
    width = query_c // (NOPE + ROPE)

    small_c = -(-(LAT + ROPE + experts_n + 3) // 128) * 128
    assert small_c - 128 <= LAT + ROPE
    at_router = LAT + ROPE
    at_seg = at_router + experts_n
    seg_cols = segments.astype(bf16).reshape(w_latent.shape[0], -1)
    spare = small_c - at_seg - seg_cols.shape[1]
    small = jnp.concatenate(
        [w_latent, w_router, seg_cols, jnp.zeros((w_latent.shape[0], spare), bf16)], axis=1
    )
    small = gather_ctx(small)
    seg_all = small[:, at_seg : at_seg + seg_cols.shape[1]].astype(jnp.int32).reshape(count)
    pieces = depth // w_expand.shape[0]
    wide = expand_c // pieces
    expand_blocks = [w_expand[:, k * wide : (k + 1) * wide] for k in range(pieces)]
    heads = Heads(width, groups, depth, small_c, wide, heads_c)
    order = heads.order()
    packed = jnp.concatenate(
        [dot32(w_query, order).astype(bf16), small, jnp.concatenate(expand_blocks, axis=0), w_output.T], axis=1
    )
    packed = lax.all_gather(packed, "fsdp", axis=0, tiled=True)
    at_expand = heads.lead
    at_output = heads.output
    at_first = heads.query + at_router
    router_w = packed[:, at_first : at_first + experts_n]

    meta = jnp.concatenate(
        [routes.astype(bf16), jnp.zeros((tok_dev, 128 - top_k), bf16)], axis=1
    )
    dout_own, small = lax.optimization_barrier((jnp.concatenate([cotangent, meta], axis=1), small))
    dout_group = gather_ctx(dout_own)
    dout_all = lax.all_gather(dout_group, "fsdp", axis=0, tiled=True)
    dout_all = dout_all.reshape(groups * lanes, chunks, tok_dev // chunks, model_w + 128)

    shared = jnp.stack([shared_gate.T, shared_up.T, shared_down]).reshape(
        3, groups, sh_units, depth
    )
    shared = lax.all_to_all(shared, "fsdp", split_axis=1, concat_axis=1, tiled=True)
    shared = shared.transpose(0, 2, 1, 3).reshape(3, sh_units, model_w)
    x_all = gather_ctx(after(tokens_in, shared))

    def hidden_rows(experts, mine, router):
        gap = jnp.zeros((plan.router - units - sh_units, model_w), bf16)
        end = jnp.zeros((plan.cols - plan.router - router.shape[0], model_w), bf16)
        return jnp.concatenate([experts.reshape(units, model_w), mine, gap, router, end])

    none = jnp.zeros((0, model_w), bf16)
    w1 = plan.join(
        hidden_rows(expert_gate, shared[0], router_w.T),
        hidden_rows(routed_up_weight, shared[1], none),
    )
    wd = hidden_rows(expert_down, shared[2], none)

    steps = jnp.arange(count, dtype=jnp.int32)
    same = seg_all[:, None] == seg_all[None, :]
    start = jnp.min(jnp.where(same, steps[None, :], count), axis=1)
    place = (steps - start).astype(f32)
    freq = THETA ** (-(jnp.arange(ROPE // 2, dtype=f32) * 2.0 / ROPE))
    angle = place[:, None] * freq[None, :]
    cosine, sine = (jnp.concatenate([f(angle)] * 4, axis=1) for f in (jnp.cos, jnp.sin))
    normed, _, factor_in = norm_parts(x_all.astype(f32), norm_in)
    x_low = normed.astype(bf16)
    fixed = (cosine, sine, seg_all[:, None], seg_all[None, :], latent_gain[None, :])
    q_low, kv_low, kr_low, latent_raw, latent_low, lse, heads_low, attn = attend(
        heads, x_low, packed, *fixed, wd
    )
    resid = after(tokens_in.astype(f32) + scatter_ctx(attn), w1)
    mid, unit_mid, factor_mid = norm_parts(resid, norm_mid)
    mid_low = mid.astype(bf16)

    first = (group * exp_dev).astype(jnp.int32)[None]
    part = tok_dev // chunks
    mids, rows_parts, rows_own, held = ([], [], [], ())
    last = dout_all
    for h in range(chunks):
        mid_part = gather_ctx(mid_low[h * part : (h + 1) * part])
        last = lax.all_gather(after(mid_part, last), "fsdp", axis=0, tiled=True)
        mids.append(last)
    for h in range(chunks):
        rows_part, *held = experts_back(plan, h, first, mids[h], dout_all, w1, wd, *held)
        rows_part = after(rows_part, last)
        last = lax.psum_scatter(rows_part, "fsdp", scatter_dimension=0, tiled=True)
        rows_parts.append(last)
    gud, act = held
    edown_grad, sdown_grad = down_sum(plan, model_w, act, dout_all)
    rows_own = [scatter_ctx(rows) for rows in rows_parts]

    early = (rows_own[0],) if chunks == 2 else ()
    egate_grad, eup_grad, sgu_grad = pair_sum(plan, gud, mids, edown_grad, *early)
    out_parts = [
        experts_out(plan, groups, lanes, h, 2, act, wd, egate_grad) for h in range(0, chunks, 2)
    ]
    rows_grad = jnp.concatenate(rows_own)
    rows_grad = after(rows_grad, egate_grad, *out_parts)
    mid_grad = rows_grad[:, :model_w]
    gates_grad = (
        rows_grad[:, model_w : model_w + experts_n]
        + rows_grad[:, model_w + experts_n : model_w + 2 * experts_n]
    )

    sig = jax.nn.sigmoid(dot32(mid_low, router_w))
    hit = routes[:, :, None] == jnp.arange(experts_n, dtype=jnp.int32)[None, None, :]
    member = jnp.any(hit, axis=1).astype(f32)
    chosen_sum = jnp.sum(sig * member, axis=-1, keepdims=True)
    gates = ROUTE_SCALE * sig * member / chosen_sum
    spread = jnp.sum(gates_grad * gates, axis=-1, keepdims=True)
    chosen_grad = (ROUTE_SCALE * gates_grad - spread) / chosen_sum
    logit_grad = chosen_grad * member * sig * (1.0 - sig)
    router_grad = precise_tn(logit_grad, mid_low.astype(f32))
    mid_grad = mid_grad + precise_nt(logit_grad, router_w.astype(f32))
    resid_grad = norm_back(mid_grad, unit_mid, factor_mid, norm_mid) + cotangent.astype(f32)
    mid_gain_grad = jnp.sum(mid_grad * unit_mid, axis=0, keepdims=True)
    attn_low = gather_ctx(resid_grad.astype(bf16))

    out_sums = []
    for out_part in out_parts:
        last = lax.psum_scatter(after(out_part, last), "fsdp", scatter_dimension=0, tiled=True)
        out_sums.append(last)
    moe = jnp.concatenate([scatter_ctx(rows) for rows in out_sums])
    block_out = (resid + moe).astype(bf16)

    qr_grad, kv_grad, normed_grad, in_gain_grad, latent_gain_grad = attend_back(
        heads,
        attn_low,
        x_all,
        factor_in,
        packed,
        *fixed,
        q_low,
        kv_low,
        kr_low,
        latent_raw,
        lse,
    )
    shared_grad = jnp.concatenate([sgu_grad, sdown_grad[None]])[:, :sh_units].astype(bf16)
    shared_grad = shared_grad.reshape(3, sh_units, groups, depth).transpose(0, 2, 1, 3)
    shared_grad = after(shared_grad, qr_grad)
    shared_grad = lax.all_to_all(shared_grad, "fsdp", split_axis=1, concat_axis=1, tiled=True)
    shared_grad = shared_grad.reshape(3, sh_units * groups, depth).astype(f32)
    normed_own = scatter_ctx(normed_grad)
    _, unit_own, factor_own = norm_parts(tokens_in.astype(f32), norm_in)
    grad_input = norm_back(normed_own, unit_own, factor_own, norm_in) + resid_grad

    latent_gain_row = jnp.pad(
        latent_gain_grad.reshape(groups * lanes, -1),
        ((0, 0), (0, depth // lanes - LAT // (groups * lanes))),
    ).reshape(1, model_w)
    before = LAT + ROPE - (small_c - 128)
    extra = jnp.concatenate(
        [
            jnp.zeros((before, model_w), f32),
            router_grad,
            mid_gain_grad,
            in_gain_grad,
            latent_gain_row,
            jnp.zeros((128 - before - experts_n - 3, model_w), f32),
        ]
    )
    grads = packed_grads(
        groups, x_low, attn_low, latent_low.T, qr_grad, heads_low, kv_grad, extra
    )
    grads = lax.psum_scatter(after(grads, last), "fsdp", scatter_dimension=0, tiled=True)
    small_own = scatter_ctx(grads[:, heads.query : at_expand])
    g_query = dot_nt(grads[:, : heads.query], order)
    g_expand = grads[:, at_expand:at_output].astype(f32)
    g_expand = jnp.concatenate(
        [g_expand[k * w_expand.shape[0] : (k + 1) * w_expand.shape[0]] for k in range(pieces)],
        axis=1,
    )
    g_output = grads[:, at_output:].astype(f32).T
    at_gain = at_router + experts_n
    return (
        block_out,
        grad_input.astype(bf16),
        small_own[:, at_gain + 1],
        g_query,
        small_own[:, :at_router],
        small_own[: LAT // (groups * lanes), at_gain + 2],
        g_expand,
        g_output,
        small_own[:, at_gain],
        small_own[:, at_router:at_gain],
        shared_grad[0].T,
        shared_grad[1].T,
        shared_grad[2],
        egate_grad.reshape(expert_gate.shape),
        eup_grad.reshape(expert_gate.shape),
        edown_grad.reshape(expert_gate.shape),
    )


def solution(mesh):
    in_specs = (
        P(("fsdp", "ctx"), None),
        P(("fsdp", "ctx"), None),
        P(("fsdp", "ctx"), None),
        P(("fsdp", "ctx")),
        P(),
        P("fsdp", "ctx"),
        P(("fsdp", "ctx"), None),
        P(),
        P("fsdp", "ctx"),
        P("ctx", "fsdp"),
        P(),
        P(("fsdp", "ctx"), None),
        P("fsdp", "ctx"),
        P("fsdp", "ctx"),
        P("ctx", "fsdp"),
        P("fsdp", "ctx", None),
        P("fsdp", "ctx", None),
        P("fsdp", "ctx", None),
    )
    out_specs = (
        P(("fsdp", "ctx"), None),
        P(("fsdp", "ctx"), None),
        P(("fsdp", "ctx")),
        P("fsdp", "ctx"),
        P(("fsdp", "ctx"), None),
        P(("fsdp", "ctx")),
        P("fsdp", "ctx"),
        P("ctx", "fsdp"),
        P(("fsdp", "ctx")),
        P(("fsdp", "ctx"), None),
        P("fsdp", "ctx"),
        P("fsdp", "ctx"),
        P("ctx", "fsdp"),
        P("fsdp", "ctx", None),
        P("fsdp", "ctx", None),
        P("fsdp", "ctx", None),
    )
    return jax.shard_map(
        per_device, mesh=mesh, in_specs=in_specs, out_specs=out_specs, check_vma=False
    )
```

```python
import functools

import jax
import jax.numpy as jnp
import numpy as np
from jax import lax
from jax.experimental import pallas as pl
from jax.experimental.pallas import tpu as pltpu
from jax.sharding import PartitionSpec as P

NOPE = 128
ROPE = 64
VD = 128
LAT = 512


EPS = 1e-06
THETA = 50000.0
ROUTE_SCALE = 2.446
MIB = 1024 * 1024
NEG_FILL = -1e30


def dot32(left, right):
    return jnp.dot(left, right, preferred_element_type=jnp.float32)


def dot_nt(left, right):
    return lax.dot_general(
        left, right, (((1,), (1,)), ((), ())), preferred_element_type=jnp.float32
    )


def dot_tn(left, right):
    return lax.dot_general(
        left, right, (((0,), (0,)), ((), ())), preferred_element_type=jnp.float32
    )


def precise_nt(left, right):
    return lax.dot_general(
        left,
        right,
        (((1,), (1,)), ((), ())),
        precision=lax.Precision.HIGHEST,
        preferred_element_type=jnp.float32,
    )


def precise_tn(left, right):
    return lax.dot_general(
        left,
        right,
        (((0,), (0,)), ((), ())),
        precision=lax.Precision.HIGHEST,
        preferred_element_type=jnp.float32,
    )


def norm_parts(value, gain):
    factor = lax.rsqrt(jnp.mean(value * value, axis=-1, keepdims=True) + EPS)
    unit = value * factor
    return (unit * gain, unit, factor)


def norm_back(grad_out, unit, factor, gain):
    grad_unit = grad_out * gain
    return factor * (grad_unit - unit * jnp.mean(grad_unit * unit, axis=-1, keepdims=True))


def turn(value, cosine, sine):
    half = value.shape[-1] // 2
    first, second = (value[..., :half], value[..., half:])
    return jnp.concatenate(
        [first * cosine - second * sine, second * cosine + first * sine], axis=-1
    )


def turn_back(grad, cosine, sine):
    half = grad.shape[-1] // 2
    first, second = (grad[..., :half], grad[..., half:])
    return jnp.concatenate(
        [first * cosine + second * sine, second * cosine - first * sine], axis=-1
    )


def silu_slope(value):
    sig = jax.nn.sigmoid(value)
    return (sig * (1.0 + value * (1.0 - sig)), value * sig)


def after(value, *others):
    return lax.optimization_barrier((value,) + others)[0]


def gather_ctx(value):
    lanes, lane = (lax.axis_size("ctx"), lax.axis_index("ctx"))
    rows = value.shape[0]
    whole = jnp.zeros((lanes * rows,) + value.shape[1:], value.dtype)
    whole = lax.dynamic_update_slice_in_dim(whole, value, lane * rows, 0)
    for hop in range(1, lanes):
        got = lax.ppermute(value, "ctx", [(i, (i + hop) % lanes) for i in range(lanes)])
        source = lax.rem(lane + lanes - hop, lanes)
        whole = lax.dynamic_update_slice_in_dim(whole, got, source * rows, 0)
    return whole


def pieces_ctx(value):
    lanes, lane = (lax.axis_size("ctx"), lax.axis_index("ctx"))
    rows = value.shape[0] // lanes
    got = [lax.dynamic_slice_in_dim(value, lane * rows, rows, 0)]
    for hop in range(1, lanes):
        target = lax.rem(lane + hop, lanes)
        part = lax.dynamic_slice_in_dim(value, target * rows, rows, 0)
        got.append(lax.ppermute(part, "ctx", [(i, (i + hop) % lanes) for i in range(lanes)]))
    return got


def total_of(pieces):
    total = pieces[0].astype(jnp.float32)
    for piece in pieces[1:]:
        total = total + piece.astype(jnp.float32)
    return total


def scatter_ctx(value):
    return total_of(pieces_ctx(value))


def spread_ctx(value):
    lanes = lax.axis_size("ctx")
    return [value] + [
        lax.ppermute(value, "ctx", [(i, (i + hop) % lanes) for i in range(lanes)])
        for hop in range(1, lanes)
    ]


class Plan:
    def __init__(self, exp_dev, hidden, shared, experts, top):
        self.exp_dev, self.hidden, self.experts, self.top = (2 * exp_dev, hidden, experts, top)
        self.units = exp_dev * hidden
        self.shared = -(-shared // 8) * 8
        at = 2 * (self.units + self.shared)
        if at // 128 != (at + experts - 1) // 128:
            at = -(-at // 128) * 128
        self.router = at
        self.cols = -(-(at + experts) // 128) * 128
        self.even = (self.cols - 1) // 256 * 256
        self.tail = self.cols - self.even
        self.block = at // 128 * 128
        assert self.block >= self.even and self.block + 128 >= at + experts

    def join(self, gate, upper):
        return jnp.concatenate(
            [gate[: self.even], gate[self.even :], upper[self.even :], upper[: self.even]]
        )


def back_kernel(plan, first_ref, mid_ref, dout_ref, meta_ref, w1_ref, wd_ref, *refs):
    f32, bf16 = (jnp.float32, jnp.bfloat16)
    even, tail, hidden = (plan.even, plan.tail, plan.hidden)
    rows, model = mid_ref.shape
    rows_ref, gud_ref, act_ref = refs[-3:]
    mid = mid_ref[...]
    dout = dout_ref[...].reshape(rows, model)
    lanes = lax.broadcasted_iota(jnp.int32, (rows, 128), 1)
    off = plan.router - plan.block
    sums = [jnp.zeros((rows, 128), f32) for _ in range(plan.exp_dev)]

    def elements(own, at, gate, upper, act_grad, gate_at, up_at):
        for b in range(0, gate.shape[1], 128):
            low = at + b
            g, u, da = (gate[:, b : b + 128], upper[:, b : b + 128], act_grad[:, b : b + 128])
            sig = jax.nn.sigmoid(g)
            swish = g * sig
            act = swish * u
            weighted = act * da
            scale = None
            for e in range(plan.exp_dev):
                start, stop = (e * hidden, (e + 1) * hidden)
                if stop <= low or start >= low + 128:
                    continue
                if start <= low and stop >= low + 128:
                    scale = own[e]
                    sums[e] = sums[e] + weighted
                else:
                    mine = (low + lanes >= start) & (low + lanes < stop)
                    sums[e] = sums[e] + jnp.where(mine, weighted, 0.0)
                    rest = jnp.ones((rows, 128), f32) if scale is None else scale
                    scale = jnp.where(mine, own[e], rest)
            if scale is not None:
                act = act * scale
                da = da * scale
            act_ref[:, low : low + 128] = act.astype(bf16)
            slope = sig + swish * (1.0 - sig)
            gud_ref[:, gate_at + b : gate_at + b + 128] = (da * u * slope).astype(bf16)
            gud_ref[:, up_at + b : up_at + b + 128] = (da * swish).astype(bf16)

    joint = dot_nt(mid, w1_ref[even : even + 2 * tail, :])
    at_block = plan.block - even
    sig = jax.nn.sigmoid(joint[:, at_block : at_block + 128])
    named = meta_ref[...].reshape(rows, 128).astype(f32)
    expert = (lanes - off).astype(f32)
    member = jnp.zeros((rows, 128), f32)
    for k in range(plan.top):
        member = jnp.where(expert == named[:, k : k + 1], 1.0, member)
    member = jnp.where((lanes >= off) & (lanes < off + plan.experts), member, 0.0)
    chosen = sig * member
    gates = ROUTE_SCALE * chosen / jnp.sum(chosen, axis=1, keepdims=True)
    own = [
        jnp.sum(jnp.where(lanes - off == first_ref[e], gates, 0.0), axis=1, keepdims=True)
        for e in range(plan.exp_dev)
    ]
    act_grad = dot_nt(dout, wd_ref[even : even + tail, :])
    elements(own, even, joint[:, :tail], joint[:, tail:], act_grad, even, even + tail)
    for at in range(0, even, 256):
        up_at = even + 2 * tail + at
        elements(
            own,
            at,
            dot_nt(mid, w1_ref[at : at + 256, :]),
            dot_nt(mid, w1_ref[up_at : up_at + 256, :]),
            dot_nt(dout, wd_ref[at : at + 256, :]),
            at,
            up_at,
        )
    step = 512
    for at in range(0, model, step):
        rows_ref[:, at : at + step] = dot32(gud_ref[...], w1_ref[:, at : at + step]).astype(bf16)
    ends = jnp.zeros((rows, 128), f32)
    for e in range(plan.exp_dev):
        grad = jnp.sum(sums[e], axis=1, keepdims=True)
        high = grad.astype(bf16).astype(f32)
        ends = jnp.where(lanes == first_ref[e], high, ends)
        ends = jnp.where(lanes == plan.experts + first_ref[e], grad - high, ends)
    rows_ref[:, model:] = ends.astype(bf16)


def experts_back(plan, chunk, first, mid, dout, w1, wd, *held):
    tokens, model = mid.shape
    _, chunks, rows, _ = dout.shape
    tile = min(512, tokens)

    def row(width):
        return pl.BlockSpec((tile, width), lambda i: (i, 0))

    def slot(width):
        return pl.BlockSpec((None, tile, width), lambda i: (chunk, i, 0))

    def whole(value):
        return pl.BlockSpec(value.shape, lambda i: (0, 0), pipeline_mode=pl.Buffered(1))

    def outer(width, at):
        return pl.BlockSpec((tile // rows, None, rows, width), lambda i: (i, chunk, 0, at))

    bf16 = jnp.bfloat16
    return pl.pallas_call(
        functools.partial(back_kernel, plan),
        grid=(tokens // tile,),
        in_specs=[
            pl.BlockSpec(memory_space=pltpu.SMEM),
            row(model),
            outer(model, 0),
            outer(128, model // 128),
            whole(w1),
            whole(wd),
        ]
        + [pl.BlockSpec(memory_space=pl.ANY) for _ in held],
        out_specs=[row(model + 128), slot(2 * plan.cols), slot(plan.cols)],
        out_shape=[
            jax.ShapeDtypeStruct((tokens, model + 128), bf16),
            jax.ShapeDtypeStruct((chunks, tokens, 2 * plan.cols), bf16),
            jax.ShapeDtypeStruct((chunks, tokens, plan.cols), bf16),
        ],
        input_output_aliases={6 + n: 1 + n for n in range(len(held))},
        compiler_params=pltpu.CompilerParams(
            dimension_semantics=("arbitrary",), vmem_limit_bytes=58 * MIB
        ),
        cost_estimate=pl.CostEstimate(
            flops=10 * tokens * plan.cols * model,
            bytes_accessed=tokens * 6 * (model + plan.cols),
            transcendentals=tokens * plan.cols,
        ),
        name="experts_back",
    )(first, mid, dout, dout, w1, wd, *held)


def out_kernel(act_ref, wd_ref, *refs):
    out_ref = refs[-1]
    rows, model = (act_ref.shape[0], wd_ref.shape[1])
    act = act_ref[...]
    for at in range(0, model, 512):
        part = dot32(act, wd_ref[:, at : at + 512]).astype(jnp.bfloat16)
        out_ref[:, :, at : at + 512] = part.reshape(out_ref.shape[0], out_ref.shape[1], 512)


def experts_out(plan, groups, lanes, start, chunks, act, wd, *others):
    _, tokens, cols = act.shape
    model = wd.shape[1]
    count = tokens // groups
    rows = count // lanes
    return pl.pallas_call(
        out_kernel,
        grid=(chunks, groups),
        in_specs=[
            pl.BlockSpec((None, count, cols), lambda h, g: (start + h, g, 0)),
            pl.BlockSpec(wd.shape, lambda h, g: (0, 0), pipeline_mode=pl.Buffered(1)),
        ]
        + [pl.BlockSpec(memory_space=pl.ANY) for _ in others],
        out_specs=pl.BlockSpec((None, lanes, None, rows, model), lambda h, g: (g, 0, h, 0, 0)),
        out_shape=jax.ShapeDtypeStruct((groups, lanes, chunks, rows, model), jnp.bfloat16),
        compiler_params=pltpu.CompilerParams(
            dimension_semantics=("arbitrary", "arbitrary"), vmem_limit_bytes=60 * MIB
        ),
        cost_estimate=pl.CostEstimate(
            flops=2 * chunks * tokens * cols * model,
            bytes_accessed=2 * chunks * tokens * (cols + model),
            transcendentals=0,
        ),
        name="experts_out",
    )(act, wd, *others).reshape(groups * lanes * chunks * rows, model)


def sum_kernel(plan, kind, chunks, h_ref, *refs):
    z_refs = refs[:chunks]
    out_ref, shared_ref, other_ref, other_shared_ref, total_ref = refs[-5:]
    chunk = pl.program_id(0)

    @pl.when((chunk == 0) & (pl.program_id(1) == 0))
    def _():
        out_ref[...] = jnp.zeros_like(out_ref)
        shared_ref[...] = jnp.zeros_like(shared_ref)
        total_ref[...] = jnp.zeros_like(total_ref)

    even, tail, units, shared = (plan.even, plan.tail, plan.units, plan.shared)
    model = out_ref.shape[1]
    step = 512

    def add(z_ref):
        h = h_ref[...]
        for at in range(0, model, step):
            cut = slice(at, at + step)
            if len(z_ref.shape) == 2:
                z = z_ref[:, cut]
            else:
                z = z_ref[:, :, cut].reshape(h.shape[0], step)
            part = dot_tn(h, z)
            if kind == "up":
                part = jnp.concatenate([part[tail:], part[:tail]])
            out_ref[:, cut] += part[:units]
            total_ref[:units, cut] += part[units : 2 * units]
            shared_ref[:, cut] += part[2 * units : 2 * units + shared]
            total_ref[units:, cut] += part[2 * units + shared : 2 * (units + shared)]

    for h, z_ref in enumerate(z_refs):
        pl.when(chunk == h)(functools.partial(add, z_ref))

    @pl.when((chunk == chunks - 1) & (pl.program_id(1) == pl.num_programs(1) - 1))
    def _():
        other_ref[...] = total_ref[:units].astype(jnp.bfloat16)
        other_shared_ref[...] = total_ref[units:].astype(jnp.bfloat16)


def weight_sum(plan, kind, model, hidden, rows, *others):
    chunks, tokens, width = hidden.shape
    cols = plan.cols
    tile = min(512, tokens) if chunks <= 2 else 256
    steps = tokens // tile
    shapes = [(plan.units, model), (plan.shared, model)] * 2
    types = [jnp.float32] * 2 + [jnp.bfloat16] * 2
    half = 1 if kind == "up" else 0

    def turn_of(h, c, i):
        return jnp.where(c == h, i, jnp.where(c < h, 0, steps - 1))

    if isinstance(rows, list):
        specs = [
            pl.BlockSpec((tile, model), lambda c, i, h=h: (turn_of(h, c, i), 0))
            for h in range(chunks)
        ]
    else:
        part = rows.shape[2]
        specs = [
            pl.BlockSpec(
                (tile // part, None, part, model), lambda c, i, h=h: (turn_of(h, c, i), h, 0, 0)
            )
            for h in range(chunks)
        ]
        rows = [rows] * chunks
    return pl.pallas_call(
        functools.partial(sum_kernel, plan, kind, chunks),
        grid=(chunks, steps),
        in_specs=[pl.BlockSpec((None, tile, cols), lambda c, i: (c, i, half))]
        + specs
        + [pl.BlockSpec(memory_space=pl.ANY) for _ in others],
        out_specs=[
            pl.BlockSpec(s, lambda c, i: (0, 0), pipeline_mode=pl.Buffered(1)) for s in shapes
        ],
        out_shape=[jax.ShapeDtypeStruct(*s) for s in zip(shapes, types)],
        scratch_shapes=[pltpu.VMEM((plan.units + plan.shared, model), jnp.float32)],
        compiler_params=pltpu.CompilerParams(
            dimension_semantics=("arbitrary", "arbitrary"), vmem_limit_bytes=58 * MIB
        ),
        cost_estimate=pl.CostEstimate(
            flops=2 * chunks * tokens * cols * model,
            bytes_accessed=2 * chunks * tokens * (model + cols) + 4 * plan.units * model,
            transcendentals=0,
        ),
        name=kind + "_sum",
    )(hidden, *rows, *others)


def pack_kernel(lead, before, x_ref, heads_grad_ref, latent_ref, qr_ref, heads_ref, kv_ref, early_ref, gains_ref, *refs):
    out_ref = refs[-1]
    bf16 = jnp.bfloat16
    first = dot_tn(x_ref[...], qr_ref[...])
    out_ref[:, : lead - 128] = first[:, : lead - 128].astype(bf16)
    early, cols = early_ref.shape
    small = jnp.concatenate(
        [
            jnp.zeros((before, cols), jnp.float32),
            early_ref[...],
            gains_ref[:2],
            jnp.zeros((128 - before - early - 2, cols), jnp.float32),
        ]
    )
    out_ref[:, lead - 128 : lead] = (first[:, lead - 128 :] + small.T).astype(bf16)
    latent = dot32(latent_ref[...], kv_ref[...])
    rows = latent.shape[0]
    pieces = out_ref.shape[0] // rows
    wide = kv_ref.shape[1] // pieces
    for k in range(pieces):
        out_ref[k * rows : (k + 1) * rows, lead : lead + wide] = latent[
            :, k * wide : (k + 1) * wide
        ].astype(bf16)
    out_ref[:, lead + wide :] = dot_tn(heads_grad_ref[...], heads_ref[...]).astype(bf16)


def packed_grads(groups, before, x_low, attn_low, latent_t, qr, heads_low, kv_grad, early, gains, *others):
    count, model = x_low.shape
    depth = model // groups
    rows = latent_t.shape[0] // groups
    lead = qr.shape[1]
    wide = kv_grad.shape[1] * rows // depth
    cols = lead + wide + heads_low.shape[1]

    def whole(value):
        return pl.BlockSpec(value.shape, lambda i: (0, 0))

    return pl.pallas_call(
        functools.partial(pack_kernel, lead, before),
        grid=(groups,),
        in_specs=[
            pl.BlockSpec((count, depth), lambda i: (0, i)),
            pl.BlockSpec((count, depth), lambda i: (0, i)),
            pl.BlockSpec((rows, count), lambda i: (i, 0)),
            whole(qr),
            whole(heads_low),
            whole(kv_grad),
            pl.BlockSpec((early.shape[0], depth), lambda i: (0, i)),
            pl.BlockSpec((8, depth), lambda i: (0, i)),
        ]
        + [pl.BlockSpec(memory_space=pl.ANY) for _ in others],
        out_specs=pl.BlockSpec((depth, cols), lambda i: (i, 0)),
        out_shape=jax.ShapeDtypeStruct((model, cols), jnp.bfloat16),
        compiler_params=pltpu.CompilerParams(
            dimension_semantics=("arbitrary",), vmem_limit_bytes=60 * MIB
        ),
        cost_estimate=pl.CostEstimate(
            flops=2 * count * model * cols, bytes_accessed=16 * MIB, transcendentals=0
        ),
        name="packed_grads",
    )(x_low, attn_low, latent_t, qr, heads_low, kv_grad, early, gains, *others)


def finish_kernel(own_ref, other_ref, *refs):
    refs[-1][...] = own_ref[...] + other_ref[...].astype(jnp.float32)


def finished(own, other, *others):
    rows, cols = own.shape
    block = pl.BlockSpec((rows // 4, cols), lambda i: (i, 0))
    return pl.pallas_call(
        finish_kernel,
        grid=(4,),
        in_specs=[block, block] + [pl.BlockSpec(memory_space=pl.ANY) for _ in others],
        out_specs=block,
        out_shape=jax.ShapeDtypeStruct((rows, cols), jnp.float32),
        input_output_aliases={0: 0},
        compiler_params=pltpu.CompilerParams(
            dimension_semantics=("arbitrary",), vmem_limit_bytes=48 * MIB
        ),
        cost_estimate=pl.CostEstimate(
            flops=rows * cols, bytes_accessed=10 * rows * cols, transcendentals=0
        ),
        name="finished",
    )(own, other, *others)


def end_kernel(pieces_n, resid_ref, grad_ref, x_ref, gain_ref, *refs):
    pieces, (out_ref, dx_ref) = (refs[:pieces_n], refs[-2:])
    f32, bf16 = (jnp.float32, jnp.bfloat16)
    model = x_ref.shape[1]
    moe = pieces[0][:, :model].astype(f32)
    dnormed = pieces[0][:, model:].astype(f32)
    for piece in pieces[1:]:
        moe = moe + piece[:, :model].astype(f32)
        dnormed = dnormed + piece[:, model:].astype(f32)
    out_ref[...] = (resid_ref[...] + moe).astype(bf16)
    _, unit, factor = norm_parts(x_ref[...].astype(f32), gain_ref[...])
    dx_ref[...] = (norm_back(dnormed, unit, factor, gain_ref[...]) + grad_ref[...]).astype(bf16)


def ends(pieces, resid, resid_grad, x, gain, *others):
    shape = jax.ShapeDtypeStruct(x.shape, jnp.bfloat16)
    vmem = pl.BlockSpec(memory_space=pltpu.VMEM)
    return pl.pallas_call(
        functools.partial(end_kernel, len(pieces)),
        in_specs=[vmem] * (4 + len(pieces)) + [pl.BlockSpec(memory_space=pl.ANY) for _ in others],
        out_specs=[vmem] * 2,
        out_shape=[shape] * 2,
        compiler_params=pltpu.CompilerParams(vmem_limit_bytes=48 * MIB),
        cost_estimate=pl.CostEstimate(
            flops=20 * x.size, bytes_accessed=30 * x.size, transcendentals=0
        ),
        name="ends",
    )(resid, resid_grad, x, gain, *pieces, *others)


class Heads:
    def __init__(self, width, groups, depth, small_c, wide, heads_c):
        self.width, self.groups, self.depth = (width, groups, depth)
        self.half = ROPE // 2
        self.flat = width * NOPE
        self.query = self.flat + 256
        self.lead = self.query + small_c
        self.wide = wide
        self.output = self.lead + wide
        self.cols = self.output + heads_c
        self.scale = (NOPE + ROPE) ** (-0.5)
        assert width * self.half <= 128 and small_c == LAT + 128

    def order(self):
        at = jnp.arange(self.query)[None, :]
        rotary = at - self.flat
        head, within = (rotary % 128 // self.half, rotary % 128 % self.half)
        turned = head * (NOPE + ROPE) + NOPE + rotary // 128 * self.half + within
        plain = at // NOPE * (NOPE + ROPE) + at % NOPE
        source = jnp.where(at < self.flat, plain, jnp.where(head < self.width, turned, -1))
        return (jnp.arange(self.width * (NOPE + ROPE))[:, None] == source).astype(jnp.bfloat16)


def expand_rows(heads, w_ref, expand_ref):
    rows = LAT // heads.groups
    for f in range(heads.groups):
        for k in range(heads.depth // rows):
            at = f * heads.depth + k * rows
            expand_ref[f * rows : (f + 1) * rows, k * heads.wide : (k + 1) * heads.wide] = w_ref[
                at : at + rows, heads.lead : heads.output
            ]


def head_parts(heads, h, lanes, q_ref, kv_ref, kr_ref):
    mine = (lanes % 128 >= h * heads.half) & (lanes % 128 < (h + 1) * heads.half)
    rotary = q_ref[:, heads.flat : heads.query]
    rotary = jnp.where(mine, rotary, jnp.zeros_like(rotary))
    query = jnp.concatenate([q_ref[:, h * NOPE : (h + 1) * NOPE], rotary], axis=1)
    at = h * (NOPE + VD)
    key = jnp.concatenate([kv_ref[:, at : at + NOPE], kr_ref[...]], axis=1)
    return (mine, query, key, kv_ref[:, at + NOPE : at + NOPE + VD])


def allowed(seg_col_ref, seg_row_ref):
    count = seg_col_ref.shape[0]
    rows = lax.broadcasted_iota(jnp.int32, (count, count), 0)
    cols = lax.broadcasted_iota(jnp.int32, (count, count), 1)
    return (seg_col_ref[...] == seg_row_ref[...]) & (cols <= rows)


def attend_kernel(heads, lanes_n, chunks, extra, lane_ref, in_gain_ref, w_ref, cos_ref, sin_ref, seg_col_ref, seg_row_ref, gain_ref, *refs):
    pieces = refs[:lanes_n]
    refs = refs[lanes_n + extra :]
    x_ref, x_low_ref, factor_ref, q_ref, kv_ref, kr_ref, lat_ref, low_t_ref, lse_ref, heads_ref = refs[:10]
    attn_refs, expand_ref = (refs[10:-1], refs[-1])
    f32, bf16 = (jnp.float32, jnp.bfloat16)
    count = x_ref.shape[0]
    block = count // lanes_n
    for hop, piece in enumerate(pieces):
        source = lax.rem(lane_ref[0] + lanes_n - hop, lanes_n)
        rows = pl.ds(pl.multiple_of(source * block, block), block)
        value = piece[...]
        x_ref[rows, :] = value
        value = value.astype(f32)
        scale = lax.rsqrt(jnp.mean(value * value, axis=-1, keepdims=True) + EPS)
        factor_ref[rows, :] = jnp.broadcast_to(scale, (block, 128))
        x_low_ref[rows, :] = (value * scale * in_gain_ref[...]).astype(bf16)
    x = x_low_ref[...]
    cosine, sine = (cos_ref[...], sin_ref[...])
    query = dot32(x, w_ref[:, : heads.query])
    first = query[:, heads.flat : heads.flat + 128]
    second = query[:, heads.flat + 128 :]
    q_ref[:, : heads.flat] = query[:, : heads.flat].astype(bf16)
    q_ref[:, heads.flat : heads.flat + 128] = (first * cosine - second * sine).astype(bf16)
    q_ref[:, heads.flat + 128 :] = (second * cosine + first * sine).astype(bf16)
    latent = dot32(x, w_ref[:, heads.query : heads.lead])
    ends = latent[:, LAT:]
    latent = latent[:, :LAT]
    lat_ref[...] = latent
    factor = lax.rsqrt(jnp.mean(latent * latent, axis=-1, keepdims=True) + EPS)
    low = latent * factor * gain_ref[...]
    low_t_ref[...] = low.T.astype(bf16)
    low = low.astype(bf16)
    lanes = lax.broadcasted_iota(jnp.int32, (count, 128), 1)
    half = heads.half

    def repeated(value):
        value = value + pltpu.roll(value, half, 1)
        return value + pltpu.roll(value, 2 * half, 1)

    first = repeated(jnp.where(lanes < half, ends, 0.0))
    second = repeated(jnp.where((lanes >= half) & (lanes < 2 * half), ends, 0.0))
    kr_ref[:, :128] = (first * cosine - second * sine).astype(bf16)
    kr_ref[:, 128:] = (second * cosine + first * sine).astype(bf16)
    expand_rows(heads, w_ref, expand_ref)
    kv_ref[...] = dot32(low, expand_ref[...]).astype(bf16)
    keep = allowed(seg_col_ref, seg_row_ref)
    wide_lanes = lax.broadcasted_iota(jnp.int32, (count, 256), 1)
    lse = jnp.zeros((count, 128), f32)
    for h in range(heads.width):
        _, query, key, value = head_parts(heads, h, wide_lanes, q_ref, kv_ref, kr_ref)
        scores = jnp.where(keep, dot_nt(query, key) * heads.scale, NEG_FILL)
        peak = jnp.max(scores, axis=-1, keepdims=True)
        expo = jnp.exp(scores - peak)
        total = jnp.sum(expo, axis=-1, keepdims=True)
        lse = jnp.where(lanes == h, peak + jnp.log(total), lse)
        probs = (expo * (1.0 / total)).astype(bf16)
        heads_ref[:, h * VD : (h + 1) * VD] = dot32(probs, value).astype(bf16)
    lse_ref[...] = lse
    out = heads_ref[...]
    step = 512
    rows, model = attn_refs[0].shape
    part = rows // lanes_n
    for at in range(0, model, step):
        cut = slice(at, at + step)
        piece = dot_nt(out, w_ref[cut, heads.output :]).astype(bf16)
        for c in range(chunks):
            for j in range(lanes_n):
                start = (j * chunks + c) * part
                attn_refs[c][j * part : (j + 1) * part, cut] = piece[start : start + part]


def attend(heads, chunks, lane, in_gain, packed, cosine, sine, seg_col, seg_row, gain, pieces, *others):
    lanes = len(pieces)
    count, model = (seg_col.shape[0], packed.shape[0])
    kv_c, heads_c = (heads.width * (NOPE + VD), heads.width * VD)
    f32, bf16 = (jnp.float32, jnp.bfloat16)
    shapes = [
        ((count, model), bf16),
        ((count, model), bf16),
        ((count, 128), f32),
        ((count, heads.query), bf16),
        ((count, kv_c), bf16),
        ((count, 256), bf16),
        ((count, LAT), f32),
        ((LAT, count), bf16),
        ((count, 128), f32),
        ((count, heads_c), bf16),
    ] + [((count // chunks, model), bf16)] * chunks
    vmem = pl.BlockSpec(memory_space=pltpu.VMEM)
    return pl.pallas_call(
        functools.partial(attend_kernel, heads, lanes, chunks, len(others)),
        in_specs=[pl.BlockSpec(memory_space=pltpu.SMEM)]
        + [vmem] * (7 + lanes)
        + [pl.BlockSpec(memory_space=pl.ANY) for _ in others],
        out_specs=[vmem] * len(shapes),
        out_shape=[jax.ShapeDtypeStruct(*s) for s in shapes],
        scratch_shapes=[pltpu.VMEM((LAT, kv_c), bf16)],
        compiler_params=pltpu.CompilerParams(vmem_limit_bytes=58 * MIB),
        cost_estimate=pl.CostEstimate(
            flops=2 * count * (model * heads.cols + LAT * kv_c + heads.width * count * 512),
            bytes_accessed=2 * (model * heads.cols + 4 * count * model),
            transcendentals=heads.width * count * count,
        ),
        name="attend",
    )(lane, in_gain, packed, cosine, sine, seg_col, seg_row, gain, *pieces, *others)


def attend_back_kernel(
    heads,
    extra,
    dattn_ref,
    x_ref,
    factor_ref,
    w_ref,
    cos_ref,
    sin_ref,
    seg_col_ref,
    seg_row_ref,
    gain_ref,
    q_ref,
    kv_ref,
    kr_ref,
    lat_ref,
    lse_ref,
    *refs,
):
    spread_ref = refs[0]
    qr_ref, kvg_ref, normed_ref, gains_ref, expand_ref = refs[1 + extra :]
    f32, bf16 = (jnp.float32, jnp.bfloat16)
    count, model = x_ref.shape
    half = heads.half
    cosine, sine = (cos_ref[...], sin_ref[...])
    expand_rows(heads, w_ref, expand_ref)
    dheads = dot32(dattn_ref[...], w_ref[:, heads.output :]).astype(bf16)
    keep = allowed(seg_col_ref, seg_row_ref)
    lanes = lax.broadcasted_iota(jnp.int32, (count, 128), 1)
    wide_lanes = lax.broadcasted_iota(jnp.int32, (count, 256), 1)
    lse = lse_ref[...]
    dq_rot = jnp.zeros((count, 256), f32)
    dk_rot = jnp.zeros((count, 256), f32)
    for h in range(heads.width):
        mine, query, key, value = head_parts(heads, h, wide_lanes, q_ref, kv_ref, kr_ref)
        scores = jnp.where(keep, dot_nt(query, key) * heads.scale, NEG_FILL)
        probs = jnp.exp(scores - lse[:, h : h + 1])
        dhead = dheads[:, h * VD : (h + 1) * VD]
        dprobs = dot_nt(dhead, value)
        delta = jnp.sum(probs * dprobs, axis=-1, keepdims=True)
        dscores = (probs * (dprobs - delta)).astype(bf16)
        dquery = dot32(dscores, key) * heads.scale
        dkey = dot_tn(dscores, query) * heads.scale
        qr_ref[:, h * NOPE : (h + 1) * NOPE] = dquery[:, :NOPE].astype(bf16)
        dq_rot = dq_rot + jnp.where(mine, dquery[:, NOPE:], 0.0)
        dk_rot = dk_rot + dkey[:, NOPE:]
        at = h * (NOPE + VD)
        kvg_ref[:, at : at + NOPE] = dkey[:, :NOPE].astype(bf16)
        kvg_ref[:, at + NOPE : at + NOPE + VD] = dot_tn(probs.astype(bf16), dhead).astype(bf16)
    first, second = (dq_rot[:, :128], dq_rot[:, 128:])
    qr_ref[:, heads.flat : heads.flat + 128] = (first * cosine + second * sine).astype(bf16)
    qr_ref[:, heads.flat + 128 : heads.query] = (second * cosine - first * sine).astype(bf16)

    def folded(part):
        part = part + pltpu.roll(part, half, 1)
        return part + pltpu.roll(part, 2 * half, 1)

    first, second = (folded(dk_rot[:, :128]), folded(dk_rot[:, 128:]))
    ends = jnp.where(
        lanes < half,
        first * cosine + second * sine,
        jnp.where(lanes < 2 * half, second * cosine - first * sine, 0.0),
    )
    qr_ref[:, heads.query + LAT : heads.lead] = ends.astype(bf16)
    dlow = dot_nt(kvg_ref[...], expand_ref[...])
    latent = lat_ref[...]
    factor = lax.rsqrt(jnp.mean(latent * latent, axis=-1, keepdims=True) + EPS)
    unit = latent * factor
    lat_gain = jnp.broadcast_to(jnp.sum(dlow * unit, axis=0, keepdims=True), (8, LAT))
    parts = []
    for _ in range(3):
        parts.append(lat_gain.astype(bf16).astype(f32))
        lat_gain = lat_gain - parts[-1]
    spread = dot32(jnp.concatenate(parts).astype(bf16), spread_ref[...])
    gains_ref[...] = spread[:8] + spread[8:16] + spread[16:]
    dlatent = norm_back(dlow, unit, factor, gain_ref[...])
    qr_ref[:, heads.query : heads.query + LAT] = dlatent.astype(bf16)
    qr = qr_ref[...]
    step = 512
    for at in range(0, model, step):
        part = dot_nt(qr, w_ref[at : at + step, : heads.lead])
        normed_ref[:, at : at + step] = part.astype(bf16)
        unit_in = x_ref[:, at : at + step].astype(f32) * factor_ref[:, :1]
        gains_ref[:1, at : at + step] = jnp.sum(part * unit_in, axis=0, keepdims=True)


def attend_back(heads, *operands, others=()):
    count, model = operands[1].shape
    kv_c = heads.width * (NOPE + VD)
    f32, bf16 = (jnp.float32, jnp.bfloat16)
    shapes = [
        ((count, heads.lead), bf16),
        ((count, kv_c), bf16),
        ((count, model), bf16),
        ((8, model), f32),
    ]
    vmem = pl.BlockSpec(memory_space=pltpu.VMEM)
    return pl.pallas_call(
        functools.partial(attend_back_kernel, heads, len(others)),
        in_specs=[vmem] * len(operands) + [pl.BlockSpec(memory_space=pl.ANY) for _ in others],
        out_specs=[vmem] * len(shapes),
        out_shape=[jax.ShapeDtypeStruct(*s) for s in shapes],
        scratch_shapes=[pltpu.VMEM((LAT, kv_c), bf16)],
        compiler_params=pltpu.CompilerParams(vmem_limit_bytes=60 * MIB),
        cost_estimate=pl.CostEstimate(
            flops=2 * count * (model * heads.cols + LAT * kv_c + heads.width * count * 1600),
            bytes_accessed=2 * (model * heads.cols + 4 * count * model),
            transcendentals=heads.width * count * count,
        ),
        name="attend_back",
    )(*operands, *others)


def per_device(
    tokens_in,
    cotangent,
    routes,
    segments,
    norm_in,
    w_query,
    w_latent,
    latent_gain,
    w_expand,
    w_output,
    norm_mid,
    w_router,
    shared_gate,
    shared_up,
    shared_down,
    expert_gate,
    routed_up_weight,
    expert_down,
):
    f32, bf16 = (jnp.float32, jnp.bfloat16)
    groups, lanes = (lax.axis_size("fsdp"), lax.axis_size("ctx"))
    halves = [list(range(k, groups, 2)) for k in (0, 1)]
    half = groups // 2

    def swap(value):
        return lax.ppermute(value, "fsdp", [(i, i ^ 1) for i in range(groups)])

    def gather_half(value):
        return lax.all_gather(value, "fsdp", axis=0, tiled=True, axis_index_groups=halves)

    def scatter_half(value):
        return lax.psum_scatter(
            value, "fsdp", scatter_dimension=0, tiled=True, axis_index_groups=halves
        )

    group = lax.axis_index("fsdp")
    tok_dev, model_w = tokens_in.shape
    count = tok_dev * lanes
    depth = w_query.shape[0]
    query_c, expand_c, heads_c = (w_query.shape[1], w_expand.shape[1], w_output.shape[0])
    exp_dev, hidden, _ = expert_gate.shape
    experts_n, top_k = (w_router.shape[1], routes.shape[1])
    sh_units = shared_gate.shape[1] // groups
    plan = Plan(exp_dev, hidden, sh_units, experts_n, top_k)
    units = plan.units
    chunks = max(2, groups * count // 2048)
    width = query_c // (NOPE + ROPE)

    small_c = -(-(LAT + ROPE + experts_n + 3) // 128) * 128
    assert small_c - 128 <= LAT + ROPE
    at_router = LAT + ROPE
    at_seg = at_router + experts_n
    seg_cols = segments.astype(bf16).reshape(w_latent.shape[0], -1)
    spare = small_c - at_seg - seg_cols.shape[1]
    small = jnp.concatenate(
        [w_latent, w_router, seg_cols, jnp.zeros((w_latent.shape[0], spare), bf16)], axis=1
    )
    small = gather_ctx(small)
    seg_all = small[:, at_seg : at_seg + seg_cols.shape[1]].astype(jnp.int32).reshape(count)
    pieces = depth // w_expand.shape[0]
    wide = expand_c // pieces
    expand_blocks = [w_expand[:, k * wide : (k + 1) * wide] for k in range(pieces)]
    heads = Heads(width, groups, depth, small_c, wide, heads_c)
    order = heads.order()
    packed = jnp.concatenate(
        [dot32(w_query, order).astype(bf16), small, jnp.concatenate(expand_blocks, axis=0), w_output.T], axis=1
    )
    packed = lax.all_gather(packed, "fsdp", axis=0, tiled=True)
    at_expand = heads.lead
    at_output = heads.output
    at_first = heads.query + at_router
    router_w = packed[:, at_first : at_first + experts_n]

    meta = jnp.concatenate(
        [routes.astype(bf16), jnp.zeros((tok_dev, 128 - top_k), bf16)], axis=1
    )
    dout_own = after(jnp.concatenate([cotangent, meta], axis=1), small)
    dout_group = gather_ctx(dout_own)
    dout_all = gather_half(dout_group)
    dout_all = dout_all.reshape(half * lanes, chunks, tok_dev // chunks, model_w + 128)

    x_pieces = spread_ctx(after(tokens_in, dout_group))

    steps = jnp.arange(count, dtype=jnp.int32)
    same = seg_all[:, None] == seg_all[None, :]
    start = jnp.min(jnp.where(same, steps[None, :], count), axis=1)
    place = (steps - start).astype(f32)
    freq = THETA ** (-(jnp.arange(ROPE // 2, dtype=f32) * 2.0 / ROPE))
    angle = place[:, None] * freq[None, :]
    cosine, sine = (jnp.concatenate([f(angle)] * 4, axis=1) for f in (jnp.cos, jnp.sin))
    fixed = (cosine, sine, seg_all[:, None], seg_all[None, :], latent_gain[None, :])
    lane = lax.axis_index("ctx").astype(jnp.int32)[None]
    x_all, x_low, factor_in, q_low, kv_low, kr_low, latent_raw, latent_low_t, lse, heads_low, *attn = (
        attend(heads, chunks, lane, norm_in[None, :], packed, *fixed, x_pieces)
    )
    def pair_weights(*others):
        shared = jnp.stack([shared_gate.T, shared_up.T, shared_down]).reshape(
            3, groups, sh_units, depth
        )
        shared, *pack = after((shared, expert_gate, routed_up_weight, expert_down), *others)
        shared = lax.all_to_all(shared, "fsdp", split_axis=1, concat_axis=1, tiled=True)
        shared = shared.transpose(0, 2, 1, 3).reshape(3, sh_units, model_w)

        if plan.shared > sh_units:
            shared = jnp.pad(shared, ((0, 0), (0, plan.shared - sh_units), (0, 0)))
        shared_pair = swap(shared)

        pack = [weights.reshape(units, model_w) for weights in pack]
        pair = [swap(weights) for weights in pack]

        def hidden_rows(k, router):
            gap = jnp.zeros((plan.router - 2 * (units + plan.shared), model_w), bf16)
            end = jnp.zeros((plan.cols - plan.router - router.shape[0], model_w), bf16)
            return jnp.concatenate([pack[k], pair[k], shared[k], shared_pair[k], gap, router, end])

        none = jnp.zeros((0, model_w), bf16)
        w1 = plan.join(
            hidden_rows(0, router_w.T),
            hidden_rows(1, none),
        )
        wd = hidden_rows(2, none)
        return (w1, wd)

    w1, wd = pair_weights(lse)

    own_experts = group * exp_dev + jnp.arange(exp_dev, dtype=jnp.int32)
    pair_experts = (group ^ 1) * exp_dev + jnp.arange(exp_dev, dtype=jnp.int32)
    first = jnp.concatenate([own_experts, pair_experts])
    part = tok_dev // chunks
    mids, rows_parts, held = ([], [], ())
    resid, unit_mid, factor_mid, mid_low = ([], [], [], [])
    last, sent = (dout_all, ())
    for h in range(chunks):
        rows = tokens_in[h * part : (h + 1) * part].astype(f32)
        attn_part = after(attn[h], *sent)
        resid.append(rows + scatter_ctx(attn_part))
        mid, unit, factor = norm_parts(resid[h], norm_mid)
        unit_mid.append(unit)
        factor_mid.append(factor)
        mid_low.append(mid.astype(bf16))
        mid_part = gather_ctx(mid_low[h])
        sent = (mid_part,)
        mid_part = after(mid_part, w1, wd)
        last = gather_half(after(mid_part, last))
        mids.append(last)
    for h in range(chunks):
        rows_part, *held = experts_back(plan, h, first, mids[h], dout_all, w1, wd, *held)
        rows_part = after(rows_part, last)
        last = scatter_half(rows_part)
        rows_parts.append(last)
    gud, act = held

    router_f = router_w.astype(f32)

    def middle_back(h, pieces, *others):
        own = total_of([after(pieces[0], *others)] + pieces[1:])
        rows = slice(h * part, (h + 1) * part)
        mid_grad = own[:, :model_w]
        gates_grad = (
            own[:, model_w : model_w + experts_n]
            + own[:, model_w + experts_n : model_w + 2 * experts_n]
        )
        sig = jax.nn.sigmoid(dot32(mid_low[h], router_w))
        hit = routes[rows, :, None] == jnp.arange(experts_n, dtype=jnp.int32)[None, None, :]
        member = jnp.any(hit, axis=1).astype(f32)
        chosen_sum = jnp.sum(sig * member, axis=-1, keepdims=True)
        gates = ROUTE_SCALE * sig * member / chosen_sum
        spread = jnp.sum(gates_grad * gates, axis=-1, keepdims=True)
        chosen_grad = (ROUTE_SCALE * gates_grad - spread) / chosen_sum
        logit_grad = chosen_grad * member * sig * (1.0 - sig)
        mid_grad = mid_grad + precise_nt(logit_grad, router_f)
        grad = norm_back(mid_grad, unit_mid[h], factor_mid[h], norm_mid)
        grad = grad + cotangent[rows].astype(f32)
        return (
            grad,
            grad.astype(bf16),
            jnp.sum(mid_grad * unit_mid[h], axis=0, keepdims=True),
            precise_tn(logit_grad, mid_low[h].astype(f32)),
        )

    def outputs(*others):
        return [
            experts_out(plan, half, lanes, h, 2, act, wd, *others) for h in range(0, chunks, 2)
        ]

    if chunks == 2:
        back = [middle_back(0, pieces_ctx(rows_parts[0]))]
        gate_sums = weight_sum(plan, "gate", model_w, gud, mids)
        attn_low = [gather_ctx(back[0][1])]
        out_parts = outputs(back[0][1], gate_sums[3])
        out_parts = [after(out_parts[0], attn_low[0])]
        back.append(middle_back(1, pieces_ctx(after(rows_parts[1], *out_parts))))
        down_sums = weight_sum(plan, "down", model_w, act, dout_all, rows_parts[1])
        attn_low.append(gather_ctx(back[1][1]))
        up_sums = weight_sum(plan, "up", model_w, gud, mids, back[1][1])
        early_swaps = [swap(gate_sums[2]), swap(down_sums[2])]
    else:
        gate_sums = weight_sum(plan, "gate", model_w, gud, mids)
        down_sums = weight_sum(plan, "down", model_w, act, dout_all)
        up_sums = weight_sum(plan, "up", model_w, gud, mids)
        out_parts = outputs(down_sums[3], gate_sums[3], up_sums[3])
        back = [middle_back(h, pieces_ctx(rows_parts[h])) for h in range(chunks)]
        attn_low = [gather_ctx(grad[1]) for grad in back]
        early_swaps = [swap(gate_sums[2]), swap(down_sums[2])]
    attn_low = jnp.stack([a.reshape(lanes, part, model_w) for a in attn_low], axis=1)
    attn_low = attn_low.reshape(count, model_w)
    resid_grad = jnp.concatenate([grad[0] for grad in back])
    mid_gain_grad = sum(grad[2] for grad in back)
    router_grad = sum(grad[3] for grad in back)

    out_sums = []
    for out_part in out_parts:
        last = scatter_half(after(out_part, last))
        out_sums.append(last)

    share = LAT // (groups * lanes)
    column = np.arange(model_w)[None, :]
    spot = column * lanes * groups // model_w * share + column % (depth // lanes)
    inside = column % (depth // lanes) < share
    spread = jnp.asarray(((np.arange(LAT)[:, None] == spot) & inside).astype(np.float32), bf16)
    qr_grad, kv_grad, normed_grad, gains = attend_back(
        heads,
        attn_low,
        x_all,
        factor_in,
        packed,
        *fixed,
        q_low,
        kv_low,
        kr_low,
        latent_raw,
        lse,
        spread,
        others=early_swaps + [up_sums[3]],
    )
    if chunks == 2:
        end_pieces = pieces_ctx(jnp.concatenate([out_sums[0], normed_grad], axis=1))
    else:
        moe = jnp.concatenate([scatter_ctx(rows) for rows in out_sums])
        end_pieces = pieces_ctx(normed_grad)
        normed_own = total_of(end_pieces)
        block_out = (jnp.concatenate(resid) + moe).astype(bf16)
    before = LAT + ROPE - (small_c - 128)
    early = jnp.concatenate([router_grad, mid_gain_grad])
    grads = packed_grads(
        groups,
        before,
        x_low,
        attn_low,
        latent_low_t,
        qr_grad,
        heads_low,
        kv_grad,
        early,
        gains,
    )
    all_sums = (gate_sums, up_sums, down_sums)
    swapped = (early_swaps[0], swap(up_sums[2]), early_swaps[1])
    expert_grads = [
        finished(sums[0], other, end_pieces[1]).reshape(expert_gate.shape)
        for sums, other in zip(all_sums, swapped)
    ]
    shared_other = swap(after(jnp.stack([sums[3] for sums in all_sums]), end_pieces[1]))
    shared_grad = jnp.stack([sums[1] for sums in all_sums]) + shared_other.astype(f32)
    shared_grad = shared_grad[:, :sh_units].astype(bf16)
    shared_grad = shared_grad.reshape(3, sh_units, groups, depth).transpose(0, 2, 1, 3)
    shared_grad = lax.all_to_all(shared_grad, "fsdp", split_axis=1, concat_axis=1, tiled=True)
    shared_grad = shared_grad.reshape(3, sh_units * groups, depth).astype(f32)
    if chunks == 2:
        block_out, grad_input = ends(
            end_pieces,
            jnp.concatenate(resid),
            resid_grad,
            tokens_in,
            norm_in[None, :],
            *expert_grads,
        )
    else:
        _, unit_own, factor_own = norm_parts(tokens_in.astype(f32), norm_in)
        grad_input = norm_back(normed_own, unit_own, factor_own, norm_in) + resid_grad
    grads = lax.psum_scatter(after(grads, last), "fsdp", scatter_dimension=0, tiled=True)
    small_own = scatter_ctx(grads[:, heads.query : at_expand])
    g_query = dot_nt(grads[:, : heads.query], order)
    g_expand = grads[:, at_expand:at_output].astype(f32)
    g_expand = jnp.concatenate(
        [g_expand[k * w_expand.shape[0] : (k + 1) * w_expand.shape[0]] for k in range(pieces)],
        axis=1,
    )
    g_output = grads[:, at_output:].astype(f32).T
    at_gain = at_router + experts_n
    return (
        block_out,
        grad_input.astype(bf16),
        small_own[:, at_gain + 1],
        g_query,
        small_own[:, :at_router],
        small_own[: LAT // (groups * lanes), at_gain + 2],
        g_expand,
        g_output,
        small_own[:, at_gain],
        small_own[:, at_router:at_gain],
        shared_grad[0].T,
        shared_grad[1].T,
        shared_grad[2],
        *expert_grads,
    )


def solution(mesh):
    in_specs = (
        P(("fsdp", "ctx"), None),
        P(("fsdp", "ctx"), None),
        P(("fsdp", "ctx"), None),
        P(("fsdp", "ctx")),
        P(),
        P("fsdp", "ctx"),
        P(("fsdp", "ctx"), None),
        P(),
        P("fsdp", "ctx"),
        P("ctx", "fsdp"),
        P(),
        P(("fsdp", "ctx"), None),
        P("fsdp", "ctx"),
        P("fsdp", "ctx"),
        P("ctx", "fsdp"),
        P("fsdp", "ctx", None),
        P("fsdp", "ctx", None),
        P("fsdp", "ctx", None),
    )
    out_specs = (
        P(("fsdp", "ctx"), None),
        P(("fsdp", "ctx"), None),
        P(("fsdp", "ctx")),
        P("fsdp", "ctx"),
        P(("fsdp", "ctx"), None),
        P(("fsdp", "ctx")),
        P("fsdp", "ctx"),
        P("ctx", "fsdp"),
        P(("fsdp", "ctx")),
        P(("fsdp", "ctx"), None),
        P("fsdp", "ctx"),
        P("fsdp", "ctx"),
        P("ctx", "fsdp"),
        P("fsdp", "ctx", None),
        P("fsdp", "ctx", None),
        P("fsdp", "ctx", None),
    )
    return jax.shard_map(
        per_device, mesh=mesh, in_specs=in_specs, out_specs=out_specs, check_vma=False
    )
```

```python
import functools

import jax
import jax.numpy as jnp
import numpy as np
from jax import lax
from jax.experimental import pallas as pl
from jax.experimental.pallas import tpu as pltpu
from jax.sharding import PartitionSpec as P

NOPE = 128
ROPE = 64
VD = 128
LAT = 512


EPS = 1e-06
THETA = 50000.0
ROUTE_SCALE = 2.446
MIB = 1024 * 1024
NEG_FILL = -1e30


def dot32(left, right):
    return jnp.dot(left, right, preferred_element_type=jnp.float32)


def dot_nt(left, right):
    return lax.dot_general(
        left, right, (((1,), (1,)), ((), ())), preferred_element_type=jnp.float32
    )


def dot_tn(left, right):
    return lax.dot_general(
        left, right, (((0,), (0,)), ((), ())), preferred_element_type=jnp.float32
    )


def precise_nt(left, right):
    return lax.dot_general(
        left,
        right,
        (((1,), (1,)), ((), ())),
        precision=lax.Precision.HIGHEST,
        preferred_element_type=jnp.float32,
    )


def precise_tn(left, right):
    return lax.dot_general(
        left,
        right,
        (((0,), (0,)), ((), ())),
        precision=lax.Precision.HIGHEST,
        preferred_element_type=jnp.float32,
    )


def norm_parts(value, gain):
    factor = lax.rsqrt(jnp.mean(value * value, axis=-1, keepdims=True) + EPS)
    unit = value * factor
    return (unit * gain, unit, factor)


def norm_back(grad_out, unit, factor, gain):
    grad_unit = grad_out * gain
    return factor * (grad_unit - unit * jnp.mean(grad_unit * unit, axis=-1, keepdims=True))


def turn(value, cosine, sine):
    half = value.shape[-1] // 2
    first, second = (value[..., :half], value[..., half:])
    return jnp.concatenate(
        [first * cosine - second * sine, second * cosine + first * sine], axis=-1
    )


def turn_back(grad, cosine, sine):
    half = grad.shape[-1] // 2
    first, second = (grad[..., :half], grad[..., half:])
    return jnp.concatenate(
        [first * cosine + second * sine, second * cosine - first * sine], axis=-1
    )


def silu_slope(value):
    sig = jax.nn.sigmoid(value)
    return (sig * (1.0 + value * (1.0 - sig)), value * sig)


def after(value, *others):
    return lax.optimization_barrier((value,) + others)[0]


def gather_ctx(value):
    lanes, lane = (lax.axis_size("ctx"), lax.axis_index("ctx"))
    rows = value.shape[0]
    whole = jnp.zeros((lanes * rows,) + value.shape[1:], value.dtype)
    whole = lax.dynamic_update_slice_in_dim(whole, value, lane * rows, 0)
    for hop in range(1, lanes):
        got = lax.ppermute(value, "ctx", [(i, (i + hop) % lanes) for i in range(lanes)])
        source = lax.rem(lane + lanes - hop, lanes)
        whole = lax.dynamic_update_slice_in_dim(whole, got, source * rows, 0)
    return whole


def pieces_ctx(value):
    lanes, lane = (lax.axis_size("ctx"), lax.axis_index("ctx"))
    rows = value.shape[0] // lanes
    got = [lax.dynamic_slice_in_dim(value, lane * rows, rows, 0)]
    for hop in range(1, lanes):
        target = lax.rem(lane + hop, lanes)
        part = lax.dynamic_slice_in_dim(value, target * rows, rows, 0)
        got.append(lax.ppermute(part, "ctx", [(i, (i + hop) % lanes) for i in range(lanes)]))
    return got


def total_of(pieces):
    total = pieces[0].astype(jnp.float32)
    for piece in pieces[1:]:
        total = total + piece.astype(jnp.float32)
    return total


def scatter_ctx(value):
    return total_of(pieces_ctx(value))


def spread_ctx(value):
    lanes = lax.axis_size("ctx")
    return [value] + [
        lax.ppermute(value, "ctx", [(i, (i + hop) % lanes) for i in range(lanes)])
        for hop in range(1, lanes)
    ]


class Plan:
    def __init__(self, exp_dev, hidden, shared, experts, top):
        self.exp_dev, self.hidden, self.experts, self.top = (2 * exp_dev, hidden, experts, top)
        self.units = exp_dev * hidden
        self.shared = -(-shared // 8) * 8
        at = 2 * (self.units + self.shared)
        if at // 128 != (at + experts - 1) // 128:
            at = -(-at // 128) * 128
        self.router = at
        self.cols = -(-(at + experts) // 128) * 128
        self.even = (self.cols - 1) // 256 * 256
        self.tail = self.cols - self.even
        self.block = at // 128 * 128
        assert self.block >= self.even and self.block + 128 >= at + experts

    def places(self, model):
        both, end = (2 * self.units, self.cols)
        up_at = self.even + 2 * self.tail
        head = self.even - both
        gate = [(0, self.units, 0), (0, self.units, self.units), (0, end - both, both)]
        up = [(0, self.units, up_at), (0, self.units, up_at + self.units)]
        up.append((head, self.tail, self.cols))
        if head:
            up.append((0, head, up_at + both))
        return (gate, up, gate)


def weight_copies(plan, pieces, w1_ref, wd_ref, sems):
    copies = ([], [], [])
    turn = 0
    for k, places in enumerate(plan.places(None)):
        target = wd_ref if k == 2 else w1_ref
        if target is None:
            continue
        for n, (start, rows, at) in enumerate(places):
            source = pieces[3 * k + min(n, 2)]
            copy = pltpu.make_async_copy(
                source.at[pl.ds(start, rows)], target.at[pl.ds(at, rows)], sems.at[turn]
            )
            copies[(1, 2, 0, 0)[n]].append(copy)
            turn += 1
    return copies


def back_kernel(plan, first_ref, mid_ref, dout_ref, meta_ref, *refs):
    f32, bf16 = (jnp.float32, jnp.bfloat16)
    even, tail, hidden = (plan.even, plan.tail, plan.hidden)
    rows, model = mid_ref.shape
    rows_ref, gud_ref, act_ref, w1_ref, wd_ref, sems = refs[-6:]
    step0 = pl.program_id(0) == 0
    copies = weight_copies(plan, refs[:9], w1_ref, wd_ref, sems)

    @pl.when(step0)
    def _():
        for group in copies:
            for copy in group:
                copy.start()

    def arrived(n):
        @pl.when(step0)
        def _():
            for copy in copies[n]:
                copy.wait()

    mid = mid_ref[...]
    dout = dout_ref[...].reshape(rows, model)
    lanes = lax.broadcasted_iota(jnp.int32, (rows, 128), 1)
    off = plan.router - plan.block
    sums = [jnp.zeros((rows, 128), f32) for _ in range(plan.exp_dev)]

    def elements(own, at, gate, upper, act_grad, gate_at, up_at):
        for b in range(0, gate.shape[1], 128):
            low = at + b
            g, u, da = (gate[:, b : b + 128], upper[:, b : b + 128], act_grad[:, b : b + 128])
            sig = jax.nn.sigmoid(g)
            swish = g * sig
            act = swish * u
            weighted = act * da
            scale = None
            for e in range(plan.exp_dev):
                start, stop = (e * hidden, (e + 1) * hidden)
                if stop <= low or start >= low + 128:
                    continue
                if start <= low and stop >= low + 128:
                    scale = own[e]
                    sums[e] = sums[e] + weighted
                else:
                    mine = (low + lanes >= start) & (low + lanes < stop)
                    sums[e] = sums[e] + jnp.where(mine, weighted, 0.0)
                    rest = jnp.ones((rows, 128), f32) if scale is None else scale
                    scale = jnp.where(mine, own[e], rest)
            if scale is not None:
                act = act * scale
                da = da * scale
            act_ref[:, low : low + 128] = act.astype(bf16)
            slope = sig + swish * (1.0 - sig)
            gud_ref[:, gate_at + b : gate_at + b + 128] = (da * u * slope).astype(bf16)
            gud_ref[:, up_at + b : up_at + b + 128] = (da * swish).astype(bf16)

    arrived(0)
    if even < 2 * plan.units:
        arrived(1)
        arrived(2)
    joint = dot_nt(mid, w1_ref[even : even + 2 * tail, :])
    at_block = plan.block - even
    sig = jax.nn.sigmoid(joint[:, at_block : at_block + 128])
    named = meta_ref[...].reshape(rows, 128).astype(f32)
    expert = (lanes - off).astype(f32)
    member = jnp.zeros((rows, 128), f32)
    for k in range(plan.top):
        member = jnp.where(expert == named[:, k : k + 1], 1.0, member)
    member = jnp.where((lanes >= off) & (lanes < off + plan.experts), member, 0.0)
    chosen = sig * member
    gates = ROUTE_SCALE * chosen / jnp.sum(chosen, axis=1, keepdims=True)
    own = [
        jnp.sum(jnp.where(lanes - off == first_ref[e], gates, 0.0), axis=1, keepdims=True)
        for e in range(plan.exp_dev)
    ]
    act_grad = dot_nt(dout, wd_ref[even : even + tail, :])
    elements(own, even, joint[:, :tail], joint[:, tail:], act_grad, even, even + tail)
    for at in range(0, even, 256):
        if even >= 2 * plan.units and at == 0:
            arrived(1)
        if even >= 2 * plan.units and at <= plan.units < at + 256:
            arrived(2)
        up_at = even + 2 * tail + at
        elements(
            own,
            at,
            dot_nt(mid, w1_ref[at : at + 256, :]),
            dot_nt(mid, w1_ref[up_at : up_at + 256, :]),
            dot_nt(dout, wd_ref[at : at + 256, :]),
            at,
            up_at,
        )
    step = 512
    for at in range(0, model, step):
        rows_ref[:, at : at + step] = dot32(gud_ref[...], w1_ref[:, at : at + step]).astype(bf16)
    ends = jnp.zeros((rows, 128), f32)
    for e in range(plan.exp_dev):
        grad = jnp.sum(sums[e], axis=1, keepdims=True)
        high = grad.astype(bf16).astype(f32)
        ends = jnp.where(lanes == first_ref[e], high, ends)
        ends = jnp.where(lanes == plan.experts + first_ref[e], grad - high, ends)
    rows_ref[:, model:] = ends.astype(bf16)


def experts_back(plan, chunk, first, mid, dout, pieces, *held):
    tokens, model = mid.shape
    _, chunks, rows, _ = dout.shape
    tile = min(512, tokens)

    def row(width):
        return pl.BlockSpec((tile, width), lambda i: (i, 0))

    def slot(width):
        return pl.BlockSpec((None, tile, width), lambda i: (chunk, i, 0))

    def outer(width, at):
        return pl.BlockSpec((tile // rows, None, rows, width), lambda i: (i, chunk, 0, at))

    bf16 = jnp.bfloat16
    return pl.pallas_call(
        functools.partial(back_kernel, plan),
        grid=(tokens // tile,),
        in_specs=[
            pl.BlockSpec(memory_space=pltpu.SMEM),
            row(model),
            outer(model, 0),
            outer(128, model // 128),
        ]
        + [pl.BlockSpec(memory_space=pl.ANY) for _ in (*pieces, *held)],
        out_specs=[row(model + 128), slot(2 * plan.cols), slot(plan.cols)],
        out_shape=[
            jax.ShapeDtypeStruct((tokens, model + 128), bf16),
            jax.ShapeDtypeStruct((chunks, tokens, 2 * plan.cols), bf16),
            jax.ShapeDtypeStruct((chunks, tokens, plan.cols), bf16),
        ],
        input_output_aliases={4 + len(pieces) + n: 1 + n for n in range(len(held))},
        scratch_shapes=[
            pltpu.VMEM((2 * plan.cols, model), bf16),
            pltpu.VMEM((plan.cols, model), bf16),
            pltpu.SemaphoreType.DMA((11,)),
        ],
        compiler_params=pltpu.CompilerParams(
            dimension_semantics=("arbitrary",), vmem_limit_bytes=58 * MIB
        ),
        cost_estimate=pl.CostEstimate(
            flops=10 * tokens * plan.cols * model,
            bytes_accessed=tokens * 6 * (model + plan.cols),
            transcendentals=tokens * plan.cols,
        ),
        name="experts_back",
    )(first, mid, dout, dout, *pieces, *held)


def out_kernel(plan, act_ref, *refs):
    out_ref, wd_ref, sems = refs[-3:]
    copies = weight_copies(plan, [None] * 6 + list(refs[:3]), None, wd_ref, sems)

    @pl.when((pl.program_id(0) == 0) & (pl.program_id(1) == 0))
    def _():
        for group in copies:
            for copy in group:
                copy.start()
        for group in copies:
            for copy in group:
                copy.wait()

    act = act_ref[...]
    for at in range(0, wd_ref.shape[1], 512):
        part = dot32(act, wd_ref[:, at : at + 512]).astype(jnp.bfloat16)
        out_ref[:, :, at : at + 512] = part.reshape(out_ref.shape[0], out_ref.shape[1], 512)


def experts_out(plan, groups, lanes, start, chunks, act, down, *others):
    _, tokens, cols = act.shape
    model = down[0].shape[1]
    count = tokens // groups
    rows = count // lanes
    return pl.pallas_call(
        functools.partial(out_kernel, plan),
        grid=(chunks, groups),
        in_specs=[
            pl.BlockSpec((None, count, cols), lambda h, g: (start + h, g, 0)),
        ]
        + [pl.BlockSpec(memory_space=pl.ANY) for _ in (*down, *others)],
        out_specs=pl.BlockSpec((None, lanes, None, rows, model), lambda h, g: (g, 0, h, 0, 0)),
        out_shape=jax.ShapeDtypeStruct((groups, lanes, chunks, rows, model), jnp.bfloat16),
        scratch_shapes=[
            pltpu.VMEM((plan.cols, model), jnp.bfloat16),
            pltpu.SemaphoreType.DMA((3,)),
        ],
        compiler_params=pltpu.CompilerParams(
            dimension_semantics=("arbitrary", "arbitrary"), vmem_limit_bytes=60 * MIB
        ),
        cost_estimate=pl.CostEstimate(
            flops=2 * chunks * tokens * cols * model,
            bytes_accessed=2 * chunks * tokens * (cols + model),
            transcendentals=0,
        ),
        name="experts_out",
    )(act, *down, *others).reshape(groups * lanes * chunks * rows, model)


def sum_kernel(plan, kind, chunks, h_ref, *refs):
    z_refs = refs[:chunks]
    out_ref, shared_ref, other_ref, other_shared_ref, total_ref = refs[-5:]
    chunk = pl.program_id(0)

    @pl.when((chunk == 0) & (pl.program_id(1) == 0))
    def _():
        out_ref[...] = jnp.zeros_like(out_ref)
        shared_ref[...] = jnp.zeros_like(shared_ref)
        total_ref[...] = jnp.zeros_like(total_ref)

    even, tail, units, shared = (plan.even, plan.tail, plan.units, plan.shared)
    model = out_ref.shape[1]
    step = 512

    def add(z_ref):
        h = h_ref[...]
        for at in range(0, model, step):
            cut = slice(at, at + step)
            if len(z_ref.shape) == 2:
                z = z_ref[:, cut]
            else:
                z = z_ref[:, :, cut].reshape(h.shape[0], step)
            part = dot_tn(h, z)
            if kind == "up":
                part = jnp.concatenate([part[tail:], part[:tail]])
            out_ref[:, cut] += part[:units]
            total_ref[:units, cut] += part[units : 2 * units]
            shared_ref[:, cut] += part[2 * units : 2 * units + shared]
            total_ref[units:, cut] += part[2 * units + shared : 2 * (units + shared)]

    for h, z_ref in enumerate(z_refs):
        pl.when(chunk == h)(functools.partial(add, z_ref))

    @pl.when((chunk == chunks - 1) & (pl.program_id(1) == pl.num_programs(1) - 1))
    def _():
        other_ref[...] = total_ref[:units].astype(jnp.bfloat16)
        other_shared_ref[...] = total_ref[units:].astype(jnp.bfloat16)


def weight_sum(plan, kind, model, hidden, rows, *others):
    chunks, tokens, width = hidden.shape
    cols = plan.cols
    tile = min(512, tokens) if chunks <= 2 else 256
    steps = tokens // tile
    shapes = [(plan.units, model), (plan.shared, model)] * 2
    types = [jnp.float32] * 2 + [jnp.bfloat16] * 2
    half = 1 if kind == "up" else 0

    def turn_of(h, c, i):
        return jnp.where(c == h, i, jnp.where(c < h, 0, steps - 1))

    if isinstance(rows, list):
        specs = [
            pl.BlockSpec((tile, model), lambda c, i, h=h: (turn_of(h, c, i), 0))
            for h in range(chunks)
        ]
    else:
        part = rows.shape[2]
        specs = [
            pl.BlockSpec(
                (tile // part, None, part, model), lambda c, i, h=h: (turn_of(h, c, i), h, 0, 0)
            )
            for h in range(chunks)
        ]
        rows = [rows] * chunks
    return pl.pallas_call(
        functools.partial(sum_kernel, plan, kind, chunks),
        grid=(chunks, steps),
        in_specs=[pl.BlockSpec((None, tile, cols), lambda c, i: (c, i, half))]
        + specs
        + [pl.BlockSpec(memory_space=pl.ANY) for _ in others],
        out_specs=[
            pl.BlockSpec(s, lambda c, i: (0, 0), pipeline_mode=pl.Buffered(1)) for s in shapes
        ],
        out_shape=[jax.ShapeDtypeStruct(*s) for s in zip(shapes, types)],
        scratch_shapes=[pltpu.VMEM((plan.units + plan.shared, model), jnp.float32)],
        compiler_params=pltpu.CompilerParams(
            dimension_semantics=("arbitrary", "arbitrary"), vmem_limit_bytes=58 * MIB
        ),
        cost_estimate=pl.CostEstimate(
            flops=2 * chunks * tokens * cols * model,
            bytes_accessed=2 * chunks * tokens * (model + cols) + 4 * plan.units * model,
            transcendentals=0,
        ),
        name=kind + "_sum",
    )(hidden, *rows, *others)


def pack_kernel(lead, before, x_ref, heads_grad_ref, latent_ref, qr_ref, heads_ref, kv_ref, early_ref, gains_ref, *refs):
    out_ref = refs[-1]
    bf16 = jnp.bfloat16
    first = dot_tn(x_ref[...], qr_ref[...])
    out_ref[:, : lead - 128] = first[:, : lead - 128].astype(bf16)
    early, cols = early_ref.shape
    small = jnp.concatenate(
        [
            jnp.zeros((before, cols), jnp.float32),
            early_ref[...],
            gains_ref[:2],
            jnp.zeros((128 - before - early - 2, cols), jnp.float32),
        ]
    )
    out_ref[:, lead - 128 : lead] = (first[:, lead - 128 :] + small.T).astype(bf16)
    latent = dot32(latent_ref[...], kv_ref[...])
    rows = latent.shape[0]
    pieces = out_ref.shape[0] // rows
    wide = kv_ref.shape[1] // pieces
    for k in range(pieces):
        out_ref[k * rows : (k + 1) * rows, lead : lead + wide] = latent[
            :, k * wide : (k + 1) * wide
        ].astype(bf16)
    out_ref[:, lead + wide :] = dot_tn(heads_grad_ref[...], heads_ref[...]).astype(bf16)


def packed_grads(groups, before, x_low, attn_low, latent_t, qr, heads_low, kv_grad, early, gains, *others):
    count, model = x_low.shape
    depth = model // groups
    rows = latent_t.shape[0] // groups
    lead = qr.shape[1]
    wide = kv_grad.shape[1] * rows // depth
    cols = lead + wide + heads_low.shape[1]

    def whole(value):
        return pl.BlockSpec(value.shape, lambda i: (0, 0))

    return pl.pallas_call(
        functools.partial(pack_kernel, lead, before),
        grid=(groups,),
        in_specs=[
            pl.BlockSpec((count, depth), lambda i: (0, i)),
            pl.BlockSpec((count, depth), lambda i: (0, i)),
            pl.BlockSpec((rows, count), lambda i: (i, 0)),
            whole(qr),
            whole(heads_low),
            whole(kv_grad),
            pl.BlockSpec((early.shape[0], depth), lambda i: (0, i)),
            pl.BlockSpec((8, depth), lambda i: (0, i)),
        ]
        + [pl.BlockSpec(memory_space=pl.ANY) for _ in others],
        out_specs=pl.BlockSpec((depth, cols), lambda i: (i, 0)),
        out_shape=jax.ShapeDtypeStruct((model, cols), jnp.bfloat16),
        compiler_params=pltpu.CompilerParams(
            dimension_semantics=("arbitrary",), vmem_limit_bytes=60 * MIB
        ),
        cost_estimate=pl.CostEstimate(
            flops=2 * count * model * cols, bytes_accessed=16 * MIB, transcendentals=0
        ),
        name="packed_grads",
    )(x_low, attn_low, latent_t, qr, heads_low, kv_grad, early, gains, *others)


def finish_kernel(own_ref, other_ref, *refs):
    refs[-1][...] = own_ref[...] + other_ref[...].astype(jnp.float32)


def finished(own, other, *others):
    rows, cols = own.shape
    block = pl.BlockSpec((rows // 4, cols), lambda i: (i, 0))
    return pl.pallas_call(
        finish_kernel,
        grid=(4,),
        in_specs=[block, block] + [pl.BlockSpec(memory_space=pl.ANY) for _ in others],
        out_specs=block,
        out_shape=jax.ShapeDtypeStruct((rows, cols), jnp.float32),
        input_output_aliases={0: 0},
        compiler_params=pltpu.CompilerParams(
            dimension_semantics=("arbitrary",), vmem_limit_bytes=48 * MIB
        ),
        cost_estimate=pl.CostEstimate(
            flops=rows * cols, bytes_accessed=10 * rows * cols, transcendentals=0
        ),
        name="finished",
    )(own, other, *others)


def end_kernel(pieces_n, resid_ref, grad_ref, x_ref, gain_ref, *refs):
    pieces, (out_ref, dx_ref) = (refs[:pieces_n], refs[-2:])
    f32, bf16 = (jnp.float32, jnp.bfloat16)
    model = x_ref.shape[1]
    moe = pieces[0][:, :model].astype(f32)
    dnormed = pieces[0][:, model:].astype(f32)
    for piece in pieces[1:]:
        moe = moe + piece[:, :model].astype(f32)
        dnormed = dnormed + piece[:, model:].astype(f32)
    out_ref[...] = (resid_ref[...] + moe).astype(bf16)
    _, unit, factor = norm_parts(x_ref[...].astype(f32), gain_ref[...])
    dx_ref[...] = (norm_back(dnormed, unit, factor, gain_ref[...]) + grad_ref[...]).astype(bf16)


def ends(pieces, resid, resid_grad, x, gain, *others):
    shape = jax.ShapeDtypeStruct(x.shape, jnp.bfloat16)
    vmem = pl.BlockSpec(memory_space=pltpu.VMEM)
    return pl.pallas_call(
        functools.partial(end_kernel, len(pieces)),
        in_specs=[vmem] * (4 + len(pieces)) + [pl.BlockSpec(memory_space=pl.ANY) for _ in others],
        out_specs=[vmem] * 2,
        out_shape=[shape] * 2,
        compiler_params=pltpu.CompilerParams(vmem_limit_bytes=48 * MIB),
        cost_estimate=pl.CostEstimate(
            flops=20 * x.size, bytes_accessed=30 * x.size, transcendentals=0
        ),
        name="ends",
    )(resid, resid_grad, x, gain, *pieces, *others)


class Heads:
    def __init__(self, width, groups, depth, small_c, wide, heads_c):
        self.width, self.groups, self.depth = (width, groups, depth)
        self.half = ROPE // 2
        self.flat = width * NOPE
        self.query = self.flat + 256
        self.lead = self.query + small_c
        self.wide = wide
        self.output = self.lead + wide
        self.cols = self.output + heads_c
        self.scale = (NOPE + ROPE) ** (-0.5)
        assert width * self.half <= 128 and small_c == LAT + 128

    def order(self):
        at = jnp.arange(self.query)[None, :]
        rotary = at - self.flat
        head, within = (rotary % 128 // self.half, rotary % 128 % self.half)
        turned = head * (NOPE + ROPE) + NOPE + rotary // 128 * self.half + within
        plain = at // NOPE * (NOPE + ROPE) + at % NOPE
        source = jnp.where(at < self.flat, plain, jnp.where(head < self.width, turned, -1))
        return (jnp.arange(self.width * (NOPE + ROPE))[:, None] == source).astype(jnp.bfloat16)


def expand_rows(heads, w_ref, expand_ref):
    rows = LAT // heads.groups
    for f in range(heads.groups):
        for k in range(heads.depth // rows):
            at = f * heads.depth + k * rows
            expand_ref[f * rows : (f + 1) * rows, k * heads.wide : (k + 1) * heads.wide] = w_ref[
                at : at + rows, heads.lead : heads.output
            ]


def head_parts(heads, h, lanes, q_ref, kv_ref, kr_ref):
    mine = (lanes % 128 >= h * heads.half) & (lanes % 128 < (h + 1) * heads.half)
    rotary = q_ref[:, heads.flat : heads.query]
    rotary = jnp.where(mine, rotary, jnp.zeros_like(rotary))
    query = jnp.concatenate([q_ref[:, h * NOPE : (h + 1) * NOPE], rotary], axis=1)
    at = h * (NOPE + VD)
    key = jnp.concatenate([kv_ref[:, at : at + NOPE], kr_ref[...]], axis=1)
    return (mine, query, key, kv_ref[:, at + NOPE : at + NOPE + VD])


def allowed(seg_col_ref, seg_row_ref):
    count = seg_col_ref.shape[0]
    rows = lax.broadcasted_iota(jnp.int32, (count, count), 0)
    cols = lax.broadcasted_iota(jnp.int32, (count, count), 1)
    return (seg_col_ref[...] == seg_row_ref[...]) & (cols <= rows)


def attend_kernel(heads, lanes_n, chunks, extra, lane_ref, in_gain_ref, w_ref, cos_ref, sin_ref, seg_col_ref, seg_row_ref, gain_ref, *refs):
    pieces = refs[:lanes_n]
    refs = refs[lanes_n + extra :]
    x_ref, x_low_ref, factor_ref, q_ref, kv_ref, kr_ref, lat_ref, low_t_ref, lse_ref, heads_ref = refs[:10]
    attn_refs, expand_ref = (refs[10:-1], refs[-1])
    f32, bf16 = (jnp.float32, jnp.bfloat16)
    count = x_ref.shape[0]
    block = count // lanes_n
    for hop, piece in enumerate(pieces):
        source = lax.rem(lane_ref[0] + lanes_n - hop, lanes_n)
        rows = pl.ds(pl.multiple_of(source * block, block), block)
        value = piece[...]
        x_ref[rows, :] = value
        value = value.astype(f32)
        scale = lax.rsqrt(jnp.mean(value * value, axis=-1, keepdims=True) + EPS)
        factor_ref[rows, :] = jnp.broadcast_to(scale, (block, 128))
        x_low_ref[rows, :] = (value * scale * in_gain_ref[...]).astype(bf16)
    x = x_low_ref[...]
    cosine, sine = (cos_ref[...], sin_ref[...])
    query = dot32(x, w_ref[:, : heads.query])
    first = query[:, heads.flat : heads.flat + 128]
    second = query[:, heads.flat + 128 :]
    q_ref[:, : heads.flat] = query[:, : heads.flat].astype(bf16)
    q_ref[:, heads.flat : heads.flat + 128] = (first * cosine - second * sine).astype(bf16)
    q_ref[:, heads.flat + 128 :] = (second * cosine + first * sine).astype(bf16)
    latent = dot32(x, w_ref[:, heads.query : heads.lead])
    ends = latent[:, LAT:]
    latent = latent[:, :LAT]
    lat_ref[...] = latent
    factor = lax.rsqrt(jnp.mean(latent * latent, axis=-1, keepdims=True) + EPS)
    low = latent * factor * gain_ref[...]
    low_t_ref[...] = low.T.astype(bf16)
    low = low.astype(bf16)
    lanes = lax.broadcasted_iota(jnp.int32, (count, 128), 1)
    half = heads.half

    def repeated(value):
        value = value + pltpu.roll(value, half, 1)
        return value + pltpu.roll(value, 2 * half, 1)

    first = repeated(jnp.where(lanes < half, ends, 0.0))
    second = repeated(jnp.where((lanes >= half) & (lanes < 2 * half), ends, 0.0))
    kr_ref[:, :128] = (first * cosine - second * sine).astype(bf16)
    kr_ref[:, 128:] = (second * cosine + first * sine).astype(bf16)
    expand_rows(heads, w_ref, expand_ref)
    kv_ref[...] = dot32(low, expand_ref[...]).astype(bf16)
    keep = allowed(seg_col_ref, seg_row_ref)
    wide_lanes = lax.broadcasted_iota(jnp.int32, (count, 256), 1)
    lse = jnp.zeros((count, 128), f32)
    for h in range(heads.width):
        _, query, key, value = head_parts(heads, h, wide_lanes, q_ref, kv_ref, kr_ref)
        scores = jnp.where(keep, dot_nt(query, key) * heads.scale, NEG_FILL)
        peak = jnp.max(scores, axis=-1, keepdims=True)
        expo = jnp.exp(scores - peak)
        total = jnp.sum(expo, axis=-1, keepdims=True)
        lse = jnp.where(lanes == h, peak + jnp.log(total), lse)
        probs = (expo * (1.0 / total)).astype(bf16)
        heads_ref[:, h * VD : (h + 1) * VD] = dot32(probs, value).astype(bf16)
    lse_ref[...] = lse
    out = heads_ref[...]
    step = 512
    rows, model = attn_refs[0].shape
    part = rows // lanes_n
    for at in range(0, model, step):
        cut = slice(at, at + step)
        piece = dot_nt(out, w_ref[cut, heads.output :]).astype(bf16)
        for c in range(chunks):
            for j in range(lanes_n):
                start = (j * chunks + c) * part
                attn_refs[c][j * part : (j + 1) * part, cut] = piece[start : start + part]


def attend(heads, chunks, lane, in_gain, packed, cosine, sine, seg_col, seg_row, gain, pieces, *others):
    lanes = len(pieces)
    count, model = (seg_col.shape[0], packed.shape[0])
    kv_c, heads_c = (heads.width * (NOPE + VD), heads.width * VD)
    f32, bf16 = (jnp.float32, jnp.bfloat16)
    shapes = [
        ((count, model), bf16),
        ((count, model), bf16),
        ((count, 128), f32),
        ((count, heads.query), bf16),
        ((count, kv_c), bf16),
        ((count, 256), bf16),
        ((count, LAT), f32),
        ((LAT, count), bf16),
        ((count, 128), f32),
        ((count, heads_c), bf16),
    ] + [((count // chunks, model), bf16)] * chunks
    vmem = pl.BlockSpec(memory_space=pltpu.VMEM)
    return pl.pallas_call(
        functools.partial(attend_kernel, heads, lanes, chunks, len(others)),
        in_specs=[pl.BlockSpec(memory_space=pltpu.SMEM)]
        + [vmem] * (7 + lanes)
        + [pl.BlockSpec(memory_space=pl.ANY) for _ in others],
        out_specs=[vmem] * len(shapes),
        out_shape=[jax.ShapeDtypeStruct(*s) for s in shapes],
        scratch_shapes=[pltpu.VMEM((LAT, kv_c), bf16)],
        compiler_params=pltpu.CompilerParams(vmem_limit_bytes=58 * MIB),
        cost_estimate=pl.CostEstimate(
            flops=2 * count * (model * heads.cols + LAT * kv_c + heads.width * count * 512),
            bytes_accessed=2 * (model * heads.cols + 4 * count * model),
            transcendentals=heads.width * count * count,
        ),
        name="attend",
    )(lane, in_gain, packed, cosine, sine, seg_col, seg_row, gain, *pieces, *others)


def attend_back_kernel(
    heads,
    extra,
    dattn_ref,
    x_ref,
    factor_ref,
    w_ref,
    cos_ref,
    sin_ref,
    seg_col_ref,
    seg_row_ref,
    gain_ref,
    q_ref,
    kv_ref,
    kr_ref,
    lat_ref,
    lse_ref,
    *refs,
):
    spread_ref = refs[0]
    qr_ref, kvg_ref, normed_ref, gains_ref, expand_ref = refs[1 + extra :]
    f32, bf16 = (jnp.float32, jnp.bfloat16)
    count, model = x_ref.shape
    half = heads.half
    cosine, sine = (cos_ref[...], sin_ref[...])
    expand_rows(heads, w_ref, expand_ref)
    dheads = dot32(dattn_ref[...], w_ref[:, heads.output :]).astype(bf16)
    keep = allowed(seg_col_ref, seg_row_ref)
    lanes = lax.broadcasted_iota(jnp.int32, (count, 128), 1)
    wide_lanes = lax.broadcasted_iota(jnp.int32, (count, 256), 1)
    lse = lse_ref[...]
    dq_rot = jnp.zeros((count, 256), f32)
    dk_rot = jnp.zeros((count, 256), f32)
    for h in range(heads.width):
        mine, query, key, value = head_parts(heads, h, wide_lanes, q_ref, kv_ref, kr_ref)
        scores = jnp.where(keep, dot_nt(query, key) * heads.scale, NEG_FILL)
        probs = jnp.exp(scores - lse[:, h : h + 1])
        dhead = dheads[:, h * VD : (h + 1) * VD]
        dprobs = dot_nt(dhead, value)
        delta = jnp.sum(probs * dprobs, axis=-1, keepdims=True)
        dscores = (probs * (dprobs - delta)).astype(bf16)
        dquery = dot32(dscores, key) * heads.scale
        dkey = dot_tn(dscores, query) * heads.scale
        qr_ref[:, h * NOPE : (h + 1) * NOPE] = dquery[:, :NOPE].astype(bf16)
        dq_rot = dq_rot + jnp.where(mine, dquery[:, NOPE:], 0.0)
        dk_rot = dk_rot + dkey[:, NOPE:]
        at = h * (NOPE + VD)
        kvg_ref[:, at : at + NOPE] = dkey[:, :NOPE].astype(bf16)
        kvg_ref[:, at + NOPE : at + NOPE + VD] = dot_tn(probs.astype(bf16), dhead).astype(bf16)
    first, second = (dq_rot[:, :128], dq_rot[:, 128:])
    qr_ref[:, heads.flat : heads.flat + 128] = (first * cosine + second * sine).astype(bf16)
    qr_ref[:, heads.flat + 128 : heads.query] = (second * cosine - first * sine).astype(bf16)

    def folded(part):
        part = part + pltpu.roll(part, half, 1)
        return part + pltpu.roll(part, 2 * half, 1)

    first, second = (folded(dk_rot[:, :128]), folded(dk_rot[:, 128:]))
    ends = jnp.where(
        lanes < half,
        first * cosine + second * sine,
        jnp.where(lanes < 2 * half, second * cosine - first * sine, 0.0),
    )
    qr_ref[:, heads.query + LAT : heads.lead] = ends.astype(bf16)
    dlow = dot_nt(kvg_ref[...], expand_ref[...])
    latent = lat_ref[...]
    factor = lax.rsqrt(jnp.mean(latent * latent, axis=-1, keepdims=True) + EPS)
    unit = latent * factor
    lat_gain = jnp.broadcast_to(jnp.sum(dlow * unit, axis=0, keepdims=True), (8, LAT))
    parts = []
    for _ in range(3):
        parts.append(lat_gain.astype(bf16).astype(f32))
        lat_gain = lat_gain - parts[-1]
    spread = dot32(jnp.concatenate(parts).astype(bf16), spread_ref[...])
    gains_ref[...] = spread[:8] + spread[8:16] + spread[16:]
    dlatent = norm_back(dlow, unit, factor, gain_ref[...])
    qr_ref[:, heads.query : heads.query + LAT] = dlatent.astype(bf16)
    qr = qr_ref[...]
    step = 512
    for at in range(0, model, step):
        part = dot_nt(qr, w_ref[at : at + step, : heads.lead])
        normed_ref[:, at : at + step] = part.astype(bf16)
        unit_in = x_ref[:, at : at + step].astype(f32) * factor_ref[:, :1]
        gains_ref[:1, at : at + step] = jnp.sum(part * unit_in, axis=0, keepdims=True)


def attend_back(heads, *operands, others=()):
    count, model = operands[1].shape
    kv_c = heads.width * (NOPE + VD)
    f32, bf16 = (jnp.float32, jnp.bfloat16)
    shapes = [
        ((count, heads.lead), bf16),
        ((count, kv_c), bf16),
        ((count, model), bf16),
        ((8, model), f32),
    ]
    vmem = pl.BlockSpec(memory_space=pltpu.VMEM)
    return pl.pallas_call(
        functools.partial(attend_back_kernel, heads, len(others)),
        in_specs=[vmem] * len(operands) + [pl.BlockSpec(memory_space=pl.ANY) for _ in others],
        out_specs=[vmem] * len(shapes),
        out_shape=[jax.ShapeDtypeStruct(*s) for s in shapes],
        scratch_shapes=[pltpu.VMEM((LAT, kv_c), bf16)],
        compiler_params=pltpu.CompilerParams(vmem_limit_bytes=60 * MIB),
        cost_estimate=pl.CostEstimate(
            flops=2 * count * (model * heads.cols + LAT * kv_c + heads.width * count * 1600),
            bytes_accessed=2 * (model * heads.cols + 4 * count * model),
            transcendentals=heads.width * count * count,
        ),
        name="attend_back",
    )(*operands, *others)


def per_device(
    tokens_in,
    cotangent,
    routes,
    segments,
    norm_in,
    w_query,
    w_latent,
    latent_gain,
    w_expand,
    w_output,
    norm_mid,
    w_router,
    shared_gate,
    shared_up,
    shared_down,
    expert_gate,
    routed_up_weight,
    expert_down,
):
    f32, bf16 = (jnp.float32, jnp.bfloat16)
    groups, lanes = (lax.axis_size("fsdp"), lax.axis_size("ctx"))
    halves = [list(range(k, groups, 2)) for k in (0, 1)]
    half = groups // 2

    def swap(value):
        return lax.ppermute(value, "fsdp", [(i, i ^ 1) for i in range(groups)])

    def gather_half(value):
        return lax.all_gather(value, "fsdp", axis=0, tiled=True, axis_index_groups=halves)

    def scatter_half(value):
        return lax.psum_scatter(
            value, "fsdp", scatter_dimension=0, tiled=True, axis_index_groups=halves
        )

    group = lax.axis_index("fsdp")
    tok_dev, model_w = tokens_in.shape
    count = tok_dev * lanes
    depth = w_query.shape[0]
    query_c, expand_c, heads_c = (w_query.shape[1], w_expand.shape[1], w_output.shape[0])
    exp_dev, hidden, _ = expert_gate.shape
    experts_n, top_k = (w_router.shape[1], routes.shape[1])
    sh_units = shared_gate.shape[1] // groups
    plan = Plan(exp_dev, hidden, sh_units, experts_n, top_k)
    units = plan.units
    chunks = max(2, groups * count // 2048)
    width = query_c // (NOPE + ROPE)

    small_c = -(-(LAT + ROPE + experts_n + 3) // 128) * 128
    assert small_c - 128 <= LAT + ROPE
    at_router = LAT + ROPE
    at_seg = at_router + experts_n
    seg_cols = segments.astype(bf16).reshape(w_latent.shape[0], -1)
    spare = small_c - at_seg - seg_cols.shape[1]
    small = jnp.concatenate(
        [w_latent, w_router, seg_cols, jnp.zeros((w_latent.shape[0], spare), bf16)], axis=1
    )
    small = gather_ctx(small)
    seg_all = small[:, at_seg : at_seg + seg_cols.shape[1]].astype(jnp.int32).reshape(count)
    folds = depth // w_expand.shape[0]
    wide = expand_c // folds
    expand_blocks = [w_expand[:, k * wide : (k + 1) * wide] for k in range(folds)]
    heads = Heads(width, groups, depth, small_c, wide, heads_c)
    order = heads.order()
    packed = jnp.concatenate(
        [dot32(w_query, order).astype(bf16), small, jnp.concatenate(expand_blocks, axis=0), w_output.T], axis=1
    )
    packed = lax.all_gather(packed, "fsdp", axis=0, tiled=True)
    at_expand = heads.lead
    at_output = heads.output
    at_first = heads.query + at_router
    router_w = packed[:, at_first : at_first + experts_n]

    meta = jnp.concatenate(
        [routes.astype(bf16), jnp.zeros((tok_dev, 128 - top_k), bf16)], axis=1
    )
    dout_own = after(jnp.concatenate([cotangent, meta], axis=1), small)
    dout_group = gather_ctx(dout_own)
    dout_all = gather_half(dout_group)
    dout_all = dout_all.reshape(half * lanes, chunks, tok_dev // chunks, model_w + 128)

    x_pieces = spread_ctx(after(tokens_in, dout_group))

    steps = jnp.arange(count, dtype=jnp.int32)
    same = seg_all[:, None] == seg_all[None, :]
    start = jnp.min(jnp.where(same, steps[None, :], count), axis=1)
    place = (steps - start).astype(f32)
    freq = THETA ** (-(jnp.arange(ROPE // 2, dtype=f32) * 2.0 / ROPE))
    angle = place[:, None] * freq[None, :]
    cosine, sine = (jnp.concatenate([f(angle)] * 4, axis=1) for f in (jnp.cos, jnp.sin))
    fixed = (cosine, sine, seg_all[:, None], seg_all[None, :], latent_gain[None, :])
    lane = lax.axis_index("ctx").astype(jnp.int32)[None]
    early_pair = [swap(w.reshape(units, model_w)) for w in (expert_gate, routed_up_weight)]
    x_all, x_low, factor_in, q_low, kv_low, kr_low, latent_raw, latent_low_t, lse, heads_low, *attn = (
        attend(heads, chunks, lane, norm_in[None, :], packed, *fixed, x_pieces, *early_pair)
    )
    def pair_weights(*others):
        shared = jnp.stack([shared_gate.T, shared_up.T, shared_down]).reshape(
            3, groups, sh_units, depth
        )
        shared, late_down = after((shared, expert_down), *others)
        shared = lax.all_to_all(shared, "fsdp", split_axis=1, concat_axis=1, tiled=True)
        shared = shared.transpose(0, 2, 1, 3).reshape(3, sh_units, model_w)

        if plan.shared > sh_units:
            shared = jnp.pad(shared, ((0, 0), (0, plan.shared - sh_units), (0, 0)))
        shared_pair = swap(shared)

        pack = [w.reshape(units, model_w) for w in (expert_gate, routed_up_weight, late_down)]
        pair = [*early_pair, swap(pack[2])]

        def rest(k, router):
            gap = jnp.zeros((plan.router - 2 * (units + plan.shared), model_w), bf16)
            end = jnp.zeros((plan.cols - plan.router - router.shape[0], model_w), bf16)
            return jnp.concatenate([shared[k], shared_pair[k], gap, router, end])

        none = jnp.zeros((0, model_w), bf16)
        rests = (rest(0, router_w.T), rest(1, none), rest(2, none))
        return [part for k in range(3) for part in (pack[k], pair[k], rests[k])]

    pieces = pair_weights(lse)

    own_experts = group * exp_dev + jnp.arange(exp_dev, dtype=jnp.int32)
    pair_experts = (group ^ 1) * exp_dev + jnp.arange(exp_dev, dtype=jnp.int32)
    first = jnp.concatenate([own_experts, pair_experts])
    part = tok_dev // chunks
    mids, rows_parts, held = ([], [], ())
    resid, unit_mid, factor_mid, mid_low = ([], [], [], [])
    last, sent = (dout_all, ())
    for h in range(chunks):
        rows = tokens_in[h * part : (h + 1) * part].astype(f32)
        attn_part = after(attn[h], *sent)
        resid.append(rows + scatter_ctx(attn_part))
        mid, unit, factor = norm_parts(resid[h], norm_mid)
        unit_mid.append(unit)
        factor_mid.append(factor)
        mid_low.append(mid.astype(bf16))
        mid_part = gather_ctx(mid_low[h])
        mid_part = after(mid_part, *pieces)
        sent = (mid_part,)
        last = gather_half(after(mid_part, last))
        mids.append(last)
    for h in range(chunks):
        rows_part, *held = experts_back(plan, h, first, mids[h], dout_all, pieces, *held)
        rows_part = after(rows_part, last)
        last = scatter_half(rows_part)
        rows_parts.append(last)
    gud, act = held

    router_f = router_w.astype(f32)

    def middle_back(h, pieces, *others):
        own = total_of([after(pieces[0], *others)] + pieces[1:])
        rows = slice(h * part, (h + 1) * part)
        mid_grad = own[:, :model_w]
        gates_grad = (
            own[:, model_w : model_w + experts_n]
            + own[:, model_w + experts_n : model_w + 2 * experts_n]
        )
        sig = jax.nn.sigmoid(dot32(mid_low[h], router_w))
        hit = routes[rows, :, None] == jnp.arange(experts_n, dtype=jnp.int32)[None, None, :]
        member = jnp.any(hit, axis=1).astype(f32)
        chosen_sum = jnp.sum(sig * member, axis=-1, keepdims=True)
        gates = ROUTE_SCALE * sig * member / chosen_sum
        spread = jnp.sum(gates_grad * gates, axis=-1, keepdims=True)
        chosen_grad = (ROUTE_SCALE * gates_grad - spread) / chosen_sum
        logit_grad = chosen_grad * member * sig * (1.0 - sig)
        mid_grad = mid_grad + precise_nt(logit_grad, router_f)
        grad = norm_back(mid_grad, unit_mid[h], factor_mid[h], norm_mid)
        grad = grad + cotangent[rows].astype(f32)
        return (
            grad,
            grad.astype(bf16),
            jnp.sum(mid_grad * unit_mid[h], axis=0, keepdims=True),
            precise_tn(logit_grad, mid_low[h].astype(f32)),
        )

    def outputs(*others):
        return [
            experts_out(plan, half, lanes, h, 2, act, pieces[6:], *others) for h in range(0, chunks, 2)
        ]

    if chunks == 2:
        back = [middle_back(0, pieces_ctx(rows_parts[0]))]
        gate_sums = weight_sum(plan, "gate", model_w, gud, mids)
        attn_low = [gather_ctx(back[0][1])]
        out_parts = outputs(back[0][1], gate_sums[3])
        out_parts = [after(out_parts[0], attn_low[0])]
        back.append(middle_back(1, pieces_ctx(after(rows_parts[1], *out_parts))))
        down_sums = weight_sum(plan, "down", model_w, act, dout_all, rows_parts[1])
        attn_low.append(gather_ctx(back[1][1]))
        up_sums = weight_sum(plan, "up", model_w, gud, mids, back[1][1])
        early_swaps = [swap(gate_sums[2]), swap(down_sums[2])]
    else:
        gate_sums = weight_sum(plan, "gate", model_w, gud, mids)
        down_sums = weight_sum(plan, "down", model_w, act, dout_all)
        up_sums = weight_sum(plan, "up", model_w, gud, mids)
        out_parts = outputs(down_sums[3], gate_sums[3], up_sums[3])
        back = [middle_back(h, pieces_ctx(rows_parts[h])) for h in range(chunks)]
        attn_low = [gather_ctx(grad[1]) for grad in back]
        early_swaps = [swap(gate_sums[2]), swap(down_sums[2])]
    attn_low = jnp.stack([a.reshape(lanes, part, model_w) for a in attn_low], axis=1)
    attn_low = attn_low.reshape(count, model_w)
    resid_grad = jnp.concatenate([grad[0] for grad in back])
    mid_gain_grad = sum(grad[2] for grad in back)
    router_grad = sum(grad[3] for grad in back)

    out_sums = []
    for out_part in out_parts:
        last = scatter_half(after(out_part, last))
        out_sums.append(last)

    share = LAT // (groups * lanes)
    column = np.arange(model_w)[None, :]
    spot = column * lanes * groups // model_w * share + column % (depth // lanes)
    inside = column % (depth // lanes) < share
    spread = jnp.asarray(((np.arange(LAT)[:, None] == spot) & inside).astype(np.float32), bf16)
    qr_grad, kv_grad, normed_grad, gains = attend_back(
        heads,
        attn_low,
        x_all,
        factor_in,
        packed,
        *fixed,
        q_low,
        kv_low,
        kr_low,
        latent_raw,
        lse,
        spread,
        others=early_swaps + [up_sums[3]],
    )
    if chunks == 2:
        end_pieces = pieces_ctx(jnp.concatenate([out_sums[0], normed_grad], axis=1))
    else:
        moe = jnp.concatenate([scatter_ctx(rows) for rows in out_sums])
        end_pieces = pieces_ctx(normed_grad)
        normed_own = total_of(end_pieces)
        block_out = (jnp.concatenate(resid) + moe).astype(bf16)
    before = LAT + ROPE - (small_c - 128)
    early = jnp.concatenate([router_grad, mid_gain_grad])
    grads = packed_grads(
        groups,
        before,
        x_low,
        attn_low,
        latent_low_t,
        qr_grad,
        heads_low,
        kv_grad,
        early,
        gains,
    )
    all_sums = (gate_sums, up_sums, down_sums)
    swapped = (early_swaps[0], swap(up_sums[2]), early_swaps[1])
    expert_grads = [
        finished(sums[0], other, end_pieces[1]).reshape(expert_gate.shape)
        for sums, other in zip(all_sums, swapped)
    ]
    shared_other = swap(after(jnp.stack([sums[3] for sums in all_sums]), end_pieces[1]))
    shared_grad = jnp.stack([sums[1] for sums in all_sums]) + shared_other.astype(f32)
    shared_grad = shared_grad[:, :sh_units].astype(bf16)
    shared_grad = shared_grad.reshape(3, sh_units, groups, depth).transpose(0, 2, 1, 3)
    shared_grad = lax.all_to_all(shared_grad, "fsdp", split_axis=1, concat_axis=1, tiled=True)
    shared_grad = shared_grad.reshape(3, sh_units * groups, depth).astype(f32)
    if chunks == 2:
        block_out, grad_input = ends(
            end_pieces,
            jnp.concatenate(resid),
            resid_grad,
            tokens_in,
            norm_in[None, :],
            *expert_grads,
        )
    else:
        _, unit_own, factor_own = norm_parts(tokens_in.astype(f32), norm_in)
        grad_input = norm_back(normed_own, unit_own, factor_own, norm_in) + resid_grad
    grads = lax.psum_scatter(after(grads, last), "fsdp", scatter_dimension=0, tiled=True)
    small_own = scatter_ctx(grads[:, heads.query : at_expand])
    g_query = dot_nt(grads[:, : heads.query], order)
    g_expand = grads[:, at_expand:at_output].astype(f32)
    g_expand = jnp.concatenate(
        [g_expand[k * w_expand.shape[0] : (k + 1) * w_expand.shape[0]] for k in range(folds)],
        axis=1,
    )
    g_output = grads[:, at_output:].astype(f32).T
    at_gain = at_router + experts_n
    return (
        block_out,
        grad_input.astype(bf16),
        small_own[:, at_gain + 1],
        g_query,
        small_own[:, :at_router],
        small_own[: LAT // (groups * lanes), at_gain + 2],
        g_expand,
        g_output,
        small_own[:, at_gain],
        small_own[:, at_router:at_gain],
        shared_grad[0].T,
        shared_grad[1].T,
        shared_grad[2],
        *expert_grads,
    )


def solution(mesh):
    in_specs = (
        P(("fsdp", "ctx"), None),
        P(("fsdp", "ctx"), None),
        P(("fsdp", "ctx"), None),
        P(("fsdp", "ctx")),
        P(),
        P("fsdp", "ctx"),
        P(("fsdp", "ctx"), None),
        P(),
        P("fsdp", "ctx"),
        P("ctx", "fsdp"),
        P(),
        P(("fsdp", "ctx"), None),
        P("fsdp", "ctx"),
        P("fsdp", "ctx"),
        P("ctx", "fsdp"),
        P("fsdp", "ctx", None),
        P("fsdp", "ctx", None),
        P("fsdp", "ctx", None),
    )
    out_specs = (
        P(("fsdp", "ctx"), None),
        P(("fsdp", "ctx"), None),
        P(("fsdp", "ctx")),
        P("fsdp", "ctx"),
        P(("fsdp", "ctx"), None),
        P(("fsdp", "ctx")),
        P("fsdp", "ctx"),
        P("ctx", "fsdp"),
        P(("fsdp", "ctx")),
        P(("fsdp", "ctx"), None),
        P("fsdp", "ctx"),
        P("fsdp", "ctx"),
        P("ctx", "fsdp"),
        P("fsdp", "ctx", None),
        P("fsdp", "ctx", None),
        P("fsdp", "ctx", None),
    )
    return jax.shard_map(
        per_device, mesh=mesh, in_specs=in_specs, out_specs=out_specs, check_vma=False
    )
```

```python
import functools

import jax
import jax.numpy as jnp
import numpy as np
from jax import lax
from jax.experimental import pallas as pl
from jax.experimental.pallas import tpu as pltpu
from jax.sharding import PartitionSpec as P

NOPE = 128
ROPE = 64
VD = 128
LAT = 512


EPS = 1e-06
THETA = 50000.0
ROUTE_SCALE = 2.446
MIB = 1024 * 1024
NEG_FILL = -1e30


def dot32(left, right):
    return jnp.dot(left, right, preferred_element_type=jnp.float32)


def dot_nt(left, right):
    return lax.dot_general(
        left, right, (((1,), (1,)), ((), ())), preferred_element_type=jnp.float32
    )


def dot_tn(left, right):
    return lax.dot_general(
        left, right, (((0,), (0,)), ((), ())), preferred_element_type=jnp.float32
    )


def precise_nt(left, right):
    return lax.dot_general(
        left,
        right,
        (((1,), (1,)), ((), ())),
        precision=lax.Precision.HIGHEST,
        preferred_element_type=jnp.float32,
    )


def precise_tn(left, right):
    return lax.dot_general(
        left,
        right,
        (((0,), (0,)), ((), ())),
        precision=lax.Precision.HIGHEST,
        preferred_element_type=jnp.float32,
    )


def norm_parts(value, gain):
    factor = lax.rsqrt(jnp.mean(value * value, axis=-1, keepdims=True) + EPS)
    unit = value * factor
    return (unit * gain, unit, factor)


def norm_back(grad_out, unit, factor, gain):
    grad_unit = grad_out * gain
    return factor * (grad_unit - unit * jnp.mean(grad_unit * unit, axis=-1, keepdims=True))


def turn(value, cosine, sine):
    half = value.shape[-1] // 2
    first, second = (value[..., :half], value[..., half:])
    return jnp.concatenate(
        [first * cosine - second * sine, second * cosine + first * sine], axis=-1
    )


def turn_back(grad, cosine, sine):
    half = grad.shape[-1] // 2
    first, second = (grad[..., :half], grad[..., half:])
    return jnp.concatenate(
        [first * cosine + second * sine, second * cosine - first * sine], axis=-1
    )


def silu_slope(value):
    sig = jax.nn.sigmoid(value)
    return (sig * (1.0 + value * (1.0 - sig)), value * sig)


def after(value, *others):
    return lax.optimization_barrier((value,) + others)[0]


def gather_ctx(value):
    lanes, lane = (lax.axis_size("ctx"), lax.axis_index("ctx"))
    rows = value.shape[0]
    whole = jnp.zeros((lanes * rows,) + value.shape[1:], value.dtype)
    whole = lax.dynamic_update_slice_in_dim(whole, value, lane * rows, 0)
    for hop in range(1, lanes):
        got = lax.ppermute(value, "ctx", [(i, (i + hop) % lanes) for i in range(lanes)])
        source = lax.rem(lane + lanes - hop, lanes)
        whole = lax.dynamic_update_slice_in_dim(whole, got, source * rows, 0)
    return whole


def pieces_ctx(value):
    lanes, lane = (lax.axis_size("ctx"), lax.axis_index("ctx"))
    rows = value.shape[0] // lanes
    got = [lax.dynamic_slice_in_dim(value, lane * rows, rows, 0)]
    for hop in range(1, lanes):
        target = lax.rem(lane + hop, lanes)
        part = lax.dynamic_slice_in_dim(value, target * rows, rows, 0)
        got.append(lax.ppermute(part, "ctx", [(i, (i + hop) % lanes) for i in range(lanes)]))
    return got


def total_of(pieces):
    total = pieces[0].astype(jnp.float32)
    for piece in pieces[1:]:
        total = total + piece.astype(jnp.float32)
    return total


def scatter_ctx(value):
    return total_of(pieces_ctx(value))


def spread_ctx(value):
    lanes = lax.axis_size("ctx")
    return [value] + [
        lax.ppermute(value, "ctx", [(i, (i + hop) % lanes) for i in range(lanes)])
        for hop in range(1, lanes)
    ]


class Plan:
    def __init__(self, exp_dev, hidden, shared, experts, top):
        self.exp_dev, self.hidden, self.experts, self.top = (2 * exp_dev, hidden, experts, top)
        self.units = exp_dev * hidden
        self.shared = -(-shared // 8) * 8
        at = 2 * (self.units + self.shared)
        if at // 128 != (at + experts - 1) // 128:
            at = -(-at // 128) * 128
        self.router = at
        self.cols = -(-(at + experts) // 128) * 128
        self.even = (self.cols - 1) // 256 * 256
        self.tail = self.cols - self.even
        self.block = at // 128 * 128
        assert self.block >= self.even and self.block + 128 >= at + experts

    def places(self, model):
        both, end = (2 * self.units, self.cols)
        up_at = self.even + 2 * self.tail
        head = self.even - both
        gate = [(0, self.units, 0), (0, self.units, self.units), (0, end - both, both)]
        up = [(0, self.units, up_at), (0, self.units, up_at + self.units)]
        up.append((head, self.tail, self.cols))
        if head:
            up.append((0, head, up_at + both))
        return (gate, up, gate)


def weight_copies(plan, pieces, w1_ref, wd_ref, sems):
    copies = ([], [], [])
    turn = 0
    for k, places in enumerate(plan.places(None)):
        target = wd_ref if k == 2 else w1_ref
        if target is None:
            continue
        for n, (start, rows, at) in enumerate(places):
            source = pieces[3 * k + min(n, 2)]
            copy = pltpu.make_async_copy(
                source.at[pl.ds(start, rows)], target.at[pl.ds(at, rows)], sems.at[turn]
            )
            copies[(1, 2, 0, 0)[n]].append(copy)
            turn += 1
    return copies


def back_kernel(plan, first_ref, mid_ref, dout_ref, meta_ref, *refs):
    f32, bf16 = (jnp.float32, jnp.bfloat16)
    even, tail, hidden = (plan.even, plan.tail, plan.hidden)
    rows, model = mid_ref.shape
    rows_ref, gud_ref, act_ref, w1_ref, wd_ref, sems = refs[-6:]
    step0 = pl.program_id(0) == 0
    copies = weight_copies(plan, refs[:9], w1_ref, wd_ref, sems)

    @pl.when(step0)
    def _():
        for group in copies:
            for copy in group:
                copy.start()

    def arrived(n):
        @pl.when(step0)
        def _():
            for copy in copies[n]:
                copy.wait()

    mid = mid_ref[...]
    dout = dout_ref[...].reshape(rows, model)
    lanes = lax.broadcasted_iota(jnp.int32, (rows, 128), 1)
    off = plan.router - plan.block
    sums = [jnp.zeros((rows, 128), f32) for _ in range(plan.exp_dev)]

    def elements(own, at, gate, upper, act_grad, gate_at, up_at):
        for b in range(0, gate.shape[1], 128):
            low = at + b
            g, u, da = (gate[:, b : b + 128], upper[:, b : b + 128], act_grad[:, b : b + 128])
            sig = jax.nn.sigmoid(g)
            swish = g * sig
            act = swish * u
            weighted = act * da
            scale = None
            for e in range(plan.exp_dev):
                start, stop = (e * hidden, (e + 1) * hidden)
                if stop <= low or start >= low + 128:
                    continue
                if start <= low and stop >= low + 128:
                    scale = own[e]
                    sums[e] = sums[e] + weighted
                else:
                    mine = (low + lanes >= start) & (low + lanes < stop)
                    sums[e] = sums[e] + jnp.where(mine, weighted, 0.0)
                    rest = jnp.ones((rows, 128), f32) if scale is None else scale
                    scale = jnp.where(mine, own[e], rest)
            if scale is not None:
                act = act * scale
                da = da * scale
            act_ref[:, low : low + 128] = act.astype(bf16)
            slope = sig + swish * (1.0 - sig)
            gud_ref[:, gate_at + b : gate_at + b + 128] = (da * u * slope).astype(bf16)
            gud_ref[:, up_at + b : up_at + b + 128] = (da * swish).astype(bf16)

    arrived(0)
    if even < 2 * plan.units:
        arrived(1)
        arrived(2)
    joint = dot_nt(mid, w1_ref[even : even + 2 * tail, :])
    at_block = plan.block - even
    sig = jax.nn.sigmoid(joint[:, at_block : at_block + 128])
    named = meta_ref[...].reshape(rows, 128).astype(f32)
    expert = (lanes - off).astype(f32)
    member = jnp.zeros((rows, 128), f32)
    for k in range(plan.top):
        member = jnp.where(expert == named[:, k : k + 1], 1.0, member)
    member = jnp.where((lanes >= off) & (lanes < off + plan.experts), member, 0.0)
    chosen = sig * member
    gates = ROUTE_SCALE * chosen / jnp.sum(chosen, axis=1, keepdims=True)
    own = [
        jnp.sum(jnp.where(lanes - off == first_ref[e], gates, 0.0), axis=1, keepdims=True)
        for e in range(plan.exp_dev)
    ]
    act_grad = dot_nt(dout, wd_ref[even : even + tail, :])
    elements(own, even, joint[:, :tail], joint[:, tail:], act_grad, even, even + tail)
    for at in range(0, even, 256):
        if even >= 2 * plan.units and at == 0:
            arrived(1)
        if even >= 2 * plan.units and at <= plan.units < at + 256:
            arrived(2)
        up_at = even + 2 * tail + at
        elements(
            own,
            at,
            dot_nt(mid, w1_ref[at : at + 256, :]),
            dot_nt(mid, w1_ref[up_at : up_at + 256, :]),
            dot_nt(dout, wd_ref[at : at + 256, :]),
            at,
            up_at,
        )
    step = 512
    for at in range(0, model, step):
        rows_ref[:, at : at + step] = dot32(gud_ref[...], w1_ref[:, at : at + step]).astype(bf16)
    ends = jnp.zeros((rows, 128), f32)
    for e in range(plan.exp_dev):
        grad = jnp.sum(sums[e], axis=1, keepdims=True)
        high = grad.astype(bf16).astype(f32)
        ends = jnp.where(lanes == first_ref[e], high, ends)
        ends = jnp.where(lanes == plan.experts + first_ref[e], grad - high, ends)
    rows_ref[:, model:] = ends.astype(bf16)


def experts_back(plan, chunk, first, mid, dout, pieces, *held):
    tokens, model = mid.shape
    _, chunks, rows, _ = dout.shape
    tile = min(512, tokens)

    def row(width):
        return pl.BlockSpec((tile, width), lambda i: (i, 0))

    def slot(width):
        return pl.BlockSpec((None, tile, width), lambda i: (chunk, i, 0))

    def outer(width, at):
        return pl.BlockSpec((tile // rows, None, rows, width), lambda i: (i, chunk, 0, at))

    bf16 = jnp.bfloat16
    return pl.pallas_call(
        functools.partial(back_kernel, plan),
        grid=(tokens // tile,),
        in_specs=[
            pl.BlockSpec(memory_space=pltpu.SMEM),
            row(model),
            outer(model, 0),
            outer(128, model // 128),
        ]
        + [pl.BlockSpec(memory_space=pl.ANY) for _ in (*pieces, *held)],
        out_specs=[row(model + 128), slot(2 * plan.cols), slot(plan.cols)],
        out_shape=[
            jax.ShapeDtypeStruct((tokens, model + 128), bf16),
            jax.ShapeDtypeStruct((chunks, tokens, 2 * plan.cols), bf16),
            jax.ShapeDtypeStruct((chunks, tokens, plan.cols), bf16),
        ],
        input_output_aliases={4 + len(pieces) + n: 1 + n for n in range(len(held))},
        scratch_shapes=[
            pltpu.VMEM((2 * plan.cols, model), bf16),
            pltpu.VMEM((plan.cols, model), bf16),
            pltpu.SemaphoreType.DMA((11,)),
        ],
        compiler_params=pltpu.CompilerParams(
            dimension_semantics=("arbitrary",), vmem_limit_bytes=58 * MIB
        ),
        cost_estimate=pl.CostEstimate(
            flops=10 * tokens * plan.cols * model,
            bytes_accessed=tokens * 6 * (model + plan.cols),
            transcendentals=tokens * plan.cols,
        ),
        name="experts_back",
    )(first, mid, dout, dout, *pieces, *held)


def out_kernel(plan, act_ref, *refs):
    out_ref, wd_ref, sems = refs[-3:]
    copies = weight_copies(plan, [None] * 6 + list(refs[:3]), None, wd_ref, sems)

    @pl.when((pl.program_id(0) == 0) & (pl.program_id(1) == 0))
    def _():
        for group in copies:
            for copy in group:
                copy.start()
        for group in copies:
            for copy in group:
                copy.wait()

    act = act_ref[...]
    for at in range(0, wd_ref.shape[1], 512):
        part = dot32(act, wd_ref[:, at : at + 512]).astype(jnp.bfloat16)
        out_ref[:, :, at : at + 512] = part.reshape(out_ref.shape[0], out_ref.shape[1], 512)


def experts_out(plan, groups, lanes, start, chunks, act, down, *others):
    _, tokens, cols = act.shape
    model = down[0].shape[1]
    count = tokens // groups
    rows = count // lanes
    return pl.pallas_call(
        functools.partial(out_kernel, plan),
        grid=(chunks, groups),
        in_specs=[
            pl.BlockSpec((None, count, cols), lambda h, g: (start + h, g, 0)),
        ]
        + [pl.BlockSpec(memory_space=pl.ANY) for _ in (*down, *others)],
        out_specs=pl.BlockSpec((None, lanes, None, rows, model), lambda h, g: (g, 0, h, 0, 0)),
        out_shape=jax.ShapeDtypeStruct((groups, lanes, chunks, rows, model), jnp.bfloat16),
        scratch_shapes=[
            pltpu.VMEM((plan.cols, model), jnp.bfloat16),
            pltpu.SemaphoreType.DMA((3,)),
        ],
        compiler_params=pltpu.CompilerParams(
            dimension_semantics=("arbitrary", "arbitrary"), vmem_limit_bytes=60 * MIB
        ),
        cost_estimate=pl.CostEstimate(
            flops=2 * chunks * tokens * cols * model,
            bytes_accessed=2 * chunks * tokens * (cols + model),
            transcendentals=0,
        ),
        name="experts_out",
    )(act, *down, *others).reshape(groups * lanes * chunks * rows, model)


def sum_kernel(plan, kind, chunks, h_ref, *refs):
    z_refs = refs[:chunks]
    out_ref, shared_ref, other_ref, other_shared_ref, total_ref = refs[-5:]
    chunk = pl.program_id(0)

    @pl.when((chunk == 0) & (pl.program_id(1) == 0))
    def _():
        out_ref[...] = jnp.zeros_like(out_ref)
        shared_ref[...] = jnp.zeros_like(shared_ref)
        total_ref[...] = jnp.zeros_like(total_ref)

    even, tail, units, shared = (plan.even, plan.tail, plan.units, plan.shared)
    model = out_ref.shape[1]
    step = 512

    def add(z_ref):
        h = h_ref[...]
        for at in range(0, model, step):
            cut = slice(at, at + step)
            if len(z_ref.shape) == 2:
                z = z_ref[:, cut]
            else:
                z = z_ref[:, :, cut].reshape(h.shape[0], step)
            part = dot_tn(h, z)
            if kind == "up":
                part = jnp.concatenate([part[tail:], part[:tail]])
            out_ref[:, cut] += part[:units]
            total_ref[:units, cut] += part[units : 2 * units]
            shared_ref[:, cut] += part[2 * units : 2 * units + shared]
            total_ref[units:, cut] += part[2 * units + shared : 2 * (units + shared)]

    for h, z_ref in enumerate(z_refs):
        pl.when(chunk == h)(functools.partial(add, z_ref))

    @pl.when((chunk == chunks - 1) & (pl.program_id(1) == pl.num_programs(1) - 1))
    def _():
        other_ref[...] = total_ref[:units].astype(jnp.bfloat16)
        other_shared_ref[...] = total_ref[units:].astype(jnp.bfloat16)


def weight_sum(plan, kind, model, hidden, rows, *others):
    chunks, tokens, width = hidden.shape
    cols = plan.cols
    tile = min(512, tokens) if chunks <= 2 else 256
    steps = tokens // tile
    shapes = [(plan.units, model), (plan.shared, model)] * 2
    types = [jnp.float32] * 2 + [jnp.bfloat16] * 2
    half = 1 if kind == "up" else 0

    def turn_of(h, c, i):
        return jnp.where(c == h, i, jnp.where(c < h, 0, steps - 1))

    if isinstance(rows, list):
        specs = [
            pl.BlockSpec((tile, model), lambda c, i, h=h: (turn_of(h, c, i), 0))
            for h in range(chunks)
        ]
    else:
        part = rows.shape[2]
        specs = [
            pl.BlockSpec(
                (tile // part, None, part, model), lambda c, i, h=h: (turn_of(h, c, i), h, 0, 0)
            )
            for h in range(chunks)
        ]
        rows = [rows] * chunks
    return pl.pallas_call(
        functools.partial(sum_kernel, plan, kind, chunks),
        grid=(chunks, steps),
        in_specs=[pl.BlockSpec((None, tile, cols), lambda c, i: (c, i, half))]
        + specs
        + [pl.BlockSpec(memory_space=pl.ANY) for _ in others],
        out_specs=[
            pl.BlockSpec(s, lambda c, i: (0, 0), pipeline_mode=pl.Buffered(1)) for s in shapes
        ],
        out_shape=[jax.ShapeDtypeStruct(*s) for s in zip(shapes, types)],
        scratch_shapes=[pltpu.VMEM((plan.units + plan.shared, model), jnp.float32)],
        compiler_params=pltpu.CompilerParams(
            dimension_semantics=("arbitrary", "arbitrary"), vmem_limit_bytes=58 * MIB
        ),
        cost_estimate=pl.CostEstimate(
            flops=2 * chunks * tokens * cols * model,
            bytes_accessed=2 * chunks * tokens * (model + cols) + 4 * plan.units * model,
            transcendentals=0,
        ),
        name=kind + "_sum",
    )(hidden, *rows, *others)


def pack_kernel(lead, before, x_ref, heads_grad_ref, latent_ref, qr_ref, heads_ref, kv_ref, early_ref, gains_ref, *refs):
    out_ref = refs[-1]
    bf16 = jnp.bfloat16
    first = dot_tn(x_ref[...], qr_ref[...])
    out_ref[:, : lead - 128] = first[:, : lead - 128].astype(bf16)
    early, cols = early_ref.shape
    small = jnp.concatenate(
        [
            jnp.zeros((before, cols), jnp.float32),
            early_ref[...],
            gains_ref[:2],
            jnp.zeros((128 - before - early - 2, cols), jnp.float32),
        ]
    )
    out_ref[:, lead - 128 : lead] = (first[:, lead - 128 :] + small.T).astype(bf16)
    latent = dot32(latent_ref[...], kv_ref[...])
    rows = latent.shape[0]
    pieces = out_ref.shape[0] // rows
    wide = kv_ref.shape[1] // pieces
    for k in range(pieces):
        out_ref[k * rows : (k + 1) * rows, lead : lead + wide] = latent[
            :, k * wide : (k + 1) * wide
        ].astype(bf16)
    out_ref[:, lead + wide :] = dot_tn(heads_grad_ref[...], heads_ref[...]).astype(bf16)


def packed_grads(groups, before, x_low, attn_low, latent_t, qr, heads_low, kv_grad, early, gains, *others):
    count, model = x_low.shape
    depth = model // groups
    rows = latent_t.shape[0] // groups
    lead = qr.shape[1]
    wide = kv_grad.shape[1] * rows // depth
    cols = lead + wide + heads_low.shape[1]

    def whole(value):
        return pl.BlockSpec(value.shape, lambda i: (0, 0))

    return pl.pallas_call(
        functools.partial(pack_kernel, lead, before),
        grid=(groups,),
        in_specs=[
            pl.BlockSpec((count, depth), lambda i: (0, i)),
            pl.BlockSpec((count, depth), lambda i: (0, i)),
            pl.BlockSpec((rows, count), lambda i: (i, 0)),
            whole(qr),
            whole(heads_low),
            whole(kv_grad),
            pl.BlockSpec((early.shape[0], depth), lambda i: (0, i)),
            pl.BlockSpec((8, depth), lambda i: (0, i)),
        ]
        + [pl.BlockSpec(memory_space=pl.ANY) for _ in others],
        out_specs=pl.BlockSpec((depth, cols), lambda i: (i, 0)),
        out_shape=jax.ShapeDtypeStruct((model, cols), jnp.bfloat16),
        compiler_params=pltpu.CompilerParams(
            dimension_semantics=("arbitrary",), vmem_limit_bytes=60 * MIB
        ),
        cost_estimate=pl.CostEstimate(
            flops=2 * count * model * cols, bytes_accessed=16 * MIB, transcendentals=0
        ),
        name="packed_grads",
    )(x_low, attn_low, latent_t, qr, heads_low, kv_grad, early, gains, *others)


def finish_kernel(own_ref, other_ref, *refs):
    refs[-1][...] = own_ref[...] + other_ref[...].astype(jnp.float32)


def finished(own, other, *others):
    rows, cols = own.shape
    block = pl.BlockSpec((rows // 4, cols), lambda i: (i, 0))
    return pl.pallas_call(
        finish_kernel,
        grid=(4,),
        in_specs=[block, block] + [pl.BlockSpec(memory_space=pl.ANY) for _ in others],
        out_specs=block,
        out_shape=jax.ShapeDtypeStruct((rows, cols), jnp.float32),
        input_output_aliases={0: 0},
        compiler_params=pltpu.CompilerParams(
            dimension_semantics=("arbitrary",), vmem_limit_bytes=48 * MIB
        ),
        cost_estimate=pl.CostEstimate(
            flops=rows * cols, bytes_accessed=10 * rows * cols, transcendentals=0
        ),
        name="finished",
    )(own, other, *others)


def end_kernel(pieces_n, resid_ref, grad_ref, x_ref, gain_ref, *refs):
    pieces, (out_ref, dx_ref) = (refs[:pieces_n], refs[-2:])
    f32, bf16 = (jnp.float32, jnp.bfloat16)
    model = x_ref.shape[1]
    moe = pieces[0][:, :model].astype(f32)
    dnormed = pieces[0][:, model:].astype(f32)
    for piece in pieces[1:]:
        moe = moe + piece[:, :model].astype(f32)
        dnormed = dnormed + piece[:, model:].astype(f32)
    out_ref[...] = (resid_ref[...] + moe).astype(bf16)
    _, unit, factor = norm_parts(x_ref[...].astype(f32), gain_ref[...])
    dx_ref[...] = (norm_back(dnormed, unit, factor, gain_ref[...]) + grad_ref[...]).astype(bf16)


def ends(pieces, resid, resid_grad, x, gain, *others):
    shape = jax.ShapeDtypeStruct(x.shape, jnp.bfloat16)
    vmem = pl.BlockSpec(memory_space=pltpu.VMEM)
    return pl.pallas_call(
        functools.partial(end_kernel, len(pieces)),
        in_specs=[vmem] * (4 + len(pieces)) + [pl.BlockSpec(memory_space=pl.ANY) for _ in others],
        out_specs=[vmem] * 2,
        out_shape=[shape] * 2,
        compiler_params=pltpu.CompilerParams(vmem_limit_bytes=48 * MIB),
        cost_estimate=pl.CostEstimate(
            flops=20 * x.size, bytes_accessed=30 * x.size, transcendentals=0
        ),
        name="ends",
    )(resid, resid_grad, x, gain, *pieces, *others)


class Heads:
    def __init__(self, width, groups, depth, small_c, wide, heads_c):
        self.width, self.groups, self.depth = (width, groups, depth)
        self.half = ROPE // 2
        self.flat = width * NOPE
        self.query = self.flat + 256
        self.lead = self.query + small_c
        self.wide = wide
        self.output = self.lead + wide
        self.cols = self.output + heads_c
        self.scale = (NOPE + ROPE) ** (-0.5)
        assert width * self.half <= 128 and small_c == LAT + 128

    def order(self):
        at = jnp.arange(self.query)[None, :]
        rotary = at - self.flat
        head, within = (rotary % 128 // self.half, rotary % 128 % self.half)
        turned = head * (NOPE + ROPE) + NOPE + rotary // 128 * self.half + within
        plain = at // NOPE * (NOPE + ROPE) + at % NOPE
        source = jnp.where(at < self.flat, plain, jnp.where(head < self.width, turned, -1))
        return (jnp.arange(self.width * (NOPE + ROPE))[:, None] == source).astype(jnp.bfloat16)


def expand_rows(heads, w_ref, expand_ref):
    rows = LAT // heads.groups
    for f in range(heads.groups):
        for k in range(heads.depth // rows):
            at = f * heads.depth + k * rows
            expand_ref[f * rows : (f + 1) * rows, k * heads.wide : (k + 1) * heads.wide] = w_ref[
                at : at + rows, heads.lead : heads.output
            ]


def head_parts(heads, h, lanes, q_ref, kv_ref, kr_ref):
    mine = (lanes % 128 >= h * heads.half) & (lanes % 128 < (h + 1) * heads.half)
    rotary = q_ref[:, heads.flat : heads.query]
    rotary = jnp.where(mine, rotary, jnp.zeros_like(rotary))
    query = jnp.concatenate([q_ref[:, h * NOPE : (h + 1) * NOPE], rotary], axis=1)
    at = h * (NOPE + VD)
    key = jnp.concatenate([kv_ref[:, at : at + NOPE], kr_ref[...]], axis=1)
    return (mine, query, key, kv_ref[:, at + NOPE : at + NOPE + VD])


def allowed(seg_col_ref, seg_row_ref):
    count = seg_col_ref.shape[0]
    rows = lax.broadcasted_iota(jnp.int32, (count, count), 0)
    cols = lax.broadcasted_iota(jnp.int32, (count, count), 1)
    return (seg_col_ref[...] == seg_row_ref[...]) & (cols <= rows)


def attend_kernel(heads, lanes_n, chunks, extra, lane_ref, in_gain_ref, w_ref, cos_ref, sin_ref, seg_col_ref, seg_row_ref, gain_ref, *refs):
    pieces = refs[:lanes_n]
    refs = refs[lanes_n + extra :]
    x_ref, x_low_ref, factor_ref, q_ref, kv_ref, kr_ref, lat_ref, low_t_ref, lse_ref, heads_ref = refs[:10]
    attn_refs, expand_ref = (refs[10:-1], refs[-1])
    f32, bf16 = (jnp.float32, jnp.bfloat16)
    count = x_ref.shape[0]
    block = count // lanes_n
    for hop, piece in enumerate(pieces):
        source = lax.rem(lane_ref[0] + lanes_n - hop, lanes_n)
        rows = pl.ds(pl.multiple_of(source * block, block), block)
        value = piece[...]
        x_ref[rows, :] = value
        value = value.astype(f32)
        scale = lax.rsqrt(jnp.mean(value * value, axis=-1, keepdims=True) + EPS)
        factor_ref[rows, :] = jnp.broadcast_to(scale, (block, 128))
        x_low_ref[rows, :] = (value * scale * in_gain_ref[...]).astype(bf16)
    x = x_low_ref[...]
    cosine, sine = (cos_ref[...], sin_ref[...])
    query = dot32(x, w_ref[:, : heads.query])
    first = query[:, heads.flat : heads.flat + 128]
    second = query[:, heads.flat + 128 :]
    q_ref[:, : heads.flat] = query[:, : heads.flat].astype(bf16)
    q_ref[:, heads.flat : heads.flat + 128] = (first * cosine - second * sine).astype(bf16)
    q_ref[:, heads.flat + 128 :] = (second * cosine + first * sine).astype(bf16)
    latent = dot32(x, w_ref[:, heads.query : heads.lead])
    ends = latent[:, LAT:]
    latent = latent[:, :LAT]
    lat_ref[...] = latent
    factor = lax.rsqrt(jnp.mean(latent * latent, axis=-1, keepdims=True) + EPS)
    low = latent * factor * gain_ref[...]
    low_t_ref[...] = low.T.astype(bf16)
    low = low.astype(bf16)
    lanes = lax.broadcasted_iota(jnp.int32, (count, 128), 1)
    half = heads.half

    def repeated(value):
        value = value + pltpu.roll(value, half, 1)
        return value + pltpu.roll(value, 2 * half, 1)

    first = repeated(jnp.where(lanes < half, ends, 0.0))
    second = repeated(jnp.where((lanes >= half) & (lanes < 2 * half), ends, 0.0))
    kr_ref[:, :128] = (first * cosine - second * sine).astype(bf16)
    kr_ref[:, 128:] = (second * cosine + first * sine).astype(bf16)
    expand_rows(heads, w_ref, expand_ref)
    kv_ref[...] = dot32(low, expand_ref[...]).astype(bf16)
    keep = allowed(seg_col_ref, seg_row_ref)
    wide_lanes = lax.broadcasted_iota(jnp.int32, (count, 256), 1)
    lse = jnp.zeros((count, 128), f32)
    for h in range(heads.width):
        _, query, key, value = head_parts(heads, h, wide_lanes, q_ref, kv_ref, kr_ref)
        scores = jnp.where(keep, dot_nt(query, key) * heads.scale, NEG_FILL)
        peak = jnp.max(scores, axis=-1, keepdims=True)
        expo = jnp.exp(scores - peak)
        total = jnp.sum(expo, axis=-1, keepdims=True)
        lse = jnp.where(lanes == h, peak + jnp.log(total), lse)
        probs = (expo * (1.0 / total)).astype(bf16)
        heads_ref[:, h * VD : (h + 1) * VD] = dot32(probs, value).astype(bf16)
    lse_ref[...] = lse
    out = heads_ref[...]
    step = 512
    rows, model = attn_refs[0].shape
    part = rows // lanes_n
    for at in range(0, model, step):
        cut = slice(at, at + step)
        piece = dot_nt(out, w_ref[cut, heads.output :]).astype(bf16)
        for c in range(chunks):
            for j in range(lanes_n):
                start = (j * chunks + c) * part
                attn_refs[c][j * part : (j + 1) * part, cut] = piece[start : start + part]


def attend(heads, chunks, lane, in_gain, packed, cosine, sine, seg_col, seg_row, gain, pieces, *others):
    lanes = len(pieces)
    count, model = (seg_col.shape[0], packed.shape[0])
    kv_c, heads_c = (heads.width * (NOPE + VD), heads.width * VD)
    f32, bf16 = (jnp.float32, jnp.bfloat16)
    shapes = [
        ((count, model), bf16),
        ((count, model), bf16),
        ((count, 128), f32),
        ((count, heads.query), bf16),
        ((count, kv_c), bf16),
        ((count, 256), bf16),
        ((count, LAT), f32),
        ((LAT, count), bf16),
        ((count, 128), f32),
        ((count, heads_c), bf16),
    ] + [((count // chunks, model), bf16)] * chunks
    vmem = pl.BlockSpec(memory_space=pltpu.VMEM)
    return pl.pallas_call(
        functools.partial(attend_kernel, heads, lanes, chunks, len(others)),
        in_specs=[pl.BlockSpec(memory_space=pltpu.SMEM)]
        + [vmem] * (7 + lanes)
        + [pl.BlockSpec(memory_space=pl.ANY) for _ in others],
        out_specs=[vmem] * len(shapes),
        out_shape=[jax.ShapeDtypeStruct(*s) for s in shapes],
        scratch_shapes=[pltpu.VMEM((LAT, kv_c), bf16)],
        compiler_params=pltpu.CompilerParams(vmem_limit_bytes=58 * MIB),
        cost_estimate=pl.CostEstimate(
            flops=2 * count * (model * heads.cols + LAT * kv_c + heads.width * count * 512),
            bytes_accessed=2 * (model * heads.cols + 4 * count * model),
            transcendentals=heads.width * count * count,
        ),
        name="attend",
    )(lane, in_gain, packed, cosine, sine, seg_col, seg_row, gain, *pieces, *others)


def attend_back_kernel(
    heads,
    extra,
    dattn_ref,
    x_ref,
    factor_ref,
    w_ref,
    cos_ref,
    sin_ref,
    seg_col_ref,
    seg_row_ref,
    gain_ref,
    q_ref,
    kv_ref,
    kr_ref,
    lat_ref,
    lse_ref,
    *refs,
):
    spread_ref = refs[0]
    qr_ref, kvg_ref, normed_ref, gains_ref, expand_ref = refs[1 + extra :]
    f32, bf16 = (jnp.float32, jnp.bfloat16)
    count, model = x_ref.shape
    half = heads.half
    cosine, sine = (cos_ref[...], sin_ref[...])
    expand_rows(heads, w_ref, expand_ref)
    dheads = dot32(dattn_ref[...], w_ref[:, heads.output :]).astype(bf16)
    keep = allowed(seg_col_ref, seg_row_ref)
    lanes = lax.broadcasted_iota(jnp.int32, (count, 128), 1)
    wide_lanes = lax.broadcasted_iota(jnp.int32, (count, 256), 1)
    lse = lse_ref[...]
    dq_rot = jnp.zeros((count, 256), f32)
    dk_rot = jnp.zeros((count, 256), f32)
    for h in range(heads.width):
        mine, query, key, value = head_parts(heads, h, wide_lanes, q_ref, kv_ref, kr_ref)
        scores = jnp.where(keep, dot_nt(query, key) * heads.scale, NEG_FILL)
        probs = jnp.exp(scores - lse[:, h : h + 1])
        dhead = dheads[:, h * VD : (h + 1) * VD]
        dprobs = dot_nt(dhead, value)
        delta = jnp.sum(probs * dprobs, axis=-1, keepdims=True)
        dscores = (probs * (dprobs - delta)).astype(bf16)
        dquery = dot32(dscores, key) * heads.scale
        dkey = dot_tn(dscores, query) * heads.scale
        qr_ref[:, h * NOPE : (h + 1) * NOPE] = dquery[:, :NOPE].astype(bf16)
        dq_rot = dq_rot + jnp.where(mine, dquery[:, NOPE:], 0.0)
        dk_rot = dk_rot + dkey[:, NOPE:]
        at = h * (NOPE + VD)
        kvg_ref[:, at : at + NOPE] = dkey[:, :NOPE].astype(bf16)
        kvg_ref[:, at + NOPE : at + NOPE + VD] = dot_tn(probs.astype(bf16), dhead).astype(bf16)
    first, second = (dq_rot[:, :128], dq_rot[:, 128:])
    qr_ref[:, heads.flat : heads.flat + 128] = (first * cosine + second * sine).astype(bf16)
    qr_ref[:, heads.flat + 128 : heads.query] = (second * cosine - first * sine).astype(bf16)

    def folded(part):
        part = part + pltpu.roll(part, half, 1)
        return part + pltpu.roll(part, 2 * half, 1)

    first, second = (folded(dk_rot[:, :128]), folded(dk_rot[:, 128:]))
    ends = jnp.where(
        lanes < half,
        first * cosine + second * sine,
        jnp.where(lanes < 2 * half, second * cosine - first * sine, 0.0),
    )
    qr_ref[:, heads.query + LAT : heads.lead] = ends.astype(bf16)
    dlow = dot_nt(kvg_ref[...], expand_ref[...])
    latent = lat_ref[...]
    factor = lax.rsqrt(jnp.mean(latent * latent, axis=-1, keepdims=True) + EPS)
    unit = latent * factor
    lat_gain = jnp.broadcast_to(jnp.sum(dlow * unit, axis=0, keepdims=True), (8, LAT))
    parts = []
    for _ in range(3):
        parts.append(lat_gain.astype(bf16).astype(f32))
        lat_gain = lat_gain - parts[-1]
    spread = dot32(jnp.concatenate(parts).astype(bf16), spread_ref[...])
    gains_ref[...] = spread[:8] + spread[8:16] + spread[16:]
    dlatent = norm_back(dlow, unit, factor, gain_ref[...])
    qr_ref[:, heads.query : heads.query + LAT] = dlatent.astype(bf16)
    qr = qr_ref[...]
    step = 512
    for at in range(0, model, step):
        part = dot_nt(qr, w_ref[at : at + step, : heads.lead])
        normed_ref[:, at : at + step] = part.astype(bf16)
        unit_in = x_ref[:, at : at + step].astype(f32) * factor_ref[:, :1]
        gains_ref[:1, at : at + step] = jnp.sum(part * unit_in, axis=0, keepdims=True)


def attend_back(heads, *operands, others=()):
    count, model = operands[1].shape
    kv_c = heads.width * (NOPE + VD)
    f32, bf16 = (jnp.float32, jnp.bfloat16)
    shapes = [
        ((count, heads.lead), bf16),
        ((count, kv_c), bf16),
        ((count, model), bf16),
        ((8, model), f32),
    ]
    vmem = pl.BlockSpec(memory_space=pltpu.VMEM)
    return pl.pallas_call(
        functools.partial(attend_back_kernel, heads, len(others)),
        in_specs=[vmem] * len(operands) + [pl.BlockSpec(memory_space=pl.ANY) for _ in others],
        out_specs=[vmem] * len(shapes),
        out_shape=[jax.ShapeDtypeStruct(*s) for s in shapes],
        scratch_shapes=[pltpu.VMEM((LAT, kv_c), bf16)],
        compiler_params=pltpu.CompilerParams(vmem_limit_bytes=60 * MIB),
        cost_estimate=pl.CostEstimate(
            flops=2 * count * (model * heads.cols + LAT * kv_c + heads.width * count * 1600),
            bytes_accessed=2 * (model * heads.cols + 4 * count * model),
            transcendentals=heads.width * count * count,
        ),
        name="attend_back",
    )(*operands, *others)


def per_device(
    tokens_in,
    cotangent,
    routes,
    segments,
    norm_in,
    w_query,
    w_latent,
    latent_gain,
    w_expand,
    w_output,
    norm_mid,
    w_router,
    shared_gate,
    shared_up,
    shared_down,
    expert_gate,
    routed_up_weight,
    expert_down,
):
    f32, bf16 = (jnp.float32, jnp.bfloat16)
    groups, lanes = (lax.axis_size("fsdp"), lax.axis_size("ctx"))
    halves = [list(range(k, groups, 2)) for k in (0, 1)]
    half = groups // 2

    def swap(value):
        return lax.ppermute(value, "fsdp", [(i, i ^ 1) for i in range(groups)])

    def gather_half(value):
        return lax.all_gather(value, "fsdp", axis=0, tiled=True, axis_index_groups=halves)

    def scatter_half(value):
        return lax.psum_scatter(
            value, "fsdp", scatter_dimension=0, tiled=True, axis_index_groups=halves
        )

    def direct_half(value):
        chip, rows = (lax.axis_index("fsdp") // 2, value.shape[0] // half)
        total = lax.dynamic_slice_in_dim(value, chip * rows, rows, 0).astype(jnp.float32)
        for hop in range(1, half):
            part = lax.dynamic_slice_in_dim(value, (chip ^ hop) * rows, rows, 0)
            got = lax.ppermute(part, "fsdp", [(i, i ^ (2 * hop)) for i in range(groups)])
            total = total + got.astype(jnp.float32)
        return total.astype(jnp.bfloat16)

    group = lax.axis_index("fsdp")
    tok_dev, model_w = tokens_in.shape
    count = tok_dev * lanes
    depth = w_query.shape[0]
    query_c, expand_c, heads_c = (w_query.shape[1], w_expand.shape[1], w_output.shape[0])
    exp_dev, hidden, _ = expert_gate.shape
    experts_n, top_k = (w_router.shape[1], routes.shape[1])
    sh_units = shared_gate.shape[1] // groups
    plan = Plan(exp_dev, hidden, sh_units, experts_n, top_k)
    units = plan.units
    chunks = max(2, groups * count // 2048)
    width = query_c // (NOPE + ROPE)

    small_c = -(-(LAT + ROPE + experts_n + 3) // 128) * 128
    assert small_c - 128 <= LAT + ROPE
    at_router = LAT + ROPE
    at_seg = at_router + experts_n
    seg_cols = segments.astype(bf16).reshape(w_latent.shape[0], -1)
    spare = small_c - at_seg - seg_cols.shape[1]
    small = jnp.concatenate(
        [w_latent, w_router, seg_cols, jnp.zeros((w_latent.shape[0], spare), bf16)], axis=1
    )
    small = gather_ctx(small)
    seg_all = small[:, at_seg : at_seg + seg_cols.shape[1]].astype(jnp.int32).reshape(count)
    folds = depth // w_expand.shape[0]
    wide = expand_c // folds
    expand_blocks = [w_expand[:, k * wide : (k + 1) * wide] for k in range(folds)]
    heads = Heads(width, groups, depth, small_c, wide, heads_c)
    order = heads.order()
    packed = jnp.concatenate(
        [dot32(w_query, order).astype(bf16), small, jnp.concatenate(expand_blocks, axis=0), w_output.T], axis=1
    )
    packed = lax.all_gather(packed, "fsdp", axis=0, tiled=True)
    at_expand = heads.lead
    at_output = heads.output
    at_first = heads.query + at_router
    router_w = packed[:, at_first : at_first + experts_n]

    meta = jnp.concatenate(
        [routes.astype(bf16), jnp.zeros((tok_dev, 128 - top_k), bf16)], axis=1
    )
    dout_own = after(jnp.concatenate([cotangent, meta], axis=1), small)
    dout_group = gather_ctx(dout_own)
    dout_all = gather_half(dout_group)
    dout_all = dout_all.reshape(half * lanes, chunks, tok_dev // chunks, model_w + 128)

    x_pieces = spread_ctx(after(tokens_in, dout_group))

    steps = jnp.arange(count, dtype=jnp.int32)
    same = seg_all[:, None] == seg_all[None, :]
    start = jnp.min(jnp.where(same, steps[None, :], count), axis=1)
    place = (steps - start).astype(f32)
    freq = THETA ** (-(jnp.arange(ROPE // 2, dtype=f32) * 2.0 / ROPE))
    angle = place[:, None] * freq[None, :]
    cosine, sine = (jnp.concatenate([f(angle)] * 4, axis=1) for f in (jnp.cos, jnp.sin))
    fixed = (cosine, sine, seg_all[:, None], seg_all[None, :], latent_gain[None, :])
    lane = lax.axis_index("ctx").astype(jnp.int32)[None]
    early_pair = [swap(w.reshape(units, model_w)) for w in (expert_gate, routed_up_weight)]
    x_all, x_low, factor_in, q_low, kv_low, kr_low, latent_raw, latent_low_t, lse, heads_low, *attn = (
        attend(heads, chunks, lane, norm_in[None, :], packed, *fixed, x_pieces, *early_pair)
    )
    def pair_weights(*others):
        shared = jnp.stack([shared_gate.T, shared_up.T, shared_down]).reshape(
            3, groups, sh_units, depth
        )
        shared, late_down = after((shared, expert_down), *others)
        shared = lax.all_to_all(shared, "fsdp", split_axis=1, concat_axis=1, tiled=True)
        shared = shared.transpose(0, 2, 1, 3).reshape(3, sh_units, model_w)

        if plan.shared > sh_units:
            shared = jnp.pad(shared, ((0, 0), (0, plan.shared - sh_units), (0, 0)))
        shared_pair = swap(shared)

        pack = [w.reshape(units, model_w) for w in (expert_gate, routed_up_weight, late_down)]
        pair = [*early_pair, swap(pack[2])]

        def rest(k, router):
            gap = jnp.zeros((plan.router - 2 * (units + plan.shared), model_w), bf16)
            end = jnp.zeros((plan.cols - plan.router - router.shape[0], model_w), bf16)
            return jnp.concatenate([shared[k], shared_pair[k], gap, router, end])

        none = jnp.zeros((0, model_w), bf16)
        rests = (rest(0, router_w.T), rest(1, none), rest(2, none))
        return [part for k in range(3) for part in (pack[k], pair[k], rests[k])]

    pieces = pair_weights(lse)

    own_experts = group * exp_dev + jnp.arange(exp_dev, dtype=jnp.int32)
    pair_experts = (group ^ 1) * exp_dev + jnp.arange(exp_dev, dtype=jnp.int32)
    first = jnp.concatenate([own_experts, pair_experts])
    part = tok_dev // chunks
    mids, rows_parts, held = ([], [], ())
    resid, unit_mid, factor_mid, mid_low = ([], [], [], [])
    last, sent = (dout_all, ())
    for h in range(chunks):
        rows = tokens_in[h * part : (h + 1) * part].astype(f32)
        attn_part = after(attn[h], *sent)
        resid.append(rows + scatter_ctx(attn_part))
        mid, unit, factor = norm_parts(resid[h], norm_mid)
        unit_mid.append(unit)
        factor_mid.append(factor)
        mid_low.append(mid.astype(bf16))
        mid_part = gather_ctx(mid_low[h])
        mid_part = after(mid_part, *pieces)
        sent = (mid_part,)
        last = gather_half(after(mid_part, last))
        mids.append(last)
    for h in range(chunks):
        rows_part, *held = experts_back(plan, h, first, mids[h], dout_all, pieces, *held)
        if h == 0 and chunks == 2:
            rows_parts.append(direct_half(rows_part))
            continue
        rows_part = after(rows_part, last)
        last = scatter_half(rows_part)
        rows_parts.append(last)
    gud, act = held

    router_f = router_w.astype(f32)

    def middle_back(h, pieces, *others):
        own = total_of([after(pieces[0], *others)] + pieces[1:])
        rows = slice(h * part, (h + 1) * part)
        mid_grad = own[:, :model_w]
        gates_grad = (
            own[:, model_w : model_w + experts_n]
            + own[:, model_w + experts_n : model_w + 2 * experts_n]
        )
        sig = jax.nn.sigmoid(dot32(mid_low[h], router_w))
        hit = routes[rows, :, None] == jnp.arange(experts_n, dtype=jnp.int32)[None, None, :]
        member = jnp.any(hit, axis=1).astype(f32)
        chosen_sum = jnp.sum(sig * member, axis=-1, keepdims=True)
        gates = ROUTE_SCALE * sig * member / chosen_sum
        spread = jnp.sum(gates_grad * gates, axis=-1, keepdims=True)
        chosen_grad = (ROUTE_SCALE * gates_grad - spread) / chosen_sum
        logit_grad = chosen_grad * member * sig * (1.0 - sig)
        mid_grad = mid_grad + precise_nt(logit_grad, router_f)
        grad = norm_back(mid_grad, unit_mid[h], factor_mid[h], norm_mid)
        grad = grad + cotangent[rows].astype(f32)
        return (
            grad,
            grad.astype(bf16),
            jnp.sum(mid_grad * unit_mid[h], axis=0, keepdims=True),
            precise_tn(logit_grad, mid_low[h].astype(f32)),
        )

    def outputs(*others):
        return [
            experts_out(plan, half, lanes, h, 2, act, pieces[6:], *others) for h in range(0, chunks, 2)
        ]

    if chunks == 2:
        back = [middle_back(0, pieces_ctx(rows_parts[0]))]
        gate_sums = weight_sum(plan, "gate", model_w, gud, mids)
        attn_low = [gather_ctx(back[0][1])]
        out_parts = outputs(back[0][1], gate_sums[3])
        out_parts = [after(out_parts[0], attn_low[0])]
        back.append(middle_back(1, pieces_ctx(after(rows_parts[1], *out_parts))))
        down_sums = weight_sum(plan, "down", model_w, act, dout_all, rows_parts[1])
        attn_low.append(gather_ctx(back[1][1]))
        up_sums = weight_sum(plan, "up", model_w, gud, mids, back[1][1])
        early_swaps = [swap(gate_sums[2]), swap(down_sums[2])]
    else:
        gate_sums = weight_sum(plan, "gate", model_w, gud, mids)
        down_sums = weight_sum(plan, "down", model_w, act, dout_all)
        up_sums = weight_sum(plan, "up", model_w, gud, mids)
        out_parts = outputs(down_sums[3], gate_sums[3], up_sums[3])
        back = [middle_back(h, pieces_ctx(rows_parts[h])) for h in range(chunks)]
        attn_low = [gather_ctx(grad[1]) for grad in back]
        early_swaps = [swap(gate_sums[2]), swap(down_sums[2])]
    attn_low = jnp.stack([a.reshape(lanes, part, model_w) for a in attn_low], axis=1)
    attn_low = attn_low.reshape(count, model_w)
    resid_grad = jnp.concatenate([grad[0] for grad in back])
    mid_gain_grad = sum(grad[2] for grad in back)
    router_grad = sum(grad[3] for grad in back)

    out_sums = []
    for out_part in out_parts:
        last = scatter_half(after(out_part, last))
        out_sums.append(last)

    share = LAT // (groups * lanes)
    column = np.arange(model_w)[None, :]
    spot = column * lanes * groups // model_w * share + column % (depth // lanes)
    inside = column % (depth // lanes) < share
    spread = jnp.asarray(((np.arange(LAT)[:, None] == spot) & inside).astype(np.float32), bf16)
    qr_grad, kv_grad, normed_grad, gains = attend_back(
        heads,
        attn_low,
        x_all,
        factor_in,
        packed,
        *fixed,
        q_low,
        kv_low,
        kr_low,
        latent_raw,
        lse,
        spread,
        others=early_swaps + [up_sums[3]],
    )
    if chunks == 2:
        end_pieces = pieces_ctx(jnp.concatenate([out_sums[0], normed_grad], axis=1))
    else:
        moe = jnp.concatenate([scatter_ctx(rows) for rows in out_sums])
        end_pieces = pieces_ctx(normed_grad)
        normed_own = total_of(end_pieces)
        block_out = (jnp.concatenate(resid) + moe).astype(bf16)
    before = LAT + ROPE - (small_c - 128)
    early = jnp.concatenate([router_grad, mid_gain_grad])
    grads = packed_grads(
        groups,
        before,
        x_low,
        attn_low,
        latent_low_t,
        qr_grad,
        heads_low,
        kv_grad,
        early,
        gains,
    )
    all_sums = (gate_sums, up_sums, down_sums)
    swapped = (early_swaps[0], swap(up_sums[2]), early_swaps[1])
    expert_grads = [
        finished(sums[0], other, end_pieces[1]).reshape(expert_gate.shape)
        for sums, other in zip(all_sums, swapped)
    ]
    shared_other = swap(after(jnp.stack([sums[3] for sums in all_sums]), end_pieces[1]))
    shared_grad = jnp.stack([sums[1] for sums in all_sums]) + shared_other.astype(f32)
    shared_grad = shared_grad[:, :sh_units].astype(bf16)
    shared_grad = shared_grad.reshape(3, sh_units, groups, depth).transpose(0, 2, 1, 3)
    shared_grad = lax.all_to_all(shared_grad, "fsdp", split_axis=1, concat_axis=1, tiled=True)
    shared_grad = shared_grad.reshape(3, sh_units * groups, depth).astype(f32)
    if chunks == 2:
        block_out, grad_input = ends(
            end_pieces,
            jnp.concatenate(resid),
            resid_grad,
            tokens_in,
            norm_in[None, :],
            *expert_grads,
        )
    else:
        _, unit_own, factor_own = norm_parts(tokens_in.astype(f32), norm_in)
        grad_input = norm_back(normed_own, unit_own, factor_own, norm_in) + resid_grad
    grads = lax.psum_scatter(after(grads, last), "fsdp", scatter_dimension=0, tiled=True)
    small_own = scatter_ctx(grads[:, heads.query : at_expand])
    g_query = dot_nt(grads[:, : heads.query], order)
    g_expand = grads[:, at_expand:at_output].astype(f32)
    g_expand = jnp.concatenate(
        [g_expand[k * w_expand.shape[0] : (k + 1) * w_expand.shape[0]] for k in range(folds)],
        axis=1,
    )
    g_output = grads[:, at_output:].astype(f32).T
    at_gain = at_router + experts_n
    return (
        block_out,
        grad_input.astype(bf16),
        small_own[:, at_gain + 1],
        g_query,
        small_own[:, :at_router],
        small_own[: LAT // (groups * lanes), at_gain + 2],
        g_expand,
        g_output,
        small_own[:, at_gain],
        small_own[:, at_router:at_gain],
        shared_grad[0].T,
        shared_grad[1].T,
        shared_grad[2],
        *expert_grads,
    )


def solution(mesh):
    in_specs = (
        P(("fsdp", "ctx"), None),
        P(("fsdp", "ctx"), None),
        P(("fsdp", "ctx"), None),
        P(("fsdp", "ctx")),
        P(),
        P("fsdp", "ctx"),
        P(("fsdp", "ctx"), None),
        P(),
        P("fsdp", "ctx"),
        P("ctx", "fsdp"),
        P(),
        P(("fsdp", "ctx"), None),
        P("fsdp", "ctx"),
        P("fsdp", "ctx"),
        P("ctx", "fsdp"),
        P("fsdp", "ctx", None),
        P("fsdp", "ctx", None),
        P("fsdp", "ctx", None),
    )
    out_specs = (
        P(("fsdp", "ctx"), None),
        P(("fsdp", "ctx"), None),
        P(("fsdp", "ctx")),
        P("fsdp", "ctx"),
        P(("fsdp", "ctx"), None),
        P(("fsdp", "ctx")),
        P("fsdp", "ctx"),
        P("ctx", "fsdp"),
        P(("fsdp", "ctx")),
        P(("fsdp", "ctx"), None),
        P("fsdp", "ctx"),
        P("fsdp", "ctx"),
        P("ctx", "fsdp"),
        P("fsdp", "ctx", None),
        P("fsdp", "ctx", None),
        P("fsdp", "ctx", None),
    )
    return jax.shard_map(
        per_device, mesh=mesh, in_specs=in_specs, out_specs=out_specs, check_vma=False
    )
```
